32 devices in a mesh: rep: 8 (over z, y), fsdp: 4 (over x, core).
Axes of the slice: x: 2, y: 2, z: 4, core: 2. Of those that a mesh axis runs over, the one named last changes fastest.
Arguments:
- tokens: bfloat16 [8192, 2304], P(('rep', 'fsdp')), may hold values from -6 to 6
- cotangent: bfloat16 [8192, 2304], P(('rep', 'fsdp')), may hold values from -6 to 6
- gain_attn: float32 [2304], replicated, may hold values from 0.25 to 1.75
- gain_ffn: float32 [2304], replicated, may hold values from 0.25 to 1.75
- w_query: bfloat16 [2304, 2304], P(None, 'fsdp'), may hold values from -0.125 to 0.125
- w_key: bfloat16 [2304, 2304], P(None, 'fsdp'), may hold values from -0.125 to 0.125
- w_value: bfloat16 [2304, 2304], P(None, 'fsdp'), may hold values from -0.125 to 0.125
- w_out: bfloat16 [2304, 2304], P(None, 'fsdp'), may hold values from -3 to 3
- w_gate: bfloat16 [2304, 5760], P(None, 'fsdp'), may hold values from -0.125 to 0.125
- w_up: bfloat16 [2304, 5760], P(None, 'fsdp'), may hold values from -0.125 to 0.125
- w_down: bfloat16 [5760, 2304], P(None, 'fsdp'), may hold values from -0.375 to 0.375
Outputs:
- output: bfloat16 [8192, 2304], P(('rep', 'fsdp'))
- d_tokens: float32 [8192, 2304], P(('rep', 'fsdp'))
- grad_gain_attn: float32 [2304], replicated
- grad_gain_ffn: float32 [2304], replicated
- grad_query: float32 [2304, 2304], P('rep', 'fsdp')
- grad_key: float32 [2304, 2304], P('rep', 'fsdp')
- grad_value: float32 [2304, 2304], P('rep', 'fsdp')
- grad_out: float32 [2304, 2304], P('rep', 'fsdp')
- grad_gate: float32 [2304, 5760], P('rep', 'fsdp')
- grad_up: float32 [2304, 5760], P('rep', 'fsdp')
- grad_down: float32 [5760, 2304], P('rep', 'fsdp')
The draws below stay inside these ranges and needn't reach their ends.
All inputs are finite; a program needn't handle non-finite values.
Results may differ from the reference program's by a relative error of at most 0.015.
Values may be sent and summed in bfloat16 or wider, within the bound.
No kernel may reach another device: no remote copies, remote signals or barrier semaphores. Data moves between devices by JAX's collectives and lax.ppermute only.
A program may use at most 384 MiB of HBM per device.

```python
import math
import jax
import jax.numpy as jnp
from jax import lax

D = 2304
H = 36
HD = 64
FF = 5760
BLK = 256
SEQ = 1024
TOKENS = 8192


def levels(rng, shape, pieces, low, high):
    def one(axis_at, parts):
        draws = jax.random.uniform(jax.random.fold_in(jax.random.fold_in(rng, 6), axis_at), (parts,), jnp.float32, low / len(pieces), high / len(pieces))
        return jnp.repeat(jnp.exp(draws), shape[axis_at] // parts).reshape((-1,) + (1,) * (len(shape) - axis_at - 1))

    level = one(*pieces[0])
    for cut in pieces[1:]:
        level = level * one(*cut)
    return level


def normal_values(rng, extent, scale, most, pieces=(), kind=jnp.bfloat16):
    array = scale * jax.random.normal(rng, extent, jnp.float32)
    if pieces:
        array = array * levels(rng, extent, pieces, -0.22, 0.18)
    return jnp.clip(array, -most, most).astype(kind)


def setup_inputs(seed: int = 0) -> dict:
    seeds = jax.random.split(jax.random.key(seed), 12)
    return {
        "tokens": normal_values(seeds[0], (TOKENS, D), 1.0, 6.0, ((0, 32),)),
        "cotangent": normal_values(seeds[1], (TOKENS, D), 1.0, 6.0, ((0, 32),)),
        "gain_attn": jnp.clip(1.0 + 0.15 * jax.random.normal(seeds[2], (D,), jnp.float32), 0.25, 1.75),
        "gain_ffn": jnp.clip(1.0 + 0.15 * jax.random.normal(seeds[3], (D,), jnp.float32), 0.25, 1.75),
        "w_query": normal_values(seeds[4], (D, D), D ** -0.5, 0.125, ((1, 4),)),
        "w_key": normal_values(seeds[5], (D, D), D ** -0.5, 0.125, ((1, 4),)),
        "w_value": normal_values(seeds[6], (D, D), D ** -0.5, 0.125, ((1, 4),)),
        "w_out": normal_values(seeds[7], (D, D), 4 ** -0.5, 3.0, ((1, 4),)),
        "w_gate": normal_values(seeds[8], (D, FF), D ** -0.5, 0.125, ((1, 4),)),
        "w_up": normal_values(seeds[9], (D, FF), D ** -0.5, 0.125, ((1, 4),)),
        "w_down": normal_values(seeds[10], (FF, D), (FF // 20) ** -0.5, 0.375, ((1, 4),)),
    }


@jax.custom_vjp
def low(v):
    return lax.optimization_barrier(v.astype(jnp.bfloat16)).astype(jnp.float32)

@jax.custom_vjp
def low_back(v):
    return v

def low_keep(v):
    return (low(v), None)

def low_pass(kept, grad):
    return (grad,)

def back_keep(v):
    return (v, None)

def back_low(kept, grad):
    return (low(grad),)
low.defvjp(low_keep, low_pass)
low_back.defvjp(back_keep, back_low)
epsilon = 1e-05
branch_scale = 1.4 / math.sqrt(40.0)
highest = lax.Precision.HIGHEST

def rotate(field, positions):
    half = field.shape[-1] // 2
    frequency = 10000.0 ** (-(jnp.arange(half, dtype=jnp.float32) * 2.0 / field.shape[-1]))
    angles = positions.astype(jnp.float32)[:, None] * frequency[None, :]
    cosine = jnp.cos(angles)[:, None, :]
    sine = jnp.sin(angles)[:, None, :]
    first = field[..., :half]
    second = field[..., half:]
    return jnp.concatenate([first * cosine - second * sine, second * cosine + first * sine], axis=-1)

def normalize(field, gain):
    factor = lax.rsqrt(lax.optimization_barrier(jnp.mean(field * field, axis=-1, keepdims=True)) + epsilon)
    return field * factor * gain

def sequence_forward(sequence, gain_attn, gain_ffn, w_query, w_key, w_value, w_out, w_gate, w_up, w_down):
    length = sequence.shape[0]
    positions = jnp.arange(length, dtype=jnp.int32)
    normed = low(normalize(sequence, gain_attn))
    query = low_back(jnp.dot(normed, w_query, precision=highest))
    keys = low_back(jnp.dot(normed, w_key, precision=highest))
    values = low(low_back(jnp.dot(normed, w_value, precision=highest)))
    query_rot = low(rotate(query.reshape(length, H, HD), positions))
    key_rot = low(rotate(keys.reshape(length, H, HD), positions))
    raw_scores = jnp.einsum('thd,shd->hts', query_rot, key_rot, precision=highest)
    scores = low_back(raw_scores) * HD ** (-0.5)
    blocks = positions // BLK
    allowed = blocks[None, :] <= blocks[:, None]
    scores = jnp.where(allowed[None], scores, -1e+30)
    probs_low = low(jax.nn.softmax(scores, axis=-1))
    mixed = jnp.einsum('hts,shd->thd', probs_low, values.reshape(length, H, HD), precision=highest)
    attended = low(low_back(mixed.reshape(length, H * HD)))
    attn_result = low_back(jnp.dot(attended, w_out, precision=highest))
    hidden_state = sequence + branch_scale * attn_result
    normed_ffn = low(normalize(hidden_state, gain_ffn))
    gate_value = low_back(jnp.dot(normed_ffn, w_gate, precision=highest))
    up_value = low_back(jnp.dot(normed_ffn, w_up, precision=highest))
    inner = low(jax.nn.silu(gate_value) * up_value)
    ffn_result = low_back(jnp.dot(inner, w_down, precision=highest))
    return hidden_state + branch_scale * ffn_result

def reference(tokens, cotangent, gain_attn, gain_ffn, w_query, w_key, w_value, w_out, w_gate, w_up, w_down):
    sequences = tokens.astype(jnp.float32).reshape(TOKENS // SEQ, SEQ, D)
    upstream = cotangent.astype(jnp.float32).reshape(TOKENS // SEQ, SEQ, D)

    def forward(batch, g_attn, g_ffn, m_query, m_key, m_value, m_out, m_gate, m_up, m_down):

        def single(sequence):
            return sequence_forward(sequence, g_attn, g_ffn, m_query, m_key, m_value, m_out, m_gate, m_up, m_down)
        return lax.map(jax.checkpoint(single), batch)
    result, pullback = jax.vjp(forward, sequences, gain_attn.astype(jnp.float32), gain_ffn.astype(jnp.float32), w_query.astype(jnp.float32), w_key.astype(jnp.float32), w_value.astype(jnp.float32), w_out.astype(jnp.float32), w_gate.astype(jnp.float32), w_up.astype(jnp.float32), w_down.astype(jnp.float32))
    grads = pullback(upstream)
    return (result.reshape(TOKENS, D).astype(jnp.bfloat16), grads[0].reshape(TOKENS, D), grads[1], grads[2], grads[3], grads[4], grads[5], grads[6], grads[7], grads[8], grads[9])
```

```python
import math

import jax
import jax.numpy as jnp
from jax import lax
from jax.experimental import pallas as pl
from jax.experimental.pallas import tpu as pltpu
from jax.sharding import PartitionSpec as P

HD = 64
BLK = 256
NT = (((1,), (1,)), ((), ()))

epsilon = 1e-05
branch_scale = 1.4 / math.sqrt(40.0)
low = jnp.bfloat16
full = jnp.float32


def turn(field, cosine, sine):
    half = field.shape[0] // 2
    first, second = field[:half], field[half:]
    return jnp.concatenate(
        [first * cosine - second * sine, second * cosine + first * sine], axis=0
    )


def forward_kernel(
    q_ref, k_ref, v_ref, cos_ref, sin_ref, out_ref, ql_ref, kl_ref, vl_ref, lse_ref
):
    cosine, sine = cos_ref[...], sin_ref[...]
    span = q_ref.shape[2]
    q_low = turn(q_ref[0], cosine, sine).astype(low)
    k_low = turn(k_ref[0], cosine, sine).astype(low)
    v_low = v_ref[0].astype(low)
    ql_ref[0] = q_low
    kl_ref[0] = k_low
    vl_ref[0] = v_low
    q_scaled = (q_low * (HD ** (-0.5))).astype(low)
    k_rows = k_low.T
    for j in range(span // BLK):
        kv = (j + 1) * BLK
        cols = slice(j * BLK, kv)
        scores = jnp.dot(k_rows[:kv], q_scaled[:, cols], preferred_element_type=full)
        top = jnp.max(scores, axis=0, keepdims=True)
        expo = jnp.exp(scores - top)
        total = jnp.sum(expo, axis=0, keepdims=True)
        probs = (expo * (1.0 / total)).astype(low)
        out_ref[0, :, cols] = jnp.dot(
            v_low[:, :kv], probs, preferred_element_type=full
        ).astype(low)
        lse_ref[0, :, cols] = top + jnp.log(total)


def attention_forward(query, key, value, cosine, sine):
    heads, _, span = query.shape
    spec = pl.BlockSpec((1, HD, span), lambda h: (h, 0, 0))
    table = pl.BlockSpec((HD // 2, span), lambda h: (0, 0))
    field = jax.ShapeDtypeStruct((heads, HD, span), low)
    row = pl.BlockSpec((1, 1, span), lambda h: (h, 0, 0))
    return pl.pallas_call(
        forward_kernel,
        grid=(heads,),
        in_specs=[spec, spec, spec, table, table],
        out_specs=[spec, spec, spec, spec, row],
        out_shape=[field, field, field, field, jax.ShapeDtypeStruct((heads, 1, span), full)],
        compiler_params=pltpu.CompilerParams(vmem_limit_bytes=48 * 2**20),
        cost_estimate=pl.CostEstimate(
            flops=heads * span * span * HD * 10, bytes_accessed=heads * HD * span * 20,
            transcendentals=heads * span * span,
        ),
        name="attention_forward",
    )(query, key, value, cosine, sine)


def backward_kernel(
    q_ref, k_ref, v_ref, g_ref, lse_ref, cos_ref, sin_ref, dq_ref, dk_ref, dv_ref, dk_acc, dv_acc
):
    cosine, sine = cos_ref[...], sin_ref[...]
    span = q_ref.shape[2]
    q_scaled = (q_ref[0] * (HD ** (-0.5))).astype(low)
    k_low, v_low, grad = k_ref[0], v_ref[0], g_ref[0]
    k_rows, v_rows = k_low.T, v_low.T
    dk_acc[...] = jnp.zeros_like(dk_acc)
    dv_acc[...] = jnp.zeros_like(dv_acc)
    for j in range(span // BLK):
        kv = (j + 1) * BLK
        cols = slice(j * BLK, kv)
        q_j, g_j = q_scaled[:, cols], grad[:, cols]
        scores = jnp.dot(k_rows[:kv], q_j, preferred_element_type=full)
        probs = jnp.exp(scores - lse_ref[0, :, cols])
        probs_low = probs.astype(low)
        d_probs = jnp.dot(v_rows[:kv], g_j, preferred_element_type=full)
        delta = jnp.sum(probs * d_probs, axis=0, keepdims=True)
        d_scores = (probs * (d_probs - delta)).astype(low)
        dq = jnp.dot(k_low[:, :kv], d_scores, preferred_element_type=full) * (HD ** (-0.5))
        dq_ref[0, :, cols] = turn(dq, cosine[:, cols], -sine[:, cols]).astype(low)
        dk_acc[:, :kv] += lax.dot_general(q_j, d_scores, NT, preferred_element_type=full)
        dv_acc[:, :kv] += lax.dot_general(g_j, probs_low, NT, preferred_element_type=full)
    dk_ref[0] = turn(dk_acc[...], cosine, -sine).astype(low)
    dv_ref[0] = dv_acc[...].astype(low)


def attention_backward(query, key, value, grad, lse, cosine, sine):
    heads, _, span = query.shape
    spec = pl.BlockSpec((1, HD, span), lambda h: (h, 0, 0))
    table = pl.BlockSpec((HD // 2, span), lambda h: (0, 0))
    row = pl.BlockSpec((1, 1, span), lambda h: (h, 0, 0))
    field = jax.ShapeDtypeStruct((heads, HD, span), low)
    return pl.pallas_call(
        backward_kernel,
        grid=(heads,),
        in_specs=[spec, spec, spec, spec, row, table, table],
        out_specs=[spec, spec, spec],
        out_shape=[field, field, field],
        scratch_shapes=[pltpu.VMEM((HD, span), full), pltpu.VMEM((HD, span), full)],
        compiler_params=pltpu.CompilerParams(vmem_limit_bytes=48 * 2**20),
        cost_estimate=pl.CostEstimate(
            flops=heads * span * span * HD * 20, bytes_accessed=heads * HD * span * 14,
            transcendentals=heads * span * span,
        ),
        name="attention_backward",
    )(query, key, value, grad, lse, cosine, sine)


def swap(array, j):
    size = lax.axis_size("fsdp")
    return lax.ppermute(array, "fsdp", [(i, i ^ j) for i in range(size)])


def place_kernel(*refs):
    *blocks, out, held, arrived, left = refs
    me = lax.axis_index("fsdp")
    into = [
        pltpu.make_async_copy(block, held.at[j], arrived.at[j]) for j, block in enumerate(blocks)
    ]
    back = [
        pltpu.make_async_copy(
            held.at[j], out.at[lax.bitwise_xor(me, jnp.int32(j))], left.at[j]
        )
        for j in range(len(blocks))
    ]
    for copy in into:
        copy.start()
    for copy, then in zip(into, back):
        copy.wait()
        then.start()
    for copy in back:
        copy.wait()


def place(blocks):
    count = len(blocks)
    first = blocks[0]
    whole = pl.pallas_call(
        place_kernel,
        in_specs=[pl.BlockSpec(memory_space=pl.ANY)] * count,
        out_specs=pl.BlockSpec(memory_space=pl.ANY),
        out_shape=jax.ShapeDtypeStruct((count,) + first.shape, first.dtype),
        scratch_shapes=[
            pltpu.VMEM((count,) + first.shape, first.dtype),
            pltpu.SemaphoreType.DMA((count,)),
            pltpu.SemaphoreType.DMA((count,)),
        ],
        compiler_params=pltpu.CompilerParams(vmem_limit_bytes=16 * 2**20),
        cost_estimate=pl.CostEstimate(
            flops=0, bytes_accessed=2 * count * first.size * first.dtype.itemsize, transcendentals=0
        ),
        name="place",
    )(*blocks)
    return whole.reshape((count * first.shape[0],) + first.shape[1:])


def gather(array):
    core = swap(array, 1)
    chip = swap(array, 2)
    return place([array, core, chip, swap(chip, 1)])


def scatter_sum(chunk):
    far = swap(chunk(3), 1)
    across = swap((chunk(2) + far).astype(low), 2)
    near = swap(chunk(1), 1)
    return chunk(0).astype(full) + near.astype(full) + across.astype(full)


def total_of(array):
    array = array + swap(array, 1)
    return array + swap(array, 2)


def to_rows(field, rows):
    me = lax.axis_index("fsdp")
    size = lax.axis_size("fsdp")
    blocks = []
    for j in range(size):
        block = lax.dynamic_slice_in_dim(field, (me ^ j) * rows, rows, 1)
        blocks.append(block if j == 0 else swap(block, j))
    return place(blocks).T


def rep_dims(size):
    return {8: (4, 2), 32: (2, 4, 4)}.get(size, (size,))


def coordinate(index, dims, at):
    stride = math.prod(dims[at + 1 :])
    return (index // stride) % dims[at], stride


def line_sum(part, dims, at):
    count = dims[at]
    size = math.prod(dims)
    me, stride = coordinate(lax.axis_index("rep"), dims, at)

    def piece(index):
        return lax.dynamic_index_in_dim(part, jnp.clip(index, 0, count - 1), 1, False)

    def run(sign):
        moving = None
        for step in range(1, count):
            mine = piece(me + sign * (count - step))
            if moving is not None:
                mine = (mine.astype(full) + moving.astype(full)).astype(low)
            pairs = []
            for index in range(size):
                here, _ = coordinate(index, dims, at)
                far = here if sign > 0 else count - 1 - here
                if far <= step - 1:
                    pairs.append((index, index + sign * stride))
            moving = lax.ppermute(mine, "rep", pairs)
        return moving

    return piece(me).astype(full) + run(1).astype(full) + run(-1).astype(full)


def halves(act):
    size = lax.axis_size("rep")
    dims = rep_dims(size)
    if dims[-1] != 2:
        return None, act
    side = lax.axis_index("rep") % 2
    view = act.reshape(size // 2, 2, act.shape[0] // size, act.shape[1])
    rows = act.shape[0] // 2
    return (
        lax.dynamic_index_in_dim(view, 1 - side, 1, False).reshape(rows, -1),
        lax.dynamic_index_in_dim(view, side, 1, False).reshape(rows, -1),
    )


def grad_sum(parts, grad):
    other, own = parts
    size = lax.axis_size("rep")
    dims = rep_dims(size)
    columns = grad.shape[0]

    def outer(rows):
        return jnp.einsum("dt,ft->df", rows, grad, preferred_element_type=full)

    last = len(dims) - 1
    if other is not None:
        neighbours = [(i, i ^ 1) for i in range(size)]
        sent = lax.ppermute(outer(other).astype(low), "rep", neighbours)
        part = outer(own) + sent.astype(full)
        rows = 2 * own.shape[0] // size
        last -= 1
    else:
        part = outer(own)
        rows = own.shape[0] // size
    for at in range(last, -1, -1):
        part = line_sum(part.astype(low).reshape(-1, dims[at], rows, columns), dims, at)
    return part.reshape(rows, columns)


def body(
    tokens, cotangent, gain_attn, gain_ffn, w_query, w_key, w_value, w_out, w_gate, w_up, w_down
):
    rows, width = tokens.shape
    size = lax.axis_size("fsdp")
    reps = lax.axis_size("rep")
    span = rows * size
    me = lax.axis_index("fsdp")
    replica = lax.axis_index("rep")
    width_cols = width // size
    hidden_cols = w_gate.shape[1]
    heads = width_cols // HD

    half = HD // 2
    frequency = 10000.0 ** (-(jnp.arange(half, dtype=full) * 2.0 / HD))
    angles = frequency[:, None] * jnp.arange(span, dtype=jnp.int32).astype(full)[None, :]
    cosine, sine = jnp.cos(angles), jnp.sin(angles)

    def own_columns(field):
        return lax.dynamic_slice_in_dim(field, me * width_cols, width_cols, 1)

    def own_gain(gain):
        return lax.dynamic_slice_in_dim(gain, me * width_cols, width_cols, 0)[:, None]

    tokens_all = gather(tokens)
    x_all = tokens_all.astype(full)
    factor_all = lax.rsqrt(jnp.mean(x_all * x_all, axis=-1, keepdims=True) + epsilon)
    normed = (x_all * factor_all * gain_attn).astype(low)
    cotangent_all = gather(cotangent)
    d_ffn = (branch_scale * cotangent_all.astype(full)).astype(low)

    share = hidden_cols // reps

    def down_part(j):
        return lax.dynamic_slice_in_dim(w_down, (me ^ j) * hidden_cols + replica * share, share, 0)

    def down_rows(j):
        return lax.dynamic_slice_in_dim(w_down, (me ^ j) * hidden_cols, hidden_cols, 0)

    part_chip = swap(down_part(2), 2)
    part_both = swap(swap(down_part(3), 2), 1)
    down_blocks = [
        down_rows(0),
        swap(down_rows(1), 1),
        lax.all_gather(part_chip, "rep", axis=0, tiled=True),
        lax.all_gather(part_both, "rep", axis=0, tiled=True),
    ]
    down_own = place([block.T for block in down_blocks])
    d_inner = jnp.einsum("ef,te->ft", down_own, d_ffn, preferred_element_type=full)

    def project(weight):
        field = jnp.einsum("de,td->et", weight, normed, preferred_element_type=full)
        return field.reshape(heads, HD, span)

    attended, query_low, key_low, value_low, lse = attention_forward(
        project(w_query), project(w_key), project(w_value), cosine, sine
    )
    attended_all = gather(attended.reshape(width_cols, span))

    attn_result = jnp.einsum("de,dt->et", w_out, attended_all, preferred_element_type=full)
    hidden = own_columns(tokens_all).astype(full).T + branch_scale * attn_result
    squares = total_of(jnp.sum(hidden * hidden, axis=0, keepdims=True))
    factor = lax.rsqrt(squares / width + epsilon)
    gain_own = own_gain(gain_ffn)
    scaled_all = gather((hidden * gain_own).astype(low))

    gate = factor * jnp.einsum("df,dt->ft", w_gate, scaled_all, preferred_element_type=full)
    up = factor * jnp.einsum("df,dt->ft", w_up, scaled_all, preferred_element_type=full)
    sigmoid = jax.nn.sigmoid(gate)
    activated = gate * sigmoid
    inner = (activated * up).astype(low)
    d_gate_full = factor * d_inner * up * sigmoid * (1.0 + gate * (1.0 - sigmoid))
    d_up_full = factor * d_inner * activated
    d_gate = d_gate_full.astype(low)
    d_up = d_up_full.astype(low)
    mean_ffn = total_of(jnp.sum(d_gate_full * gate + d_up_full * up, axis=0, keepdims=True)) / width

    scaled_halves = halves(scaled_all)
    grad_gate = grad_sum(scaled_halves, d_gate)
    grad_up = grad_sum(scaled_halves, d_up)

    def ffn_chunk(j):
        at = (me ^ j) * width_cols
        gate_rows = lax.dynamic_slice_in_dim(w_gate, at, width_cols, 0)
        up_rows = lax.dynamic_slice_in_dim(w_up, at, width_cols, 0)
        return (
            jnp.einsum("df,ft->dt", gate_rows, d_gate, preferred_element_type=full)
            + jnp.einsum("df,ft->dt", up_rows, d_up, preferred_element_type=full)
        ).astype(low)

    d_scaled = scatter_sum(ffn_chunk)
    gain_ffn_term = jnp.sum(d_scaled * hidden, axis=1)
    d_hidden = (
        own_columns(cotangent_all).astype(full).T
        + gain_own * d_scaled
        - hidden * (factor * mean_ffn)
    )
    d_attn = (branch_scale * d_hidden).astype(low)

    def out_chunk(j):
        out_rows = lax.dynamic_slice_in_dim(w_out, (me ^ j) * width_cols, width_cols, 0)
        return jnp.einsum("de,et->dt", out_rows, d_attn, preferred_element_type=full).astype(low)

    d_attended = scatter_sum(out_chunk).astype(low).reshape(heads, HD, span)

    inner_all = gather(inner)
    ffn_result = jnp.einsum("fe,ft->et", w_down, inner_all, preferred_element_type=full)
    output = to_rows((hidden + branch_scale * ffn_result).astype(low), rows)
    grad_down = grad_sum(halves(inner_all), own_columns(d_ffn).T)
    grad_out = grad_sum(halves(attended_all), d_attn)

    d_query, d_key, d_value = (
        field.reshape(width_cols, span)
        for field in attention_backward(
            query_low, key_low, value_low, d_attended, lse, cosine, sine
        )
    )
    normed_halves = halves(normed.T)
    grad_query = grad_sum(normed_halves, d_query)
    grad_key = grad_sum(normed_halves, d_key)
    grad_value = grad_sum(normed_halves, d_value)

    def token_chunk(j):
        def product(grad, weight):
            block = lax.dynamic_slice_in_dim(grad, (me ^ j) * rows, rows, 1)
            return jnp.einsum("et,de->td", block, weight, preferred_element_type=full)

        return (product(d_query, w_query) + product(d_key, w_key) + product(d_value, w_value)).astype(low)

    d_normed = scatter_sum(token_chunk)
    x_own = tokens.astype(full)
    factor_own = lax.rsqrt(jnp.mean(x_own * x_own, axis=-1, keepdims=True) + epsilon)
    unit_own = x_own * factor_own
    scaled = d_normed * gain_attn
    d_tokens = to_rows(d_hidden.astype(low), rows).astype(full) + factor_own * (
        scaled - unit_own * jnp.mean(scaled * unit_own, axis=-1, keepdims=True)
    )
    gain_attn_term = jnp.sum(d_normed * unit_own, axis=0)
    gain_ffn_wide = lax.dynamic_update_slice_in_dim(
        jnp.zeros((width,), full), gain_ffn_term, me * width_cols, 0
    )
    grad_gain_attn, grad_gain_ffn = lax.psum((gain_attn_term, gain_ffn_wide), ("rep", "fsdp"))
    return (
        output,
        d_tokens,
        grad_gain_attn,
        grad_gain_ffn,
        grad_query,
        grad_key,
        grad_value,
        grad_out,
        grad_gate,
        grad_up,
        grad_down,
    )


def solution(mesh):
    rows = P(("rep", "fsdp"), None)
    columns = P(None, "fsdp")
    both = P("rep", "fsdp")
    return jax.shard_map(
        body,
        mesh=mesh,
        in_specs=(rows, rows, P(), P()) + (columns,) * 7,
        out_specs=(rows, rows, P(), P()) + (both,) * 7,
        check_vma=False,
    )
```

```python
import math

import jax
import jax.numpy as jnp
from jax import lax
from jax.experimental import pallas as pl
from jax.experimental.pallas import tpu as pltpu
from jax.sharding import PartitionSpec as P

HD = 64
BLK = 256
NT = (((1,), (1,)), ((), ()))

epsilon = 1e-05
branch_scale = 1.4 / math.sqrt(40.0)
low = jnp.bfloat16
full = jnp.float32

SMALL = pl.CostEstimate(flops=0, bytes_accessed=0, transcendentals=0)


def turn(field, cosine, sine):
    half = field.shape[0] // 2
    first, second = field[:half], field[half:]
    return jnp.concatenate(
        [first * cosine - second * sine, second * cosine + first * sine], axis=0
    )


def forward_kernel(
    q_here, k_here, v_here, q_there, k_there, v_there, cos_ref, sin_ref,
    out_ref, ql_ref, kl_ref, vl_ref, lse_ref,
):
    cosine, sine = cos_ref[...], sin_ref[...]
    span = cosine.shape[1]
    chip = lax.axis_index("fsdp") // 2

    def join(here, there):
        return jnp.concatenate(
            [jnp.where(chip == 0, here[0], there[0]), jnp.where(chip == 0, there[0], here[0])],
            axis=1,
        )

    q_low = turn(join(q_here, q_there), cosine, sine).astype(low)
    k_low = turn(join(k_here, k_there), cosine, sine).astype(low)
    v_low = join(v_here, v_there).astype(low)
    ql_ref[0] = q_low
    kl_ref[0] = k_low
    vl_ref[0] = v_low
    q_scaled = (q_low * (HD ** (-0.5))).astype(low)
    k_rows = k_low.T
    for j in range(span // BLK):
        kv = (j + 1) * BLK
        cols = slice(j * BLK, kv)
        scores = jnp.dot(k_rows[:kv], q_scaled[:, cols], preferred_element_type=full)
        top = jnp.max(scores, axis=0, keepdims=True)
        expo = jnp.exp(scores - top)
        total = jnp.sum(expo, axis=0, keepdims=True)
        probs = (expo * (1.0 / total)).astype(low)
        out_ref[0, :, cols] = jnp.dot(
            v_low[:, :kv], probs, preferred_element_type=full
        ).astype(low)
        lse_ref[0, :, cols] = top + jnp.log(total)


def attention_forward(here, there, cosine, sine):
    heads, _, part = here[0].shape
    span = cosine.shape[1]
    half = pl.BlockSpec((1, HD, part), lambda h: (h, 0, 0))
    spec = pl.BlockSpec((1, HD, span), lambda h: (h, 0, 0))
    table = pl.BlockSpec((HD // 2, span), lambda h: (0, 0))
    field = jax.ShapeDtypeStruct((heads, HD, span), low)
    row = pl.BlockSpec((1, 1, span), lambda h: (h, 0, 0))
    return pl.pallas_call(
        forward_kernel,
        grid=(heads,),
        in_specs=[half] * 6 + [table, table],
        out_specs=[spec, spec, spec, spec, row],
        out_shape=[field, field, field, field, jax.ShapeDtypeStruct((heads, 1, span), full)],
        compiler_params=pltpu.CompilerParams(vmem_limit_bytes=60 * 2**20),
        cost_estimate=SMALL,
        name="attention_forward",
    )(*here, *there, cosine, sine)


def backward_kernel(
    q_ref, k_ref, v_ref, g_ref, lse_ref, cos_ref, sin_ref, dq_ref, dk_ref, dv_ref, dk_acc, dv_acc
):
    cosine, sine = cos_ref[...], sin_ref[...]
    span = q_ref.shape[2]
    q_scaled = (q_ref[0] * (HD ** (-0.5))).astype(low)
    k_low, v_low, grad = k_ref[0], v_ref[0], g_ref[0]
    k_rows, v_rows = k_low.T, v_low.T
    dk_acc[...] = jnp.zeros_like(dk_acc)
    dv_acc[...] = jnp.zeros_like(dv_acc)
    for j in range(span // BLK):
        kv = (j + 1) * BLK
        cols = slice(j * BLK, kv)
        q_j, g_j = q_scaled[:, cols], grad[:, cols]
        scores = jnp.dot(k_rows[:kv], q_j, preferred_element_type=full)
        probs = jnp.exp(scores - lse_ref[0, :, cols])
        probs_low = probs.astype(low)
        d_probs = jnp.dot(v_rows[:kv], g_j, preferred_element_type=full)
        delta = jnp.sum(probs * d_probs, axis=0, keepdims=True)
        d_scores = (probs * (d_probs - delta)).astype(low)
        dq = jnp.dot(k_low[:, :kv], d_scores, preferred_element_type=full) * (HD ** (-0.5))
        dq_ref[0, :, cols] = turn(dq, cosine[:, cols], -sine[:, cols]).astype(low)
        dk_acc[:, :kv] += lax.dot_general(q_j, d_scores, NT, preferred_element_type=full)
        dv_acc[:, :kv] += lax.dot_general(g_j, probs_low, NT, preferred_element_type=full)
    dk_ref[0] = turn(dk_acc[...], cosine, -sine).astype(low)
    dv_ref[0] = dv_acc[...].astype(low)


def attention_backward(query, key, value, grad, lse, cosine, sine):
    heads, _, span = query.shape
    spec = pl.BlockSpec((1, HD, span), lambda h: (h, 0, 0))
    table = pl.BlockSpec((HD // 2, span), lambda h: (0, 0))
    row = pl.BlockSpec((1, 1, span), lambda h: (h, 0, 0))
    field = jax.ShapeDtypeStruct((heads, HD, span), low)
    return pl.pallas_call(
        backward_kernel,
        grid=(heads,),
        in_specs=[spec, spec, spec, spec, row, table, table],
        out_specs=[spec, spec, spec],
        out_shape=[field, field, field],
        scratch_shapes=[pltpu.VMEM((HD, span), full), pltpu.VMEM((HD, span), full)],
        compiler_params=pltpu.CompilerParams(vmem_limit_bytes=60 * 2**20),
        cost_estimate=SMALL,
        name="attention_backward",
    )(query, key, value, grad, lse, cosine, sine)


def swap(array, j):
    size = lax.axis_size("fsdp")
    return lax.ppermute(array, "fsdp", [(i, i ^ j) for i in range(size)])


def after(value, *earlier):
    return lax.optimization_barrier((value, *earlier))[0]


def place_kernel(*refs):
    *blocks, out, held, arrived, left = refs
    me = lax.axis_index("fsdp")
    into = [
        pltpu.make_async_copy(block, held.at[j], arrived.at[j]) for j, block in enumerate(blocks)
    ]
    back = [
        pltpu.make_async_copy(
            held.at[j], out.at[lax.bitwise_xor(me, jnp.int32(j))], left.at[j]
        )
        for j in range(len(blocks))
    ]
    for copy in into:
        copy.start()
    for copy, then in zip(into, back):
        copy.wait()
        then.start()
    for copy in back:
        copy.wait()


def place(blocks):
    count = len(blocks)
    first = blocks[0]
    whole = pl.pallas_call(
        place_kernel,
        in_specs=[pl.BlockSpec(memory_space=pl.ANY)] * count,
        out_specs=pl.BlockSpec(memory_space=pl.ANY),
        out_shape=jax.ShapeDtypeStruct((count,) + first.shape, first.dtype),
        scratch_shapes=[
            pltpu.VMEM((count,) + first.shape, first.dtype),
            pltpu.SemaphoreType.DMA((count,)),
            pltpu.SemaphoreType.DMA((count,)),
        ],
        compiler_params=pltpu.CompilerParams(vmem_limit_bytes=16 * 2**20),
        cost_estimate=SMALL,
        name="place",
    )(*blocks)
    return whole.reshape((count * first.shape[0],) + first.shape[1:])


def gather(array, *before_last):
    core = swap(array, 1)
    chip = swap(array, 2)
    return [array, core, chip, swap(after(chip, *before_last) if before_last else chip, 1)]


def bring(blocks, held, arrived, rest=None):
    me = lax.axis_index("fsdp")
    cols = held.shape[1]
    count = len(blocks)
    copies = []
    for j, block in enumerate(blocks):
        to = held.at[lax.bitwise_xor(me, jnp.int32(j))]
        if rest is None:
            copies.append(pltpu.make_async_copy(block, to, arrived.at[j]))
        else:
            copies.append(pltpu.make_async_copy(block.at[pl.ds(0, cols)], to, arrived.at[j]))
            copies.append(
                pltpu.make_async_copy(
                    block.at[pl.ds(cols, 16)], rest.at[j], arrived.at[count + j]
                )
            )
    for copy in copies:
        copy.start()
    for copy in copies:
        copy.wait()


def spread_kernel(index, *refs, count, kept, normalize):
    step = pl.program_id(0)
    blocks, gain = refs[:count], refs[count]
    outs = refs[count + 1 + kept :]
    me = index[count]
    for j, block in enumerate(blocks):

        @pl.when(step == j)
        def _():
            x = block[...].astype(full)
            cols = outs[1].shape[0]
            if normalize:
                factor = lax.rsqrt(jnp.mean(x * x, axis=-1, keepdims=True) + epsilon)
                wide = (x * factor * gain[...]).astype(low)
                outs[2][...] = wide.T
            else:
                wide = (branch_scale * x).astype(low)
            outs[0][...] = wide
            for g in range(x.shape[1] // cols):

                @pl.when(me == g)
                def _():
                    outs[1][...] = x[:, g * cols : (g + 1) * cols].T


def spread(blocks, partners, gain, normalize, earlier=None):
    rows, width = blocks[0].shape
    size = lax.axis_size("fsdp")
    count = len(blocks)
    me = lax.axis_index("fsdp")
    tokens = [me ^ j for j in partners]
    local = [block % count for block in tokens]
    index = jnp.stack([jnp.asarray(v, jnp.int32) for v in (*local, me, *tokens)])
    const = lambda shape: pl.BlockSpec(shape, lambda i, index: (0,) * len(shape))
    kept = len(earlier) if earlier else 0
    outs = [
        (
            pl.BlockSpec((rows, width), lambda i, index: (index[i], 0)),
            jax.ShapeDtypeStruct((count * rows, width), low),
        ),
        (
            pl.BlockSpec((width // size, rows), lambda i, index: (0, index[count + 1 + i])),
            jax.ShapeDtypeStruct((width // size, size * rows), full),
        ),
    ]
    if normalize:
        outs.append(
            (
                pl.BlockSpec((width, rows), lambda i, index: (0, index[count + 1 + i])),
                jax.ShapeDtypeStruct((width, size * rows), low),
            )
        )
    return pl.pallas_call(
        lambda *refs: spread_kernel(*refs, count=count, kept=kept, normalize=normalize),
        grid_spec=pltpu.PrefetchScalarGridSpec(
            num_scalar_prefetch=1,
            grid=(count,),
            in_specs=[const((rows, width))] * count
            + [const((1, width))]
            + [pl.BlockSpec(memory_space=pl.ANY)] * kept,
            out_specs=[spec for spec, _ in outs],
        ),
        out_shape=[shape for _, shape in outs],
        input_output_aliases={count + 2 + i: 1 + i for i in range(kept)},
        compiler_params=pltpu.CompilerParams(vmem_limit_bytes=32 * 2**20),
        cost_estimate=SMALL,
        name="spread",
    )(index, *blocks, gain[None, :], *(earlier or ()))


def hidden_kernel(
    own, core, chip, both, weight, tokens, gain, hidden_ref, scaled_ref, all_ref,
    squares_ref, held, arrived, left,
):
    step = pl.program_id(0)
    out = pltpu.make_async_copy(held, all_ref, left.at[0])

    @pl.when(step == 0)
    def _():
        bring((own, core, chip, both), held, arrived)
        out.start()

    span = held.shape[2]
    result = jnp.dot(
        weight[...], held[...].reshape(-1, span), preferred_element_type=full
    )
    hidden = tokens[...] + branch_scale * result
    tile = hidden.shape[0]
    at = pl.multiple_of(step * tile, tile)
    hidden_ref[pl.ds(at, tile), :] = hidden
    scaled_ref[pl.ds(at, tile), :] = (hidden * gain[...]).astype(low)
    squares = jnp.sum(hidden * hidden, axis=0, keepdims=True)

    @pl.when(step == 0)
    def _():
        squares_ref[...] = squares

    @pl.when(step != 0)
    def _():
        squares_ref[...] += squares

    @pl.when(step == pl.num_programs(0) - 1)
    def _():
        total = squares_ref[...]
        high = total.astype(low)
        rest = (total - high.astype(full)).astype(low)
        cols = hidden_ref.shape[0]
        scaled_ref[cols : cols + 8] = jnp.broadcast_to(high, (8, high.shape[1]))
        scaled_ref[cols + 8 :] = jnp.broadcast_to(rest, (8, high.shape[1]))
        out.wait()


def hidden_state(blocks, weight, tokens, gain):
    cols, span = blocks[0].shape
    size = len(blocks)
    tiles = 2
    tile = cols // tiles
    hbm = pl.BlockSpec(memory_space=pl.ANY)
    rows = lambda wide: pl.BlockSpec((tile, wide), lambda i: (i, 0))
    const = lambda shape: pl.BlockSpec(shape, lambda i: (0, 0))
    hidden, scaled, whole = pl.pallas_call(
        hidden_kernel,
        grid=(tiles,),
        in_specs=[hbm] * 4 + [rows(size * cols), rows(span), rows(1)],
        out_specs=[const((cols, span)), const((cols + 16, span)), hbm],
        out_shape=[
            jax.ShapeDtypeStruct((cols, span), full),
            jax.ShapeDtypeStruct((cols + 16, span), low),
            jax.ShapeDtypeStruct((size, cols, span), low),
        ],
        scratch_shapes=[
            pltpu.VMEM((1, span), full),
            pltpu.VMEM((size, cols, span), low),
            pltpu.SemaphoreType.DMA((size,)),
            pltpu.SemaphoreType.DMA((1,)),
        ],
        compiler_params=pltpu.CompilerParams(vmem_limit_bytes=60 * 2**20),
        cost_estimate=SMALL,
        name="hidden_state",
    )(*blocks, weight, tokens, gain)
    return hidden, scaled, whole.reshape(size * cols, span)


def inner_kernel(
    own, core, chip, both, w_gate, w_up, d_inner, inner_ref, d_gate_ref, d_up_ref, mean_ref, factor_ref,
    all_ref, held, rest, arrived, left,
):
    step = pl.program_id(0)
    out = pltpu.make_async_copy(held, all_ref, left.at[0])
    span = held.shape[2]

    @pl.when(step == 0)
    def _():
        bring((own, core, chip, both), held, arrived, rest)
        out.start()
        squares = [
            rest[j, 0:1].astype(full) + rest[j, 8:9].astype(full) for j in range(held.shape[0])
        ]
        total = (squares[0] + squares[1]) + (squares[2] + squares[3])
        factor_ref[...] = lax.rsqrt(total / (held.shape[0] * held.shape[1]) + epsilon)

        mean_ref[...] = jnp.zeros_like(mean_ref)

    wide = span // 4
    for part in range(4):
        cut = slice(part * wide, (part + 1) * wide)
        scaled = held[:, :, cut].reshape(-1, wide)
        factor = factor_ref[:, cut]
        gate = factor * jnp.dot(w_gate[...], scaled, preferred_element_type=full)
        up = factor * jnp.dot(w_up[...], scaled, preferred_element_type=full)
        sigmoid = 0.5 * jnp.tanh(0.5 * gate) + 0.5
        activated = gate * sigmoid
        inner_ref[:, cut] = (activated * up).astype(low)
        grad = factor * d_inner[:, cut].astype(full)
        d_up = grad * activated
        d_gate = grad * up * (sigmoid + activated * (1.0 - sigmoid))
        d_gate_ref[:, cut] = d_gate.astype(low)
        d_up_ref[:, cut] = d_up.astype(low)
        mean_ref[:, cut] += jnp.sum(d_gate * gate + d_up * up, axis=0, keepdims=True)

    @pl.when(step == pl.num_programs(0) - 1)
    def _():
        out.wait()


def inner_part(blocks, w_gate, w_up, d_inner):
    tall, span = blocks[0].shape
    cols = tall - 16
    size = len(blocks)
    units = w_gate.shape[0]
    tile = units // 3
    hbm = pl.BlockSpec(memory_space=pl.ANY)
    rows = lambda wide: pl.BlockSpec((tile, wide), lambda i: (i, 0))
    row = pl.BlockSpec((1, span), lambda i: (0, 0))
    field = jax.ShapeDtypeStruct((units, span), low)
    inner, d_gate, d_up, mean, factor, whole = pl.pallas_call(
        inner_kernel,
        grid=(units // tile,),
        in_specs=[hbm] * 4 + [rows(size * cols), rows(size * cols), rows(span)],
        out_specs=[rows(span), rows(span), rows(span), row, row, hbm],
        out_shape=[
            field,
            field,
            field,
            jax.ShapeDtypeStruct((1, span), full),
            jax.ShapeDtypeStruct((1, span), full),
            jax.ShapeDtypeStruct((size, cols, span), low),
        ],
        scratch_shapes=[
            pltpu.VMEM((size, cols, span), low),
            pltpu.VMEM((size, 16, span), low),
            pltpu.SemaphoreType.DMA((2 * size,)),
            pltpu.SemaphoreType.DMA((1,)),
        ],
        compiler_params=pltpu.CompilerParams(vmem_limit_bytes=60 * 2**20),
        cost_estimate=SMALL,
        name="inner_part",
    )(*blocks, w_gate, w_up, d_inner)
    return inner, d_gate, d_up, mean, factor, whole.reshape(size * cols, span)


def to_rows(field, rows):
    me = lax.axis_index("fsdp")
    size = lax.axis_size("fsdp")
    blocks = []
    for j in range(size):
        block = lax.dynamic_slice_in_dim(field, (me ^ j) * rows, rows, 1)
        blocks.append(block if j == 0 else swap(block, j))
    return place(blocks).T


def product_kernel(index, act, *refs, count, adds, turned):
    grads = refs[:count]
    added = refs[count] if adds else None
    out = refs[-1]
    rows = act[:, 0].reshape(-1, act.shape[-1])
    for k in range(count):
        pair = (grads[k][...], rows) if turned else (rows, grads[k][...])
        total = lax.dot_general(*pair, NT, preferred_element_type=full)
        if turned:
            if adds:
                total = total + added[0, k].astype(full)
            out[0, k] = total.astype(low)
            continue
        total = total.reshape((act.shape[0], act.shape[2]) + total.shape[1:])
        if adds:
            total = total + added[:, k].astype(full)
        out[:, k] = total.astype(low)


def half_product(act, grads, side, added=None, turned=False, earlier=()):
    size = lax.axis_size("rep")
    count = len(grads)
    columns, tokens = grads[0].shape
    lines, rows = size // 2, act.shape[0] // size
    index = jnp.asarray(side, jnp.int32)[None]
    if earlier:
        index = after(index, *earlier)
    steps = lines
    some = lines // steps
    shape = (columns, rows) if turned else (rows, columns)
    piece = pl.BlockSpec((some, count) + shape, lambda i, index: (i, 0, 0, 0))
    return pl.pallas_call(
        lambda *refs: product_kernel(*refs, count=count, adds=added is not None, turned=turned),
        grid_spec=pltpu.PrefetchScalarGridSpec(
            num_scalar_prefetch=1,
            grid=(steps,),
            in_specs=[pl.BlockSpec((some, 1, rows, tokens), lambda i, index: (i, index[0], 0, 0))]
            + [pl.BlockSpec((columns, tokens), lambda i, index: (0, 0))] * count
            + ([] if added is None else [piece]),
            out_specs=piece,
        ),
        out_shape=jax.ShapeDtypeStruct((lines, count) + shape, low),
        compiler_params=pltpu.CompilerParams(vmem_limit_bytes=60 * 2**20),
        cost_estimate=SMALL,
        name="half_product",
    )(index, act.reshape(lines, 2, rows, tokens), *grads, *(() if added is None else (added,)))


def whole_kernel(act, grad, out):
    out[0] = lax.dot_general(act[0], grad[...], NT, preferred_element_type=full).astype(low)


def whole_product(act, grad):
    lines = lax.axis_size("rep") // 2
    columns, tokens = grad.shape
    rows = act.shape[0] // lines
    return pl.pallas_call(
        whole_kernel,
        grid=(lines,),
        in_specs=[
            pl.BlockSpec((1, rows, tokens), lambda i: (i, 0, 0)),
            pl.BlockSpec((columns, tokens), lambda i: (0, 0)),
        ],
        out_specs=pl.BlockSpec((1, rows, columns), lambda i: (i, 0, 0)),
        out_shape=jax.ShapeDtypeStruct((lines, rows, columns), low),
        compiler_params=pltpu.CompilerParams(vmem_limit_bytes=60 * 2**20),
        cost_estimate=SMALL,
        name="whole_product",
    )(act.reshape(lines, rows, tokens), grad)


def neighbour(array):
    return lax.ppermute(array, "rep", [(i, i ^ 1) for i in range(lax.axis_size("rep"))])


def line_scatter(array):
    size = lax.axis_size("rep")
    groups = [list(range(side, size, 2)) for side in range(2)]
    return lax.psum_scatter(
        array, "rep", scatter_dimension=0, tiled=True, axis_index_groups=groups
    )


class GradSum:
    def __init__(self, act, grads, turned=False):
        self.act, self.grads, self.turned = act, grads, turned
        self.side = lax.axis_index("rep") % 2

    def send(self, earlier=()):
        sent = half_product(
            self.act, self.grads, 1 - self.side, turned=self.turned, earlier=earlier
        )
        self.arrived = neighbour(sent)
        return sent

    def keep(self, earlier=(), last=None):
        kept = half_product(
            self.act, self.grads, self.side, self.arrived, turned=self.turned, earlier=earlier
        )
        self.sums = line_scatter(kept if last is None else after(kept, last.sums))
        return kept

    def line_first(self, earlier=()):
        whole = whole_product(self.act, after(self.grads[0], *earlier))
        self.sums = line_scatter(whole)
        return whole

    def sides_last(self, earlier=()):
        _, rows, columns = self.sums.shape
        parts = self.sums.reshape(2, rows // 2, columns)
        side = after(self.side, *earlier)
        sent = lax.dynamic_index_in_dim(parts, 1 - side, 0, False)
        kept = lax.dynamic_index_in_dim(parts, side, 0, False)
        return kept.astype(full) + neighbour(sent).astype(full)

    def result(self):
        return [self.sums[0, k].astype(full) for k in range(len(self.grads))]


def sum_everywhere(array):
    array = (array + swap(array, 1)) + (swap(array, 2) + swap(array, 3))
    size = lax.axis_size("rep")
    far = 1
    while far < size:
        array = array + lax.ppermute(array, "rep", [(i, i ^ far) for i in range(size)])
        far *= 2
    return array


def flip_kernel(*refs):
    count = len(refs) // 2
    for wide, tall in zip(refs[:count], refs[count:]):
        tall[...] = wide[...].T


def flip(arrays, tiles, earlier=()):
    width = arrays[0].shape[1]
    tile = width // tiles
    index = jnp.zeros((1,), jnp.int32)
    if earlier:
        index = after(index, *earlier)
    return pl.pallas_call(
        lambda index, *refs: flip_kernel(*refs),
        grid_spec=pltpu.PrefetchScalarGridSpec(
            num_scalar_prefetch=1,
            grid=(tiles,),
            in_specs=[pl.BlockSpec((a.shape[0], tile), lambda i, index: (0, i)) for a in arrays],
            out_specs=[pl.BlockSpec((tile, a.shape[0]), lambda i, index: (i, 0)) for a in arrays],
        ),
        out_shape=[jax.ShapeDtypeStruct((width, a.shape[0]), a.dtype) for a in arrays],
        compiler_params=pltpu.CompilerParams(vmem_limit_bytes=60 * 2**20),
        cost_estimate=SMALL,
        name="flip",
    )(index, *arrays)


def chunks_kernel(index, *refs, count, ways, added, extra):
    step = pl.program_id(0)
    weights, refs = refs[:count], refs[count:]
    grads, refs = refs[:count], refs[count:]
    plus, refs = refs[:added], refs[added:]
    row, outs = refs[:extra], refs[extra:]
    total = None
    for weight, grad in zip(weights, grads):
        term = jnp.dot(weight[...], grad[...], preferred_element_type=full)
        total = term if total is None else total + term
    cols = total.shape[0]
    for way, out in enumerate(outs):

        @pl.when(step == way)
        def _():
            found = total + plus[way][:cols].astype(full) if plus else total
            out[:cols] = found.astype(out.dtype)
            if row:
                found = row[0][...]
                if plus:
                    found = found + plus[way][cols : cols + 1].astype(full)
                out[cols:] = jnp.broadcast_to(
                    found.astype(out.dtype), (out.shape[0] - cols, found.shape[1])
                )


def feature_chunks(weights, grads, partners, plus=(), extra=None, dtype=low, earlier=()):
    me = lax.axis_index("fsdp")
    span = grads[0].shape[1]
    cols = weights[0].shape[0] // lax.axis_size("fsdp")
    tall = cols + (0 if extra is None else 16)
    index = jnp.stack([jnp.asarray(me ^ j, jnp.int32) for j in partners])
    if earlier:
        index = after(index, *earlier)
    extra = () if extra is None else (extra,)
    const = lambda shape: pl.BlockSpec(shape, lambda i, index: (0, 0))
    return pl.pallas_call(
        lambda *refs: chunks_kernel(
            *refs, count=len(weights), ways=len(partners), added=len(plus), extra=len(extra)
        ),
        grid_spec=pltpu.PrefetchScalarGridSpec(
            num_scalar_prefetch=1,
            grid=(len(partners),),
            in_specs=[
                pl.BlockSpec((cols, w.shape[1]), lambda i, index: (index[i], 0)) for w in weights
            ]
            + [const(a.shape) for a in (*grads, *plus, *extra)],
            out_specs=[const((tall, span))] * len(partners),
        ),
        out_shape=[jax.ShapeDtypeStruct((tall, span), dtype)] * len(partners),
        compiler_params=pltpu.CompilerParams(vmem_limit_bytes=60 * 2**20),
        cost_estimate=SMALL,
        name="feature_chunks",
    )(index, *weights, *grads, *plus, *extra)


def blocks_kernel(index, *refs, count, added):
    step = pl.program_id(0)
    weights, refs = refs[:count], refs[count:]
    grads, refs = refs[:count], refs[count:]
    plus, outs = refs[:added], refs[added:]
    total = None
    for weight, grad in zip(weights, grads):
        term = jnp.dot(grad[...].T, weight[...], preferred_element_type=full)
        total = term if total is None else total + term
    for way, out in enumerate(outs):

        @pl.when(step == way)
        def _():
            found = total + plus[way][...].astype(full) if plus else total
            out[...] = found.astype(out.dtype)


def token_chunks(weights, grads, partners, rows, plus=(), dtype=low, earlier=()):
    me = lax.axis_index("fsdp")
    width = weights[0].shape[1]
    index = jnp.stack([jnp.asarray(me ^ j, jnp.int32) for j in partners])
    if earlier:
        index = after(index, *earlier)
    const = lambda shape: pl.BlockSpec(shape, lambda i, index: (0, 0))
    return pl.pallas_call(
        lambda *refs: blocks_kernel(*refs, count=len(weights), added=len(plus)),
        grid_spec=pltpu.PrefetchScalarGridSpec(
            num_scalar_prefetch=1,
            grid=(len(partners),),
            in_specs=[const(w.shape) for w in weights]
            + [pl.BlockSpec((g.shape[0], rows), lambda i, index: (0, index[i])) for g in grads]
            + [const(a.shape) for a in plus],
            out_specs=[const((rows, width))] * len(partners),
        ),
        out_shape=[jax.ShapeDtypeStruct((rows, width), dtype)] * len(partners),
        compiler_params=pltpu.CompilerParams(vmem_limit_bytes=60 * 2**20),
        cost_estimate=SMALL,
        name="token_chunks",
    )(index, *weights, *grads, *plus)


def body(
    tokens, cotangent, gain_attn, gain_ffn, w_query, w_key, w_value, w_out, w_gate, w_up, w_down
):
    rows, width = tokens.shape
    size = lax.axis_size("fsdp")
    reps = lax.axis_size("rep")
    span = rows * size
    me = lax.axis_index("fsdp")
    replica = lax.axis_index("rep")
    width_cols = width // size
    hidden_cols = w_gate.shape[1]
    heads = width_cols // HD

    half = HD // 2
    frequency = 10000.0 ** (-(jnp.arange(half, dtype=full) * 2.0 / HD))
    angles = frequency[:, None] * jnp.arange(span, dtype=jnp.int32).astype(full)[None, :]
    cosine, sine = jnp.cos(angles), jnp.sin(angles)

    def own_gain(gain):
        return lax.dynamic_slice_in_dim(gain, me * width_cols, width_cols, 0)[:, None]

    down_turned = w_down.T
    share = width_cols // reps

    def down_part(j):
        return lax.dynamic_slice(
            down_turned, (replica * share, (me ^ j) * hidden_cols), (share, hidden_cols)
        )

    parts = [down_part(2), down_part(3)]

    def project(normed):
        found = []
        for weight in (w_query, w_key, w_value):
            field = jnp.einsum("de,td->et", weight, normed, preferred_element_type=full)
            found.append(field.reshape(heads, HD, normed.shape[0]))
        return found

    tokens_chip = swap(tokens, 2)
    normed_here, tokens_part, normed_part = spread(
        [tokens, swap(tokens, 1)], (0, 1), gain_attn, True
    )
    here = project(normed_here)
    tokens_chip = after(tokens_chip, *here)
    parts = [swap(after(part, tokens_chip), 2) for part in parts]
    normed_there, tokens_own, normed_turned = spread(
        [tokens_chip, swap(tokens_chip, 1)],
        (2, 3),
        gain_attn,
        True,
        (tokens_part, normed_part),
    )
    there = project(normed_there)
    parts = [after(part, *there) for part in parts]
    cotangent_chip = swap(after(cotangent, *parts), 2)
    parts_all = lax.all_gather(
        jnp.stack([parts[0], swap(parts[1], 1)]), "rep", axis=1, tiled=True
    )
    attended, query_low, key_low, value_low, lse = attention_forward(here, there, cosine, sine)

    cotangent_blocks = [
        cotangent, swap(cotangent, 1), cotangent_chip, swap(after(cotangent_chip, attended), 1)
    ]
    d_ffn, cotangent_own = spread(cotangent_blocks, (0, 1, 2, 3), gain_attn, False)
    d_ffn_own = (branch_scale * cotangent_own).astype(low)
    me_later = after(me, d_ffn)

    def down_block(j):
        return lax.dynamic_slice_in_dim(
            down_turned, (me_later ^ j) * hidden_cols, hidden_cols, 1
        )

    down_near = [down_block(0), swap(down_block(1), 1)]
    gate_tall, up_tall = flip([w_gate.T, w_up.T], 6, [down_near[0]])
    (out_tall,) = flip([w_out.T], 6, [gate_tall])
    attended_blocks = gather(attended.reshape(width_cols, span), out_tall)

    gain_own = own_gain(gain_ffn)
    hidden, scaled, attended_all = hidden_state(attended_blocks, w_out.T, tokens_own, gain_own)
    down_own = place([after(down_near[0], scaled), down_near[1], parts_all[0], parts_all[1]])
    d_inner = jnp.einsum("ef,te->ft", down_own, d_ffn, preferred_element_type=full).astype(low)
    scaled_blocks = gather(scaled, d_inner)

    inner, d_gate, d_up, mean, factor, scaled_all = inner_part(
        scaled_blocks, w_gate.T, w_up.T, d_inner
    )

    sum_up = GradSum(scaled_all, [d_up])
    sum_gate = GradSum(scaled_all, [d_gate])
    ffn_weights, ffn_grads = (gate_tall, up_tall), (d_gate, d_up)
    token = sum_up.line_first()
    far, near = feature_chunks(ffn_weights, ffn_grads, (3, 1), extra=mean, earlier=[token])
    token = sum_gate.send([far])
    far, near = swap(far, 1), swap(near, 1)
    (chunk,) = feature_chunks(
        ffn_weights, ffn_grads, (2,), plus=[far], extra=mean, earlier=[token]
    )
    across = swap(chunk, 2)
    (own,) = feature_chunks(
        ffn_weights, ffn_grads, (0,), plus=[near], extra=mean, dtype=full, earlier=[chunk]
    )
    d_scaled = own + across.astype(full)
    mean_ffn = d_scaled[width_cols : width_cols + 1] / width
    d_scaled = d_scaled[:width_cols]
    gain_ffn_term = jnp.sum(d_scaled * hidden, axis=1)
    d_hidden = cotangent_own + gain_own * d_scaled - hidden * (factor * mean_ffn)
    d_attn = (branch_scale * d_hidden).astype(low)

    far, near = feature_chunks([out_tall], [d_attn], (3, 1))
    far, near = swap(far, 1), swap(near, 1)
    (chunk,) = feature_chunks([out_tall], [d_attn], (2,), plus=[far])
    across = swap(chunk, 2)
    (own,) = feature_chunks(
        [out_tall], [d_attn], (0,), plus=[near], dtype=full, earlier=[chunk]
    )
    sum_out = GradSum(attended_all, [d_attn])
    token = sum_out.send([own])
    d_attended = own + after(across, token).astype(full)
    d_attended = d_attended.astype(low).reshape(heads, HD, span)
    inner_chip = swap(after(inner, d_attended), 2)
    token = sum_gate.keep([d_attended], sum_up)

    d_query, d_key, d_value = (
        field.reshape(width_cols, span)
        for field in attention_backward(
            query_low, key_low, value_low, d_attended, after(lse, token), cosine, sine
        )
    )
    attn_weights, attn_grads = (w_query.T, w_key.T, w_value.T), (d_query, d_key, d_value)
    far, near = token_chunks(attn_weights, attn_grads, (3, 1), rows)
    sum_attn = GradSum(normed_turned, [d_query, d_key, d_value])
    token = sum_attn.send([far])
    far, near = swap(far, 1), swap(near, 1)
    (chunk,) = token_chunks(attn_weights, attn_grads, (2,), rows, plus=[far], earlier=[token])
    across = swap(chunk, 2)
    (own,) = token_chunks(
        attn_weights, attn_grads, (0,), rows, plus=[near], dtype=full, earlier=[chunk]
    )
    token = sum_out.keep([own], sum_gate)

    inner_both = swap(after(inner_chip, token), 1)
    inner_all = place([inner, swap(inner, 1), inner_chip, inner_both])
    sum_down = GradSum(inner_all, [d_ffn_own], turned=True)
    token = sum_down.send()
    ffn_result = jnp.einsum(
        "fe,ft->et", w_down, after(inner_all, token), preferred_element_type=full
    )
    output_turned = (hidden + branch_scale * ffn_result).astype(low)
    output = to_rows(output_turned, rows)
    hidden_rows = to_rows(after(d_hidden.astype(low), output_turned), rows).astype(full)

    d_normed = own + after(across, output_turned).astype(full)
    x_own = tokens.astype(full)
    factor_own = lax.rsqrt(jnp.mean(x_own * x_own, axis=-1, keepdims=True) + epsilon)
    unit_own = x_own * factor_own
    part = d_normed * gain_attn
    gain_attn_term = jnp.sum(d_normed * unit_own, axis=0)
    gain_ffn_wide = lax.dynamic_update_slice_in_dim(
        jnp.zeros((width,), full), gain_ffn_term, me * width_cols, 0
    )
    d_tokens = hidden_rows + factor_own * (
        part - unit_own * jnp.mean(part * unit_own, axis=-1, keepdims=True)
    )
    grad_up = sum_up.sides_last([output_turned])
    token = sum_attn.keep([gain_attn_term], sum_out)
    grad_gain_attn, grad_gain_ffn = sum_everywhere(
        jnp.stack([after(gain_attn_term, token), gain_ffn_wide])
    )
    token = sum_down.keep([token, d_tokens], sum_attn)
    grad_query, grad_key, grad_value = sum_attn.result()
    (grad_out,) = sum_out.result()
    (grad_gate,) = sum_gate.result()
    (grad_down,) = sum_down.result()
    return (
        output,
        d_tokens,
        grad_gain_attn,
        grad_gain_ffn,
        grad_query,
        grad_key,
        grad_value,
        grad_out,
        grad_gate,
        grad_up,
        grad_down.T,
    )


def solution(mesh):
    rows = P(("rep", "fsdp"), None)
    columns = P(None, "fsdp")
    both = P("rep", "fsdp")
    return jax.shard_map(
        body,
        mesh=mesh,
        in_specs=(rows, rows, P(), P()) + (columns,) * 7,
        out_specs=(rows, rows, P(), P()) + (both,) * 7,
        check_vma=False,
    )
```

```python
import math

import jax
import jax.numpy as jnp
from jax import lax
from jax.experimental import pallas as pl
from jax.experimental.pallas import tpu as pltpu
from jax.sharding import PartitionSpec as P

HD = 64
BLK = 256
NT = (((1,), (1,)), ((), ()))

epsilon = 1e-05
branch_scale = 1.4 / math.sqrt(40.0)
low = jnp.bfloat16
full = jnp.float32

SMALL = pl.CostEstimate(flops=0, bytes_accessed=0, transcendentals=0)


def turn(field, cosine, sine):
    half = field.shape[0] // 2
    first, second = field[:half], field[half:]
    return jnp.concatenate(
        [first * cosine - second * sine, second * cosine + first * sine], axis=0
    )


def forward_kernel(
    q_here, k_here, v_here, q_there, k_there, v_there, cos_ref, sin_ref,
    out_ref, ql_ref, kl_ref, vl_ref, lse_ref,
):
    cosine, sine = cos_ref[...], sin_ref[...]
    span = cosine.shape[1]
    chip = lax.axis_index("fsdp") // 2

    def join(here, there):
        return jnp.concatenate(
            [jnp.where(chip == 0, here[0], there[0]), jnp.where(chip == 0, there[0], here[0])],
            axis=1,
        )

    q_low = turn(join(q_here, q_there), cosine, sine).astype(low)
    k_low = turn(join(k_here, k_there), cosine, sine).astype(low)
    v_low = join(v_here, v_there).astype(low)
    ql_ref[0] = q_low
    kl_ref[0] = k_low
    vl_ref[0] = v_low
    q_scaled = (q_low * (HD ** (-0.5))).astype(low)
    k_rows = k_low.T
    for j in range(span // BLK):
        kv = (j + 1) * BLK
        cols = slice(j * BLK, kv)
        scores = jnp.dot(k_rows[:kv], q_scaled[:, cols], preferred_element_type=full)
        top = jnp.max(scores, axis=0, keepdims=True)
        expo = jnp.exp(scores - top)
        total = jnp.sum(expo, axis=0, keepdims=True)
        probs = (expo * (1.0 / total)).astype(low)
        out_ref[0, :, cols] = jnp.dot(
            v_low[:, :kv], probs, preferred_element_type=full
        ).astype(low)
        lse_ref[0, :, cols] = top + jnp.log(total)


def attention_forward(here, there, cosine, sine):
    heads, _, part = here[0].shape
    span = cosine.shape[1]
    half = pl.BlockSpec((1, HD, part), lambda h: (h, 0, 0))
    spec = pl.BlockSpec((1, HD, span), lambda h: (h, 0, 0))
    table = pl.BlockSpec((HD // 2, span), lambda h: (0, 0))
    field = jax.ShapeDtypeStruct((heads, HD, span), low)
    row = pl.BlockSpec((1, 1, span), lambda h: (h, 0, 0))
    return pl.pallas_call(
        forward_kernel,
        grid=(heads,),
        in_specs=[half] * 6 + [table, table],
        out_specs=[spec, spec, spec, spec, row],
        out_shape=[field, field, field, field, jax.ShapeDtypeStruct((heads, 1, span), full)],
        compiler_params=pltpu.CompilerParams(vmem_limit_bytes=60 * 2**20),
        cost_estimate=SMALL,
        name="attention_forward",
    )(*here, *there, cosine, sine)


def backward_kernel(
    q_ref, k_ref, v_ref, g_ref, h_ref, lse_ref, cos_ref, sin_ref, dq_ref, dk_ref, dv_ref, dk_acc, dv_acc
):
    cosine, sine = cos_ref[...], sin_ref[...]
    span = q_ref.shape[2]
    q_scaled = (q_ref[0] * (HD ** (-0.5))).astype(low)
    k_low, v_low = k_ref[0], v_ref[0]
    grad = (g_ref[0] + h_ref[0].astype(full)).astype(low)
    k_rows, v_rows = k_low.T, v_low.T
    dk_acc[...] = jnp.zeros_like(dk_acc)
    dv_acc[...] = jnp.zeros_like(dv_acc)
    for j in range(span // BLK):
        kv = (j + 1) * BLK
        cols = slice(j * BLK, kv)
        q_j, g_j = q_scaled[:, cols], grad[:, cols]
        scores = jnp.dot(k_rows[:kv], q_j, preferred_element_type=full)
        probs = jnp.exp(scores - lse_ref[0, :, cols])
        probs_low = probs.astype(low)
        d_probs = jnp.dot(v_rows[:kv], g_j, preferred_element_type=full)
        delta = jnp.sum(probs * d_probs, axis=0, keepdims=True)
        d_scores = (probs * (d_probs - delta)).astype(low)
        dq = jnp.dot(k_low[:, :kv], d_scores, preferred_element_type=full) * (HD ** (-0.5))
        dq_ref[0, :, cols] = turn(dq, cosine[:, cols], -sine[:, cols]).astype(low)
        dk_acc[:, :kv] += lax.dot_general(q_j, d_scores, NT, preferred_element_type=full)
        dv_acc[:, :kv] += lax.dot_general(g_j, probs_low, NT, preferred_element_type=full)
    dk_ref[0] = turn(dk_acc[...], cosine, -sine).astype(low)
    dv_ref[0] = dv_acc[...].astype(low)


def attention_backward(query, key, value, grad, rest, lse, cosine, sine):
    heads, _, span = query.shape
    spec = pl.BlockSpec((1, HD, span), lambda h: (h, 0, 0))
    table = pl.BlockSpec((HD // 2, span), lambda h: (0, 0))
    row = pl.BlockSpec((1, 1, span), lambda h: (h, 0, 0))
    field = jax.ShapeDtypeStruct((heads, HD, span), low)
    return pl.pallas_call(
        backward_kernel,
        grid=(heads,),
        in_specs=[spec, spec, spec, spec, spec, row, table, table],
        out_specs=[spec, spec, spec],
        out_shape=[field, field, field],
        scratch_shapes=[pltpu.VMEM((HD, span), full), pltpu.VMEM((HD, span), full)],
        compiler_params=pltpu.CompilerParams(vmem_limit_bytes=60 * 2**20),
        cost_estimate=SMALL,
        name="attention_backward",
    )(query, key, value, grad, rest, lse, cosine, sine)


def swap(array, j):
    size = lax.axis_size("fsdp")
    return lax.ppermute(array, "fsdp", [(i, i ^ j) for i in range(size)])


def after(value, *earlier):
    return lax.optimization_barrier((value, *earlier))[0]


def stage(run, *earlier):
    blank = lambda: jax.tree.map(lambda a: jnp.zeros(a.shape, a.dtype), jax.eval_shape(run))
    return lax.cond(after(jnp.bool_(True), *earlier), run, blank)


def place_kernel(*refs, parts):
    *blocks, out, held, arrived, left = refs
    me = lax.axis_index("fsdp")
    into, back = [], []
    for j in range(held.shape[0]):
        at = 0
        for i in range(j * parts, (j + 1) * parts):
            rows = blocks[i].shape[0]
            into.append(
                pltpu.make_async_copy(blocks[i], held.at[j, pl.ds(at, rows)], arrived.at[i])
            )
            at += rows
        back.append(
            pltpu.make_async_copy(
                held.at[j], out.at[lax.bitwise_xor(me, jnp.int32(j))], left.at[j]
            )
        )
    for copy in into:
        copy.start()
    for j, copy in enumerate(back):
        for part in into[j * parts : (j + 1) * parts]:
            part.wait()
        copy.start()
    for copy in back:
        copy.wait()


def place(blocks, parts=1):
    count = len(blocks)
    size = count // parts
    rows = sum(block.shape[0] for block in blocks[:parts])
    shape = (size, rows, blocks[0].shape[1])
    dtype = blocks[0].dtype
    whole = pl.pallas_call(
        lambda *refs: place_kernel(*refs, parts=parts),
        in_specs=[pl.BlockSpec(memory_space=pl.ANY)] * count,
        out_specs=pl.BlockSpec(memory_space=pl.ANY),
        out_shape=jax.ShapeDtypeStruct(shape, dtype),
        scratch_shapes=[
            pltpu.VMEM(shape, dtype),
            pltpu.SemaphoreType.DMA((count,)),
            pltpu.SemaphoreType.DMA((size,)),
        ],
        compiler_params=pltpu.CompilerParams(vmem_limit_bytes=60 * 2**20),
        cost_estimate=SMALL,
        name="place",
    )(*blocks)
    return whole.reshape(size * rows, shape[2])


def gather(array, *before_last):
    core = swap(array, 1)
    chip = swap(array, 2)
    return [array, core, chip, swap(after(chip, *before_last) if before_last else chip, 1)]


def bring(blocks, held, arrived, rest=None):
    me = lax.axis_index("fsdp")
    cols = held.shape[1]
    count = len(blocks)
    copies = []
    for j, block in enumerate(blocks):
        to = held.at[lax.bitwise_xor(me, jnp.int32(j))]
        if rest is None:
            copies.append(pltpu.make_async_copy(block, to, arrived.at[j]))
        else:
            copies.append(pltpu.make_async_copy(block.at[pl.ds(0, cols)], to, arrived.at[j]))
            copies.append(
                pltpu.make_async_copy(
                    block.at[pl.ds(cols, 16)], rest.at[j], arrived.at[count + j]
                )
            )
    for copy in copies:
        copy.start()
    for copy in copies:
        copy.wait()


def spread_kernel(index, *refs, count, kept, normalize):
    step = pl.program_id(0)
    blocks, gain = refs[:count], refs[count]
    outs = refs[count + 1 + kept :]
    me = index[count]
    for j, block in enumerate(blocks):

        @pl.when(step == j)
        def _():
            x = block[...].astype(full)
            cols = outs[1].shape[0]
            if normalize:
                factor = lax.rsqrt(jnp.mean(x * x, axis=-1, keepdims=True) + epsilon)
                wide = (x * factor * gain[...]).astype(low)
                outs[2][...] = wide.T
            else:
                wide = (branch_scale * x).astype(low)
            outs[0][...] = wide
            for g in range(x.shape[1] // cols):

                @pl.when(me == g)
                def _():
                    outs[1][...] = x[:, g * cols : (g + 1) * cols].T


def spread(blocks, partners, gain, normalize, earlier=None):
    rows, width = blocks[0].shape
    size = lax.axis_size("fsdp")
    count = len(blocks)
    me = lax.axis_index("fsdp")
    tokens = [me ^ j for j in partners]
    local = [block % count for block in tokens]
    index = jnp.stack([jnp.asarray(v, jnp.int32) for v in (*local, me, *tokens)])
    const = lambda shape: pl.BlockSpec(shape, lambda i, index: (0,) * len(shape))
    kept = len(earlier) if earlier else 0
    outs = [
        (
            pl.BlockSpec((rows, width), lambda i, index: (index[i], 0)),
            jax.ShapeDtypeStruct((count * rows, width), low),
        ),
        (
            pl.BlockSpec((width // size, rows), lambda i, index: (0, index[count + 1 + i])),
            jax.ShapeDtypeStruct((width // size, size * rows), full),
        ),
    ]
    if normalize:
        outs.append(
            (
                pl.BlockSpec((width, rows), lambda i, index: (0, index[count + 1 + i])),
                jax.ShapeDtypeStruct((width, size * rows), low),
            )
        )
    return pl.pallas_call(
        lambda *refs: spread_kernel(*refs, count=count, kept=kept, normalize=normalize),
        grid_spec=pltpu.PrefetchScalarGridSpec(
            num_scalar_prefetch=1,
            grid=(count,),
            in_specs=[const((rows, width))] * count
            + [const((1, width))]
            + [pl.BlockSpec(memory_space=pl.ANY)] * kept,
            out_specs=[spec for spec, _ in outs],
        ),
        out_shape=[shape for _, shape in outs],
        input_output_aliases={count + 2 + i: 1 + i for i in range(kept)},
        compiler_params=pltpu.CompilerParams(vmem_limit_bytes=32 * 2**20),
        cost_estimate=SMALL,
        name="spread",
    )(index, *blocks, gain[None, :], *(earlier or ()))


def hidden_kernel(
    own, core, chip, both, weight, tokens, gain, hidden_ref, scaled_ref, all_ref,
    squares_ref, held, arrived, left,
):
    step = pl.program_id(0)
    out = pltpu.make_async_copy(held, all_ref, left.at[0])

    @pl.when(step == 0)
    def _():
        bring((own, core, chip, both), held, arrived)
        out.start()

    span = held.shape[2]
    result = jnp.dot(
        weight[...], held[...].reshape(-1, span), preferred_element_type=full
    )
    hidden = tokens[...] + branch_scale * result
    tile = hidden.shape[0]
    at = pl.multiple_of(step * tile, tile)
    hidden_ref[pl.ds(at, tile), :] = hidden
    scaled_ref[pl.ds(at, tile), :] = (hidden * gain[...]).astype(low)
    squares = jnp.sum(hidden * hidden, axis=0, keepdims=True)

    @pl.when(step == 0)
    def _():
        squares_ref[...] = squares

    @pl.when(step != 0)
    def _():
        squares_ref[...] += squares

    @pl.when(step == pl.num_programs(0) - 1)
    def _():
        total = squares_ref[...]
        high = total.astype(low)
        rest = (total - high.astype(full)).astype(low)
        cols = hidden_ref.shape[0]
        scaled_ref[cols : cols + 8] = jnp.broadcast_to(high, (8, high.shape[1]))
        scaled_ref[cols + 8 :] = jnp.broadcast_to(rest, (8, high.shape[1]))
        out.wait()


def hidden_state(blocks, weight, tokens, gain):
    cols, span = blocks[0].shape
    size = len(blocks)
    tiles = 2
    tile = cols // tiles
    hbm = pl.BlockSpec(memory_space=pl.ANY)
    rows = lambda wide: pl.BlockSpec((tile, wide), lambda i: (i, 0))
    const = lambda shape: pl.BlockSpec(shape, lambda i: (0, 0))
    hidden, scaled, whole = pl.pallas_call(
        hidden_kernel,
        grid=(tiles,),
        in_specs=[hbm] * 4 + [rows(size * cols), rows(span), rows(1)],
        out_specs=[const((cols, span)), const((cols + 16, span)), hbm],
        out_shape=[
            jax.ShapeDtypeStruct((cols, span), full),
            jax.ShapeDtypeStruct((cols + 16, span), low),
            jax.ShapeDtypeStruct((size, cols, span), low),
        ],
        scratch_shapes=[
            pltpu.VMEM((1, span), full),
            pltpu.VMEM((size, cols, span), low),
            pltpu.SemaphoreType.DMA((size,)),
            pltpu.SemaphoreType.DMA((1,)),
        ],
        compiler_params=pltpu.CompilerParams(vmem_limit_bytes=60 * 2**20),
        cost_estimate=SMALL,
        name="hidden_state",
    )(*blocks, weight, tokens, gain)
    return hidden, scaled, whole.reshape(size * cols, span)


def inner_kernel(
    own, core, chip, both, w_gate, w_up, d_inner, inner_ref, grads_ref, mean_ref, factor_ref,
    all_ref, held, rest, arrived, left,
):
    step = pl.program_id(0)
    out = pltpu.make_async_copy(held, all_ref, left.at[0])
    span = held.shape[2]

    @pl.when(step == 0)
    def _():
        bring((own, core, chip, both), held, arrived, rest)
        out.start()
        squares = [
            rest[j, 0:1].astype(full) + rest[j, 8:9].astype(full) for j in range(held.shape[0])
        ]
        total = (squares[0] + squares[1]) + (squares[2] + squares[3])
        factor_ref[...] = lax.rsqrt(total / (held.shape[0] * held.shape[1]) + epsilon)

        mean_ref[...] = jnp.zeros_like(mean_ref)

    wide = span // 4
    for part in range(4):
        cut = slice(part * wide, (part + 1) * wide)
        scaled = held[:, :, cut].reshape(-1, wide)
        factor = factor_ref[:, cut]
        gate = factor * jnp.dot(w_gate[...], scaled, preferred_element_type=full)
        up = factor * jnp.dot(w_up[...], scaled, preferred_element_type=full)
        sigmoid = 0.5 * jnp.tanh(0.5 * gate) + 0.5
        activated = gate * sigmoid
        inner_ref[:, cut] = (activated * up).astype(low)
        grad = factor * d_inner[:, cut].astype(full)
        d_up = grad * activated
        d_gate = grad * up * (sigmoid + activated * (1.0 - sigmoid))
        grads_ref[0, :, cut] = d_gate.astype(low)
        grads_ref[1, :, cut] = d_up.astype(low)
        mean_ref[:, cut] += jnp.sum(d_gate * gate + d_up * up, axis=0, keepdims=True)

    @pl.when(step == pl.num_programs(0) - 1)
    def _():
        out.wait()


def inner_part(blocks, w_gate, w_up, d_inner):
    tall, span = blocks[0].shape
    cols = tall - 16
    size = len(blocks)
    units = w_gate.shape[0]
    tile = units // 3
    hbm = pl.BlockSpec(memory_space=pl.ANY)
    rows = lambda wide: pl.BlockSpec((tile, wide), lambda i: (i, 0))
    row = pl.BlockSpec((1, span), lambda i: (0, 0))
    inner, grads, mean, factor, whole = pl.pallas_call(
        inner_kernel,
        grid=(units // tile,),
        in_specs=[hbm] * 4 + [rows(size * cols), rows(size * cols), rows(span)],
        out_specs=[rows(span), pl.BlockSpec((2, tile, span), lambda i: (0, i, 0)), row, row, hbm],
        out_shape=[
            jax.ShapeDtypeStruct((units, span), low),
            jax.ShapeDtypeStruct((2, units, span), low),
            jax.ShapeDtypeStruct((1, span), full),
            jax.ShapeDtypeStruct((1, span), full),
            jax.ShapeDtypeStruct((size, cols, span), low),
        ],
        scratch_shapes=[
            pltpu.VMEM((size, cols, span), low),
            pltpu.VMEM((size, 16, span), low),
            pltpu.SemaphoreType.DMA((2 * size,)),
            pltpu.SemaphoreType.DMA((1,)),
        ],
        compiler_params=pltpu.CompilerParams(vmem_limit_bytes=60 * 2**20),
        cost_estimate=SMALL,
        name="inner_part",
    )(*blocks, w_gate, w_up, d_inner)
    return inner, grads.reshape(2 * units, span), mean, factor, whole.reshape(size * cols, span)


def to_rows(field, rows):
    me = lax.axis_index("fsdp")
    size = lax.axis_size("fsdp")
    blocks = []
    for j in range(size):
        block = lax.dynamic_slice_in_dim(field, (me ^ j) * rows, rows, 1)
        blocks.append(block if j == 0 else swap(block, j))
    return place(blocks).T


def product_kernel(index, act, *refs, count, adds, turned):
    grads = refs[:count]
    added = refs[count] if adds else None
    out = refs[-1]
    rows = act[:, 0].reshape(-1, act.shape[-1])
    for k in range(count):
        pair = (grads[k][...], rows) if turned else (rows, grads[k][...])
        total = lax.dot_general(*pair, NT, preferred_element_type=full)
        if turned:
            if adds:
                total = total + added[0, k].astype(full)
            out[0, k] = total.astype(low)
            continue
        total = total.reshape((act.shape[0], act.shape[2]) + total.shape[1:])
        if adds:
            total = total + added[:, k].astype(full)
        out[:, k] = total.astype(low)


def half_product(act, grads, side, added=None, turned=False, columns=None, earlier=()):
    size = lax.axis_size("rep")
    count = len(grads)
    tokens = grads[0].shape[1]
    columns = columns or grads[0].shape[0]
    lines, rows = size // 2, act.shape[0] // size
    index = jnp.asarray(side, jnp.int32)[None]
    if earlier:
        index = after(index, *earlier)
    steps = lines
    some = lines // steps
    shape = (columns, rows) if turned else (rows, columns)
    piece = pl.BlockSpec((some, count) + shape, lambda i, index: (i, 0, 0, 0))
    return pl.pallas_call(
        lambda *refs: product_kernel(*refs, count=count, adds=added is not None, turned=turned),
        grid_spec=pltpu.PrefetchScalarGridSpec(
            num_scalar_prefetch=1,
            grid=(steps,),
            in_specs=[pl.BlockSpec((some, 1, rows, tokens), lambda i, index: (i, index[0], 0, 0))]
            + [pl.BlockSpec((columns, tokens), lambda i, index: (0, 0))] * count
            + ([] if added is None else [piece]),
            out_specs=piece,
        ),
        out_shape=jax.ShapeDtypeStruct((lines, count) + shape, low),
        compiler_params=pltpu.CompilerParams(vmem_limit_bytes=60 * 2**20),
        cost_estimate=SMALL,
        name="half_product",
    )(index, act.reshape(lines, 2, rows, tokens), *grads, *(() if added is None else (added,)))


def whole_kernel(act, grad, out):
    out[0] = lax.dot_general(act[0], grad[...], NT, preferred_element_type=full).astype(low)


def whole_product(act, grad, columns):
    lines = lax.axis_size("rep") // 2
    tokens = grad.shape[1]
    last = grad.shape[0] // columns - 1
    rows = act.shape[0] // lines
    return pl.pallas_call(
        whole_kernel,
        grid=(lines,),
        in_specs=[
            pl.BlockSpec((1, rows, tokens), lambda i: (i, 0, 0)),
            pl.BlockSpec((columns, tokens), lambda i: (last, 0)),
        ],
        out_specs=pl.BlockSpec((1, rows, columns), lambda i: (i, 0, 0)),
        out_shape=jax.ShapeDtypeStruct((lines, rows, columns), low),
        compiler_params=pltpu.CompilerParams(vmem_limit_bytes=60 * 2**20),
        cost_estimate=SMALL,
        name="whole_product",
    )(act.reshape(lines, rows, tokens), grad)


def neighbour(array):
    return lax.ppermute(array, "rep", [(i, i ^ 1) for i in range(lax.axis_size("rep"))])


def line_scatter(array):
    size = lax.axis_size("rep")
    groups = [list(range(side, size, 2)) for side in range(2)]
    return lax.psum_scatter(
        array, "rep", scatter_dimension=0, tiled=True, axis_index_groups=groups
    )


class GradSum:
    def __init__(self, act, grads, turned=False, columns=None):
        self.act, self.grads, self.turned, self.columns = act, grads, turned, columns
        self.side = lax.axis_index("rep") % 2

    def send(self, earlier=()):
        sent = half_product(
            self.act,
            self.grads,
            1 - self.side,
            turned=self.turned,
            columns=self.columns,
            earlier=earlier,
        )
        return sent

    def transfer(self, sent):
        self.arrived = neighbour(sent)

    def keep(self, earlier=(), last=None):
        kept = half_product(
            self.act,
            self.grads,
            self.side,
            self.arrived,
            turned=self.turned,
            columns=self.columns,
            earlier=earlier,
        )
        self.sums = line_scatter(kept if last is None else after(kept, last.sums))
        return kept

    def line_first(self, earlier=()):
        whole = whole_product(self.act, after(self.grads[0], *earlier), self.columns)
        self.sums = line_scatter(whole)
        return whole

    def sides_last(self, earlier=()):
        _, rows, columns = self.sums.shape
        parts = self.sums.reshape(2, rows // 2, columns)
        side = after(self.side, *earlier)
        sent = lax.dynamic_index_in_dim(parts, 1 - side, 0, False)
        kept = lax.dynamic_index_in_dim(parts, side, 0, False)
        return kept.astype(full) + neighbour(sent).astype(full)

    def result(self):
        return [self.sums[0, k].astype(full) for k in range(len(self.grads))]


def sum_everywhere(array):
    array = (array + swap(array, 1)) + (swap(array, 2) + swap(array, 3))
    size = lax.axis_size("rep")
    far = 1
    while far < size:
        array = array + lax.ppermute(array, "rep", [(i, i ^ far) for i in range(size)])
        far *= 2
    return array


def flip_kernel(*refs):
    count = len(refs) // 2
    for wide, tall in zip(refs[:count], refs[count:]):
        tall[...] = wide[...].T


def flip(arrays, tiles, earlier=()):
    width = arrays[0].shape[1]
    tile = width // tiles
    index = jnp.zeros((1,), jnp.int32)
    if earlier:
        index = after(index, *earlier)
    return pl.pallas_call(
        lambda index, *refs: flip_kernel(*refs),
        grid_spec=pltpu.PrefetchScalarGridSpec(
            num_scalar_prefetch=1,
            grid=(tiles,),
            in_specs=[pl.BlockSpec((a.shape[0], tile), lambda i, index: (0, i)) for a in arrays],
            out_specs=[pl.BlockSpec((tile, a.shape[0]), lambda i, index: (i, 0)) for a in arrays],
        ),
        out_shape=[jax.ShapeDtypeStruct((width, a.shape[0]), a.dtype) for a in arrays],
        compiler_params=pltpu.CompilerParams(vmem_limit_bytes=60 * 2**20),
        cost_estimate=SMALL,
        name="flip",
    )(index, *arrays)


def chunks_kernel(index, *refs, count, ways, added, extra):
    step = pl.program_id(0)
    weights, grads, refs = refs[:count], refs[count], refs[count + 1 :]
    plus, refs = refs[:added], refs[added:]
    row, outs = refs[:extra], refs[extra:]
    total, at = None, 0
    for weight in weights:
        units = weight.shape[1]
        term = jnp.dot(weight[...], grads[at : at + units], preferred_element_type=full)
        total = term if total is None else total + term
        at += units
    cols = total.shape[0]
    for way, out in enumerate(outs):

        @pl.when(step == way)
        def _():
            found = total + plus[way][:cols].astype(full) if plus else total
            out[:cols] = found.astype(out.dtype)
            if row:
                found = row[0][...]
                if plus:
                    found = found + plus[way][cols : cols + 1].astype(full)
                out[cols:] = jnp.broadcast_to(
                    found.astype(out.dtype), (out.shape[0] - cols, found.shape[1])
                )


def feature_chunks(weights, grads, partners, plus=(), extra=None, dtype=low, earlier=()):
    me = lax.axis_index("fsdp")
    span = grads.shape[1]
    cols = weights[0].shape[0] // lax.axis_size("fsdp")
    tall = cols + (0 if extra is None else 16)
    index = jnp.stack([jnp.asarray(me ^ j, jnp.int32) for j in partners])
    if earlier:
        index = after(index, *earlier)
    extra = () if extra is None else (extra,)
    const = lambda shape: pl.BlockSpec(shape, lambda i, index: (0, 0))
    return pl.pallas_call(
        lambda *refs: chunks_kernel(
            *refs, count=len(weights), ways=len(partners), added=len(plus), extra=len(extra)
        ),
        grid_spec=pltpu.PrefetchScalarGridSpec(
            num_scalar_prefetch=1,
            grid=(len(partners),),
            in_specs=[
                pl.BlockSpec((cols, w.shape[1]), lambda i, index: (index[i], 0)) for w in weights
            ]
            + [const(a.shape) for a in (grads, *plus, *extra)],
            out_specs=[const((tall, span))] * len(partners),
        ),
        out_shape=[jax.ShapeDtypeStruct((tall, span), dtype)] * len(partners),
        compiler_params=pltpu.CompilerParams(vmem_limit_bytes=60 * 2**20),
        cost_estimate=SMALL,
        name="feature_chunks",
    )(index, *weights, grads, *plus, *extra)


def attn_grad_kernel(
    own, across, cotangent, hidden, gain, factor, attn_ref, hidden_ref, term_ref, *, width
):
    cols = hidden.shape[0]
    mean = (own[cols : cols + 1] + across[cols : cols + 1].astype(full)) * (1.0 / width)
    scaled = own[:cols] + across[:cols].astype(full)
    state = hidden[...]
    term = jnp.sum(scaled * state, axis=1, keepdims=True)
    step = pl.program_id(0)

    @pl.when(step == 0)
    def _():
        term_ref[...] = term

    @pl.when(step != 0)
    def _():
        term_ref[...] += term

    grad = cotangent[...] + gain[...] * scaled - state * (factor[...] * mean)
    hidden_ref[...] = grad.astype(low)
    attn_ref[...] = (branch_scale * grad).astype(low)


def attn_grad(own, across, cotangent, hidden, gain, factor, width):
    cols, span = hidden.shape
    field = jax.ShapeDtypeStruct((cols, span), low)
    tiles = 4
    tile = lambda rows: pl.BlockSpec((rows, span // tiles), lambda i: (0, i))
    once = pl.BlockSpec((cols, 1), lambda i: (0, 0))
    return pl.pallas_call(
        lambda *refs: attn_grad_kernel(*refs, width=width),
        grid=(tiles,),
        in_specs=[tile(cols + 16), tile(cols + 16), tile(cols), tile(cols), once, tile(1)],
        out_specs=[tile(cols), tile(cols), once],
        out_shape=[field, field, jax.ShapeDtypeStruct((cols, 1), full)],
        compiler_params=pltpu.CompilerParams(vmem_limit_bytes=60 * 2**20),
        cost_estimate=SMALL,
        name="attn_grad",
    )(own, across, cotangent, hidden, gain, factor)


def blocks_kernel(index, *refs, count, added):
    step = pl.program_id(0)
    weights, refs = refs[:count], refs[count:]
    grads, refs = refs[:count], refs[count:]
    plus, outs = refs[:added], refs[added:]
    total = None
    for weight, grad in zip(weights, grads):
        term = jnp.dot(grad[...].T, weight[...], preferred_element_type=full)
        total = term if total is None else total + term
    for way, out in enumerate(outs):

        @pl.when(step == way)
        def _():
            found = total + plus[way][...].astype(full) if plus else total
            out[...] = found.astype(out.dtype)


def token_chunks(weights, grads, partners, rows, plus=(), dtype=low, earlier=()):
    me = lax.axis_index("fsdp")
    width = weights[0].shape[1]
    index = jnp.stack([jnp.asarray(me ^ j, jnp.int32) for j in partners])
    if earlier:
        index = after(index, *earlier)
    const = lambda shape: pl.BlockSpec(shape, lambda i, index: (0, 0))
    return pl.pallas_call(
        lambda *refs: blocks_kernel(*refs, count=len(weights), added=len(plus)),
        grid_spec=pltpu.PrefetchScalarGridSpec(
            num_scalar_prefetch=1,
            grid=(len(partners),),
            in_specs=[const(w.shape) for w in weights]
            + [pl.BlockSpec((g.shape[0], rows), lambda i, index: (0, index[i])) for g in grads]
            + [const(a.shape) for a in plus],
            out_specs=[const((rows, width))] * len(partners),
        ),
        out_shape=[jax.ShapeDtypeStruct((rows, width), dtype)] * len(partners),
        compiler_params=pltpu.CompilerParams(vmem_limit_bytes=60 * 2**20),
        cost_estimate=SMALL,
        name="token_chunks",
    )(index, *weights, *grads, *plus)


def body(
    tokens, cotangent, gain_attn, gain_ffn, w_query, w_key, w_value, w_out, w_gate, w_up, w_down
):
    rows, width = tokens.shape
    size = lax.axis_size("fsdp")
    reps = lax.axis_size("rep")
    span = rows * size
    me = lax.axis_index("fsdp")
    replica = lax.axis_index("rep")
    width_cols = width // size
    hidden_cols = w_gate.shape[1]
    heads = width_cols // HD

    half = HD // 2
    frequency = 10000.0 ** (-(jnp.arange(half, dtype=full) * 2.0 / HD))
    angles = frequency[:, None] * jnp.arange(span, dtype=jnp.int32).astype(full)[None, :]
    cosine, sine = jnp.cos(angles), jnp.sin(angles)

    def own_gain(gain):
        return lax.dynamic_slice_in_dim(gain, me * width_cols, width_cols, 0)[:, None]

    down_turned = w_down.T
    share = width_cols // reps

    def down_part(j):
        return lax.dynamic_slice(
            down_turned, (replica * share, (me ^ j) * hidden_cols), (share, hidden_cols)
        )

    parts = [down_part(2), down_part(3)]

    def project(normed):
        found = []
        for weight in (w_query, w_key, w_value):
            field = jnp.einsum("de,td->et", weight, normed, preferred_element_type=full)
            found.append(field.reshape(heads, HD, normed.shape[0]))
        return found

    tokens_chip = swap(tokens, 2)
    normed_here, tokens_part, normed_part = spread(
        [tokens, swap(tokens, 1)], (0, 1), gain_attn, True
    )
    here = project(normed_here)
    tokens_chip = after(tokens_chip, *here)
    parts = [swap(after(part, tokens_chip), 2) for part in parts]
    normed_there, tokens_own, normed_turned = spread(
        [tokens_chip, swap(tokens_chip, 1)],
        (2, 3),
        gain_attn,
        True,
        (tokens_part, normed_part),
    )
    there = project(normed_there)
    parts = [after(part, *there) for part in parts]
    cotangent_chip = swap(after(cotangent, *parts), 2)
    parts_all = lax.all_gather(
        jnp.stack([parts[0], swap(parts[1], 1)]), "rep", axis=1, tiled=True
    )
    attended, query_low, key_low, value_low, lse = attention_forward(here, there, cosine, sine)

    cotangent_blocks = [
        cotangent, swap(cotangent, 1), cotangent_chip, swap(after(cotangent_chip, attended), 1)
    ]
    d_ffn, cotangent_own = spread(cotangent_blocks, (0, 1, 2, 3), gain_attn, False)
    d_ffn_own = (branch_scale * cotangent_own).astype(low)
    me_later = after(me, d_ffn)

    def down_block(j):
        return lax.dynamic_slice_in_dim(
            down_turned, (me_later ^ j) * hidden_cols, hidden_cols, 1
        )

    down_near = [down_block(0), swap(down_block(1), 1)]
    gate_tall, up_tall = flip([w_gate.T, w_up.T], 6, [down_near[0]])
    (out_tall,) = flip([w_out.T], 6, [gate_tall])
    attended_blocks = gather(attended.reshape(width_cols, span), out_tall)

    gain_own = own_gain(gain_ffn)
    hidden, scaled, attended_all = hidden_state(attended_blocks, w_out.T, tokens_own, gain_own)
    down_own = place([after(down_near[0], scaled), down_near[1], parts_all[0], parts_all[1]])
    d_inner = jnp.einsum("ef,te->ft", down_own, d_ffn, preferred_element_type=full).astype(low)
    scaled_blocks = gather(scaled, d_inner)

    inner, ffn_grads, mean, factor, scaled_all = inner_part(
        scaled_blocks, w_gate.T, w_up.T, d_inner
    )

    third = 2 * hidden_cols // 3
    sum_most = GradSum(scaled_all, [ffn_grads], columns=2 * third)
    sum_rest = GradSum(scaled_all, [ffn_grads], columns=third)
    token = sum_rest.line_first()
    token = sum_most.send([token])
    sum_most.transfer(token)
    inner_chip = swap(inner, 2)
    inner_core = swap(inner, 1)
    ffn_weights = (gate_tall, up_tall)

    def first_stage():
        far, near = feature_chunks(ffn_weights, ffn_grads, (3, 1), extra=mean)
        far, near = swap(far, 1), swap(near, 1)
        (chunk,) = feature_chunks(ffn_weights, ffn_grads, (2,), plus=[far], extra=mean)
        return chunk, near

    chunk, near = stage(first_stage, token)
    across = swap(chunk, 2)
    (own,) = feature_chunks(ffn_weights, ffn_grads, (0,), plus=[near], extra=mean, dtype=full)
    inner_late = after(inner_chip, own)
    inner_all = place([inner, inner_core, inner_late, swap(inner_late, 1)])
    sum_down = GradSum(inner_all, [d_ffn_own], turned=True)
    token = sum_down.send()
    sum_down.transfer(token)
    d_attn, d_hidden, gain_ffn_term = attn_grad(
        own, after(across, token), cotangent_own, hidden, gain_own, factor, width
    )

    far, near = feature_chunks([out_tall], d_attn, (3, 1))
    far, near = swap(far, 1), swap(near, 1)
    (chunk,) = feature_chunks([out_tall], d_attn, (2,), plus=[far])
    across = swap(chunk, 2)
    token = sum_most.keep([chunk], sum_rest)
    (own,) = feature_chunks([out_tall], d_attn, (0,), plus=[near], dtype=full, earlier=[token])
    sum_out = GradSum(attended_all, [d_attn])
    token = sum_out.send([own])
    sum_out.transfer(token)
    across = after(across, token)

    def second_stage():
        d_query, d_key, d_value = (
            field.reshape(width_cols, span)
            for field in attention_backward(
                query_low,
                key_low,
                value_low,
                own.reshape(heads, HD, span),
                across.reshape(heads, HD, span),
                lse,
                cosine,
                sine,
            )
        )
        sent = GradSum(normed_turned, [d_query, d_key, d_value]).send()
        return d_query, d_key, d_value, sent

    d_query, d_key, d_value, sent = second_stage()
    sum_attn = GradSum(normed_turned, [d_query, d_key, d_value])
    sum_attn.transfer(sent)
    token = sum_down.keep([sent], sum_most)

    def third_stage():
        attn_weights, attn_grads = (w_query.T, w_key.T, w_value.T), (d_query, d_key, d_value)
        far, near = token_chunks(attn_weights, attn_grads, (3, 1), rows)
        far, near = swap(far, 1), swap(near, 1)
        (chunk,) = token_chunks(attn_weights, attn_grads, (2,), rows, plus=[far])
        across = swap(chunk, 2)
        (own,) = token_chunks(
            attn_weights, attn_grads, (0,), rows, plus=[near], dtype=full, earlier=[chunk]
        )
        return own, across

    own, across = stage(third_stage, token)
    token = sum_out.keep([own], sum_down)
    ffn_result = jnp.einsum(
        "fe,ft->et", w_down, after(inner_all, token), preferred_element_type=full
    )
    output_turned = (hidden + branch_scale * ffn_result).astype(low)
    output = to_rows(output_turned, rows)
    hidden_rows = to_rows(after(d_hidden, output_turned), rows)
    d_normed = own + after(across, token).astype(full)
    x_own = tokens.astype(full)
    factor_own = lax.rsqrt(jnp.mean(x_own * x_own, axis=-1, keepdims=True) + epsilon)
    unit_own = x_own * factor_own
    part = d_normed * gain_attn
    gain_attn_term = jnp.sum(d_normed * unit_own, axis=0)
    gain_ffn_wide = lax.dynamic_update_slice_in_dim(
        jnp.zeros((width,), full), gain_ffn_term[:, 0], me * width_cols, 0
    )
    d_tokens = hidden_rows.astype(full) + factor_own * (
        part - unit_own * jnp.mean(part * unit_own, axis=-1, keepdims=True)
    )
    grad_rest = sum_rest.sides_last([token])
    token = sum_attn.keep([d_tokens, output], sum_out)
    grad_gain_attn, grad_gain_ffn = sum_everywhere(jnp.stack([gain_attn_term, gain_ffn_wide]))
    grad_rest = sum_rest.sides_last([token])
    grad_query, grad_key, grad_value = sum_attn.result()
    (grad_out,) = sum_out.result()
    (grad_most,) = sum_most.result()
    grad_gate = grad_most[:, :hidden_cols]
    grad_up = jnp.concatenate([grad_most[:, hidden_cols:], grad_rest], axis=1)
    (grad_down,) = sum_down.result()
    return (
        output,
        d_tokens,
        grad_gain_attn,
        grad_gain_ffn,
        grad_query,
        grad_key,
        grad_value,
        grad_out,
        grad_gate,
        grad_up,
        grad_down.T,
    )


def solution(mesh):
    rows = P(("rep", "fsdp"), None)
    columns = P(None, "fsdp")
    both = P("rep", "fsdp")
    return jax.shard_map(
        body,
        mesh=mesh,
        in_specs=(rows, rows, P(), P()) + (columns,) * 7,
        out_specs=(rows, rows, P(), P()) + (both,) * 7,
        check_vma=False,
    )
```

```python
import math

import jax
import jax.numpy as jnp
from jax import lax
from jax.experimental import pallas as pl
from jax.experimental.pallas import tpu as pltpu
from jax.sharding import PartitionSpec as P

HD = 64
BLK = 256
NT = (((1,), (1,)), ((), ()))

epsilon = 1e-05
branch_scale = 1.4 / math.sqrt(40.0)
low = jnp.bfloat16
full = jnp.float32

SMALL = pl.CostEstimate(flops=0, bytes_accessed=0, transcendentals=0)


def turn(field, cosine, sine):
    half = field.shape[0] // 2
    first, second = field[:half], field[half:]
    return jnp.concatenate(
        [first * cosine - second * sine, second * cosine + first * sine], axis=0
    )


def forward_kernel(
    q_here, k_here, v_here, q_there, k_there, v_there, cos_ref, sin_ref,
    out_ref, ql_ref, kl_ref, vl_ref, lse_ref,
):
    cosine, sine = cos_ref[...], sin_ref[...]
    span = cosine.shape[1]
    chip = lax.axis_index("fsdp") // 2

    def join(here, there):
        return jnp.concatenate(
            [jnp.where(chip == 0, here[0], there[0]), jnp.where(chip == 0, there[0], here[0])],
            axis=1,
        )

    q_low = turn(join(q_here, q_there), cosine, sine).astype(low)
    k_low = turn(join(k_here, k_there), cosine, sine).astype(low)
    v_low = join(v_here, v_there).astype(low)
    ql_ref[0] = q_low
    kl_ref[0] = k_low
    vl_ref[0] = v_low
    q_scaled = (q_low * (HD ** (-0.5))).astype(low)
    k_rows = k_low.T
    for j in range(span // BLK):
        kv = (j + 1) * BLK
        cols = slice(j * BLK, kv)
        scores = jnp.dot(k_rows[:kv], q_scaled[:, cols], preferred_element_type=full)
        top = jnp.max(scores, axis=0, keepdims=True)
        expo = jnp.exp(scores - top)
        total = jnp.sum(expo, axis=0, keepdims=True)
        mixed = jnp.dot(v_low[:, :kv], expo.astype(low), preferred_element_type=full)
        out_ref[0, :, cols] = (mixed * (1.0 / total)).astype(low)
        lse_ref[0, :, cols] = top + jnp.log(total)


def attention_forward(here, there, cosine, sine):
    heads, _, part = here[0].shape
    span = cosine.shape[1]
    half = pl.BlockSpec((1, HD, part), lambda h: (h, 0, 0))
    spec = pl.BlockSpec((1, HD, span), lambda h: (h, 0, 0))
    table = pl.BlockSpec((HD // 2, span), lambda h: (0, 0))
    field = jax.ShapeDtypeStruct((heads, HD, span), low)
    row = pl.BlockSpec((1, 1, span), lambda h: (h, 0, 0))
    return pl.pallas_call(
        forward_kernel,
        grid=(heads,),
        in_specs=[half] * 6 + [table, table],
        out_specs=[spec, spec, spec, spec, row],
        out_shape=[field, field, field, field, jax.ShapeDtypeStruct((heads, 1, span), full)],
        compiler_params=pltpu.CompilerParams(vmem_limit_bytes=60 * 2**20),
        cost_estimate=SMALL,
        name="attention_forward",
    )(*here, *there, cosine, sine)


def backward_kernel(
    q_ref, k_ref, v_ref, g_ref, h_ref, lse_ref, cos_ref, sin_ref, dq_ref, dk_ref, dv_ref, dk_acc, dv_acc
):
    cosine, sine = cos_ref[...], sin_ref[...]
    span = q_ref.shape[2]
    q_scaled = (q_ref[0] * (HD ** (-0.5))).astype(low)
    k_low, v_low = k_ref[0], v_ref[0]
    grad = (g_ref[0] + h_ref[0].astype(full)).astype(low)
    k_rows, v_rows = k_low.T, v_low.T
    dk_acc[...] = jnp.zeros_like(dk_acc)
    dv_acc[...] = jnp.zeros_like(dv_acc)
    for j in range(span // BLK):
        kv = (j + 1) * BLK
        cols = slice(j * BLK, kv)
        q_j, g_j = q_scaled[:, cols], grad[:, cols]
        scores = jnp.dot(k_rows[:kv], q_j, preferred_element_type=full)
        probs = jnp.exp(scores - lse_ref[0, :, cols])
        probs_low = probs.astype(low)
        d_probs = jnp.dot(v_rows[:kv], g_j, preferred_element_type=full)
        delta = jnp.sum(probs * d_probs, axis=0, keepdims=True)
        d_scores = (probs * (d_probs - delta)).astype(low)
        dq = jnp.dot(k_low[:, :kv], d_scores, preferred_element_type=full) * (HD ** (-0.5))
        dq_ref[0, :, cols] = turn(dq, cosine[:, cols], -sine[:, cols]).astype(low)
        dk_acc[:, :kv] += lax.dot_general(q_j, d_scores, NT, preferred_element_type=full)
        dv_acc[:, :kv] += lax.dot_general(g_j, probs_low, NT, preferred_element_type=full)
    dk_ref[0] = turn(dk_acc[...], cosine, -sine).astype(low)
    dv_ref[0] = dv_acc[...].astype(low)


def attention_backward(query, key, value, grad, rest, lse, cosine, sine):
    heads, _, span = query.shape
    spec = pl.BlockSpec((1, HD, span), lambda h: (h, 0, 0))
    table = pl.BlockSpec((HD // 2, span), lambda h: (0, 0))
    row = pl.BlockSpec((1, 1, span), lambda h: (h, 0, 0))
    field = jax.ShapeDtypeStruct((heads, HD, span), low)
    return pl.pallas_call(
        backward_kernel,
        grid=(heads,),
        in_specs=[spec, spec, spec, spec, spec, row, table, table],
        out_specs=[spec, spec, spec],
        out_shape=[field, field, field],
        scratch_shapes=[pltpu.VMEM((HD, span), full), pltpu.VMEM((HD, span), full)],
        compiler_params=pltpu.CompilerParams(vmem_limit_bytes=60 * 2**20),
        cost_estimate=SMALL,
        name="attention_backward",
    )(query, key, value, grad, rest, lse, cosine, sine)


def swap(array, j):
    size = lax.axis_size("fsdp")
    return lax.ppermute(array, "fsdp", [(i, i ^ j) for i in range(size)])


def after(value, *earlier):
    return lax.optimization_barrier((value, *earlier))[0]


def stage(run, *earlier):
    blank = lambda: jax.tree.map(lambda a: jnp.zeros(a.shape, a.dtype), jax.eval_shape(run))
    return lax.cond(after(jnp.bool_(True), *earlier), run, blank)


def place_kernel(*refs, parts):
    *blocks, out, held, arrived, left = refs
    me = lax.axis_index("fsdp")
    into, back = [], []
    for j in range(held.shape[0]):
        at = 0
        for i in range(j * parts, (j + 1) * parts):
            rows = blocks[i].shape[0]
            into.append(
                pltpu.make_async_copy(blocks[i], held.at[j, pl.ds(at, rows)], arrived.at[i])
            )
            at += rows
        back.append(
            pltpu.make_async_copy(
                held.at[j], out.at[lax.bitwise_xor(me, jnp.int32(j))], left.at[j]
            )
        )
    for copy in into:
        copy.start()
    for j, copy in enumerate(back):
        for part in into[j * parts : (j + 1) * parts]:
            part.wait()
        copy.start()
    for copy in back:
        copy.wait()


def place(blocks, parts=1, limit=60):
    count = len(blocks)
    size = count // parts
    rows = sum(block.shape[0] for block in blocks[:parts])
    shape = (size, rows, blocks[0].shape[1])
    dtype = blocks[0].dtype
    whole = pl.pallas_call(
        lambda *refs: place_kernel(*refs, parts=parts),
        in_specs=[pl.BlockSpec(memory_space=pl.ANY)] * count,
        out_specs=pl.BlockSpec(memory_space=pl.ANY),
        out_shape=jax.ShapeDtypeStruct(shape, dtype),
        scratch_shapes=[
            pltpu.VMEM(shape, dtype),
            pltpu.SemaphoreType.DMA((count,)),
            pltpu.SemaphoreType.DMA((size,)),
        ],
        compiler_params=pltpu.CompilerParams(vmem_limit_bytes=limit * 2**20),
        cost_estimate=SMALL,
        name="place",
    )(*blocks)
    return whole.reshape(size * rows, shape[2])


def gather(array, *before_last):
    core = swap(array, 1)
    chip = swap(array, 2)
    return [array, core, chip, swap(after(chip, *before_last) if before_last else chip, 1)]


def bring(blocks, held, arrived, rest=None):
    me = lax.axis_index("fsdp")
    cols = held.shape[1]
    count = len(blocks)
    copies = []
    for j, block in enumerate(blocks):
        to = held.at[lax.bitwise_xor(me, jnp.int32(j))]
        if rest is None:
            copies.append(pltpu.make_async_copy(block, to, arrived.at[j]))
        else:
            copies.append(pltpu.make_async_copy(block.at[pl.ds(0, cols)], to, arrived.at[j]))
            copies.append(
                pltpu.make_async_copy(
                    block.at[pl.ds(cols, 16)], rest.at[j], arrived.at[count + j]
                )
            )
    for copy in copies:
        copy.start()
    for copy in copies:
        copy.wait()


def spread_kernel(index, *refs, count, kept, normalize):
    step = pl.program_id(0)
    blocks, gain = refs[:count], refs[count]
    outs = refs[count + 1 + kept :]
    me = index[count]
    for j, block in enumerate(blocks):

        @pl.when(step == j)
        def _():
            x = block[...].astype(full)
            cols = outs[1].shape[0]
            if normalize:
                factor = lax.rsqrt(jnp.mean(x * x, axis=-1, keepdims=True) + epsilon)
                wide = (x * factor * gain[...]).astype(low)
                outs[2][...] = wide.T
            else:
                wide = (branch_scale * x).astype(low)
            outs[0][...] = wide
            for g in range(x.shape[1] // cols):

                @pl.when(me == g)
                def _():
                    outs[1][...] = x[:, g * cols : (g + 1) * cols].T


def spread(blocks, partners, gain, normalize, earlier=None):
    rows, width = blocks[0].shape
    size = lax.axis_size("fsdp")
    count = len(blocks)
    me = lax.axis_index("fsdp")
    tokens = [me ^ j for j in partners]
    local = [block % count for block in tokens]
    index = jnp.stack([jnp.asarray(v, jnp.int32) for v in (*local, me, *tokens)])
    const = lambda shape: pl.BlockSpec(shape, lambda i, index: (0,) * len(shape))
    kept = len(earlier) if earlier else 0
    outs = [
        (
            pl.BlockSpec((rows, width), lambda i, index: (index[i], 0)),
            jax.ShapeDtypeStruct((count * rows, width), low),
        ),
        (
            pl.BlockSpec((width // size, rows), lambda i, index: (0, index[count + 1 + i])),
            jax.ShapeDtypeStruct((width // size, size * rows), full),
        ),
    ]
    if normalize:
        outs.append(
            (
                pl.BlockSpec((width, rows), lambda i, index: (0, index[count + 1 + i])),
                jax.ShapeDtypeStruct((width, size * rows), low),
            )
        )
    return pl.pallas_call(
        lambda *refs: spread_kernel(*refs, count=count, kept=kept, normalize=normalize),
        grid_spec=pltpu.PrefetchScalarGridSpec(
            num_scalar_prefetch=1,
            grid=(count,),
            in_specs=[const((rows, width))] * count
            + [const((1, width))]
            + [pl.BlockSpec(memory_space=pl.ANY)] * kept,
            out_specs=[spec for spec, _ in outs],
        ),
        out_shape=[shape for _, shape in outs],
        input_output_aliases={count + 2 + i: 1 + i for i in range(kept)},
        compiler_params=pltpu.CompilerParams(vmem_limit_bytes=32 * 2**20),
        cost_estimate=SMALL,
        name="spread",
    )(index, *blocks, gain[None, :], *(earlier or ()))


def hidden_kernel(
    own, core, chip, both, weight, tokens, gain, hidden_ref, first_ref, second_ref, all_ref,
    squares_ref, held, arrived, left,
):
    step = pl.program_id(0)
    out = pltpu.make_async_copy(held, all_ref, left.at[0])

    @pl.when(step == 0)
    def _():
        bring((own, core, chip, both), held, arrived)
        out.start()

    span = held.shape[2]
    result = jnp.dot(
        weight[...], held[...].reshape(-1, span), preferred_element_type=full
    )
    hidden = tokens[...] + branch_scale * result
    tile = hidden.shape[0]
    at = pl.multiple_of(step * tile, tile)
    hidden_ref[pl.ds(at, tile), :] = hidden
    part = span // 2
    halves = [(first_ref, slice(0, part)), (second_ref, slice(part, span))]
    for ref, cut in halves:
        ref[pl.ds(at, tile), :] = (hidden[:, cut] * gain[...]).astype(low)
    squares = jnp.sum(hidden * hidden, axis=0, keepdims=True)

    @pl.when(step == 0)
    def _():
        squares_ref[...] = squares

    @pl.when(step != 0)
    def _():
        squares_ref[...] += squares

    @pl.when(step == pl.num_programs(0) - 1)
    def _():
        total = squares_ref[...]
        high = total.astype(low)
        rest = (total - high.astype(full)).astype(low)
        cols = hidden_ref.shape[0]
        for ref, cut in halves:
            ref[cols : cols + 8] = jnp.broadcast_to(high[:, cut], (8, part))
            ref[cols + 8 :] = jnp.broadcast_to(rest[:, cut], (8, part))
        out.wait()


def hidden_state(blocks, weight, tokens, gain):
    cols, span = blocks[0].shape
    size = len(blocks)
    tiles = 2
    tile = cols // tiles
    hbm = pl.BlockSpec(memory_space=pl.ANY)
    rows = lambda wide: pl.BlockSpec((tile, wide), lambda i: (i, 0))
    const = lambda shape: pl.BlockSpec(shape, lambda i: (0, 0))
    half = const((cols + 16, span // 2))
    hidden, first, second, whole = pl.pallas_call(
        hidden_kernel,
        grid=(tiles,),
        in_specs=[hbm] * 4 + [rows(size * cols), rows(span), rows(1)],
        out_specs=[const((cols, span)), half, half, hbm],
        out_shape=[
            jax.ShapeDtypeStruct((cols, span), full),
            jax.ShapeDtypeStruct((cols + 16, span // 2), low),
            jax.ShapeDtypeStruct((cols + 16, span // 2), low),
            jax.ShapeDtypeStruct((size, cols, span), low),
        ],
        scratch_shapes=[
            pltpu.VMEM((1, span), full),
            pltpu.VMEM((size, cols, span), low),
            pltpu.SemaphoreType.DMA((size,)),
            pltpu.SemaphoreType.DMA((1,)),
        ],
        compiler_params=pltpu.CompilerParams(vmem_limit_bytes=60 * 2**20),
        cost_estimate=SMALL,
        name="hidden_state",
    )(*blocks, weight, tokens, gain)
    return hidden, first, second, whole.reshape(size * cols, span)


def inner_kernel(*refs, half):
    blocks, (w_gate, w_up, d_inner), refs = refs[:4], refs[4:7], refs[7:]
    inner_ref, grads_ref, mean_ref, factor_ref, all_ref, held, rest, arrived, left = refs[5 * half :]
    step = pl.program_id(0)
    span = held.shape[2]
    out = pltpu.make_async_copy(
        held, all_ref.at[:, :, pl.ds(half * span, span)], left.at[0]
    )

    @pl.when(step == 0)
    def _():
        bring(blocks, held, arrived, rest)
        out.start()
        squares = [
            rest[j, 0:1].astype(full) + rest[j, 8:9].astype(full) for j in range(held.shape[0])
        ]
        total = (squares[0] + squares[1]) + (squares[2] + squares[3])
        factor_ref[...] = lax.rsqrt(total / (held.shape[0] * held.shape[1]) + epsilon)

        mean_ref[...] = jnp.zeros_like(mean_ref)

    wide = BLK
    for part in range(span // wide):
        cut = slice(part * wide, (part + 1) * wide)
        scaled = held[:, :, cut].reshape(-1, wide)
        factor = factor_ref[:, cut]
        gate = factor * jnp.dot(w_gate[...], scaled, preferred_element_type=full)
        up = factor * jnp.dot(w_up[...], scaled, preferred_element_type=full)
        sigmoid = 0.5 * jnp.tanh(0.5 * gate) + 0.5
        activated = gate * sigmoid
        inner_ref[:, cut] = (activated * up).astype(low)
        grad = factor * d_inner[:, cut].astype(full)
        d_up = grad * activated
        d_gate = grad * up * (sigmoid + activated * (1.0 - sigmoid))
        grads_ref[0, :, cut] = d_gate.astype(low)
        grads_ref[1, :, cut] = d_up.astype(low)
        mean_ref[:, cut] += jnp.sum(d_gate * gate + d_up * up, axis=0, keepdims=True)

    @pl.when(step == pl.num_programs(0) - 1)
    def _():
        out.wait()


def inner_part(half, blocks, w_gate, w_up, d_inner, before=()):
    tall, span = blocks[0].shape
    cols = tall - 16
    size = len(blocks)
    units = w_gate.shape[0]
    tile = units // 3
    hbm = pl.BlockSpec(memory_space=pl.ANY)
    weight = pl.BlockSpec((tile, size * cols), lambda i: (i, 0))
    part = pl.BlockSpec((tile, span), lambda i: (i, half))
    row = pl.BlockSpec((1, span), lambda i: (0, half))
    return pl.pallas_call(
        lambda *refs: inner_kernel(*refs, half=half),
        grid=(units // tile,),
        in_specs=[hbm] * 4 + [weight, weight, part] + [hbm] * len(before),
        out_specs=[part, pl.BlockSpec((2, tile, span), lambda i: (0, i, half)), row, row, hbm],
        out_shape=[
            jax.ShapeDtypeStruct((units, 2 * span), low),
            jax.ShapeDtypeStruct((2, units, 2 * span), low),
            jax.ShapeDtypeStruct((1, 2 * span), full),
            jax.ShapeDtypeStruct((1, 2 * span), full),
            jax.ShapeDtypeStruct((size, cols, 2 * span), low),
        ],
        input_output_aliases={7 + i: i for i in range(len(before))},
        scratch_shapes=[
            pltpu.VMEM((size, cols, span), low),
            pltpu.VMEM((size, 16, span), low),
            pltpu.SemaphoreType.DMA((2 * size,)),
            pltpu.SemaphoreType.DMA((1,)),
        ],
        compiler_params=pltpu.CompilerParams(vmem_limit_bytes=60 * 2**20),
        cost_estimate=SMALL,
        name="inner_part",
    )(*blocks, w_gate, w_up, d_inner, *before)


def to_rows(field, rows):
    me = lax.axis_index("fsdp")
    size = lax.axis_size("fsdp")
    blocks = []
    for j in range(size):
        block = lax.dynamic_slice_in_dim(field, (me ^ j) * rows, rows, 1)
        blocks.append(block if j == 0 else swap(block, j))
    return place(blocks).T


def product_kernel(index, act, *refs, count, adds, turned):
    grads = refs[:count]
    added = refs[count] if adds else None
    out = refs[-1]
    rows = act[:, 0].reshape(-1, act.shape[-1])
    for k in range(count):
        pair = (grads[k][...], rows) if turned else (rows, grads[k][...])
        total = lax.dot_general(*pair, NT, preferred_element_type=full)
        if turned:
            if adds:
                total = total + added[0, k].astype(full)
            out[0, k] = total.astype(low)
            continue
        total = total.reshape((act.shape[0], act.shape[2]) + total.shape[1:])
        if adds:
            total = total + added[:, k].astype(full)
        out[:, k] = total.astype(low)


def half_product(act, grads, side, added=None, turned=False, columns=None, earlier=()):
    size = lax.axis_size("rep")
    count = len(grads)
    tokens = grads[0].shape[1]
    columns = columns or grads[0].shape[0]
    lines, rows = size // 2, act.shape[0] // size
    index = jnp.asarray(side, jnp.int32)[None]
    if earlier:
        index = after(index, *earlier)
    steps = lines
    some = lines // steps
    shape = (columns, rows) if turned else (rows, columns)
    piece = pl.BlockSpec((some, count) + shape, lambda i, index: (i, 0, 0, 0))
    return pl.pallas_call(
        lambda *refs: product_kernel(*refs, count=count, adds=added is not None, turned=turned),
        grid_spec=pltpu.PrefetchScalarGridSpec(
            num_scalar_prefetch=1,
            grid=(steps,),
            in_specs=[pl.BlockSpec((some, 1, rows, tokens), lambda i, index: (i, index[0], 0, 0))]
            + [pl.BlockSpec((columns, tokens), lambda i, index: (0, 0))] * count
            + ([] if added is None else [piece]),
            out_specs=piece,
        ),
        out_shape=jax.ShapeDtypeStruct((lines, count) + shape, low),
        compiler_params=pltpu.CompilerParams(vmem_limit_bytes=60 * 2**20),
        cost_estimate=SMALL,
        name="half_product",
    )(index, act.reshape(lines, 2, rows, tokens), *grads, *(() if added is None else (added,)))


def whole_kernel(act, grad, out):
    out[0] = lax.dot_general(act[0], grad[...], NT, preferred_element_type=full).astype(low)


def whole_product(act, grad, columns):
    lines = lax.axis_size("rep") // 2
    tokens = grad.shape[1]
    last = grad.shape[0] // columns - 1
    rows = act.shape[0] // lines
    return pl.pallas_call(
        whole_kernel,
        grid=(lines,),
        in_specs=[
            pl.BlockSpec((1, rows, tokens), lambda i: (i, 0, 0)),
            pl.BlockSpec((columns, tokens), lambda i: (last, 0)),
        ],
        out_specs=pl.BlockSpec((1, rows, columns), lambda i: (i, 0, 0)),
        out_shape=jax.ShapeDtypeStruct((lines, rows, columns), low),
        compiler_params=pltpu.CompilerParams(vmem_limit_bytes=60 * 2**20),
        cost_estimate=SMALL,
        name="whole_product",
    )(act.reshape(lines, rows, tokens), grad)


def neighbour(array):
    return lax.ppermute(array, "rep", [(i, i ^ 1) for i in range(lax.axis_size("rep"))])


def line_scatter(array):
    size = lax.axis_size("rep")
    groups = [list(range(side, size, 2)) for side in range(2)]
    return lax.psum_scatter(
        array, "rep", scatter_dimension=0, tiled=True, axis_index_groups=groups
    )


class GradSum:
    def __init__(self, act, grads, turned=False, columns=None):
        self.act, self.grads, self.turned, self.columns = act, grads, turned, columns
        self.side = lax.axis_index("rep") % 2

    def send(self, earlier=()):
        sent = half_product(
            self.act,
            self.grads,
            1 - self.side,
            turned=self.turned,
            columns=self.columns,
            earlier=earlier,
        )
        return sent

    def transfer(self, sent):
        self.arrived = neighbour(sent)

    def keep(self, earlier=(), last=None):
        kept = half_product(
            self.act,
            self.grads,
            self.side,
            self.arrived,
            turned=self.turned,
            columns=self.columns,
            earlier=earlier,
        )
        self.sums = line_scatter(kept if last is None else after(kept, last.sums))
        return kept

    def line_first(self, earlier=()):
        whole = whole_product(self.act, after(self.grads[0], *earlier), self.columns)
        self.sums = line_scatter(whole)
        return whole

    def sides_last(self, earlier=()):
        _, rows, columns = self.sums.shape
        parts = self.sums.reshape(2, rows // 2, columns)
        side = after(self.side, *earlier)
        sent = lax.dynamic_index_in_dim(parts, 1 - side, 0, False)
        kept = lax.dynamic_index_in_dim(parts, side, 0, False)
        return kept.astype(full) + neighbour(sent).astype(full)

    def result(self):
        return [self.sums[0, k].astype(full) for k in range(len(self.grads))]


def sum_everywhere(array):
    array = (array + swap(array, 1)) + (swap(array, 2) + swap(array, 3))
    size = lax.axis_size("rep")
    far = 1
    while far < size:
        array = array + lax.ppermute(array, "rep", [(i, i ^ far) for i in range(size)])
        far *= 2
    return array


def flip_kernel(*refs):
    count = len(refs) // 2
    for wide, tall in zip(refs[:count], refs[count:]):
        tall[...] = wide[...].T


def flip(arrays, tiles, earlier=()):
    width = arrays[0].shape[1]
    tile = width // tiles
    index = jnp.zeros((1,), jnp.int32)
    if earlier:
        index = after(index, *earlier)
    return pl.pallas_call(
        lambda index, *refs: flip_kernel(*refs),
        grid_spec=pltpu.PrefetchScalarGridSpec(
            num_scalar_prefetch=1,
            grid=(tiles,),
            in_specs=[pl.BlockSpec((a.shape[0], tile), lambda i, index: (0, i)) for a in arrays],
            out_specs=[pl.BlockSpec((tile, a.shape[0]), lambda i, index: (i, 0)) for a in arrays],
        ),
        out_shape=[jax.ShapeDtypeStruct((width, a.shape[0]), a.dtype) for a in arrays],
        compiler_params=pltpu.CompilerParams(vmem_limit_bytes=60 * 2**20),
        cost_estimate=SMALL,
        name="flip",
    )(index, *arrays)


def chunks_kernel(index, *refs, count, ways, added, extra):
    step = pl.program_id(0)
    weights, grads, refs = refs[:count], refs[count], refs[count + 1 :]
    plus, refs = refs[:added], refs[added:]
    row, outs = refs[:extra], refs[extra:]
    total, at = None, 0
    for weight in weights:
        units = weight.shape[1]
        term = jnp.dot(weight[...], grads[at : at + units], preferred_element_type=full)
        total = term if total is None else total + term
        at += units
    cols = total.shape[0]
    for way, out in enumerate(outs):

        @pl.when(step == way)
        def _():
            found = total + plus[way][:cols].astype(full) if plus else total
            out[:cols] = found.astype(out.dtype)
            if row:
                found = row[0][...]
                if plus:
                    found = found + plus[way][cols : cols + 1].astype(full)
                out[cols:] = jnp.broadcast_to(
                    found.astype(out.dtype), (out.shape[0] - cols, found.shape[1])
                )


def feature_chunks(weights, grads, partners, plus=(), extra=None, dtype=low, earlier=()):
    me = lax.axis_index("fsdp")
    span = grads.shape[1]
    cols = weights[0].shape[0] // lax.axis_size("fsdp")
    tall = cols + (0 if extra is None else 16)
    index = jnp.stack([jnp.asarray(me ^ j, jnp.int32) for j in partners])
    if earlier:
        index = after(index, *earlier)
    extra = () if extra is None else (extra,)
    const = lambda shape: pl.BlockSpec(shape, lambda i, index: (0, 0))
    return pl.pallas_call(
        lambda *refs: chunks_kernel(
            *refs, count=len(weights), ways=len(partners), added=len(plus), extra=len(extra)
        ),
        grid_spec=pltpu.PrefetchScalarGridSpec(
            num_scalar_prefetch=1,
            grid=(len(partners),),
            in_specs=[
                pl.BlockSpec((cols, w.shape[1]), lambda i, index: (index[i], 0)) for w in weights
            ]
            + [const(a.shape) for a in (grads, *plus, *extra)],
            out_specs=[const((tall, span))] * len(partners),
        ),
        out_shape=[jax.ShapeDtypeStruct((tall, span), dtype)] * len(partners),
        compiler_params=pltpu.CompilerParams(vmem_limit_bytes=60 * 2**20),
        cost_estimate=SMALL,
        name="feature_chunks",
    )(index, *weights, grads, *plus, *extra)


def attn_grad_kernel(
    own, across, cotangent, hidden, gain, factor, attn_ref, hidden_ref, term_ref, *, width
):
    cols = hidden.shape[0]
    mean = (own[cols : cols + 1] + across[cols : cols + 1].astype(full)) * (1.0 / width)
    scaled = own[:cols] + across[:cols].astype(full)
    state = hidden[...]
    term = jnp.sum(scaled * state, axis=1, keepdims=True)
    step = pl.program_id(0)

    @pl.when(step == 0)
    def _():
        term_ref[...] = term

    @pl.when(step != 0)
    def _():
        term_ref[...] += term

    grad = cotangent[...] + gain[...] * scaled - state * (factor[...] * mean)
    hidden_ref[...] = grad.astype(low)
    attn_ref[...] = (branch_scale * grad).astype(low)


def attn_grad(own, across, cotangent, hidden, gain, factor, width):
    cols, span = hidden.shape
    field = jax.ShapeDtypeStruct((cols, span), low)
    tiles = 4
    tile = lambda rows: pl.BlockSpec((rows, span // tiles), lambda i: (0, i))
    once = pl.BlockSpec((cols, 1), lambda i: (0, 0))
    return pl.pallas_call(
        lambda *refs: attn_grad_kernel(*refs, width=width),
        grid=(tiles,),
        in_specs=[tile(cols + 16), tile(cols + 16), tile(cols), tile(cols), once, tile(1)],
        out_specs=[tile(cols), tile(cols), once],
        out_shape=[field, field, jax.ShapeDtypeStruct((cols, 1), full)],
        compiler_params=pltpu.CompilerParams(vmem_limit_bytes=60 * 2**20),
        cost_estimate=SMALL,
        name="attn_grad",
    )(own, across, cotangent, hidden, gain, factor)


def blocks_kernel(index, *refs, count, added):
    step = pl.program_id(0)
    weights, refs = refs[:count], refs[count:]
    grads, refs = refs[:count], refs[count:]
    plus, outs = refs[:added], refs[added:]
    total = None
    for weight, grad in zip(weights, grads):
        term = jnp.dot(grad[...].T, weight[...], preferred_element_type=full)
        total = term if total is None else total + term
    for way, out in enumerate(outs):

        @pl.when(step == way)
        def _():
            found = total + plus[way][...].astype(full) if plus else total
            out[...] = found.astype(out.dtype)


def token_chunks(weights, grads, partners, rows, plus=(), dtype=low, earlier=()):
    me = lax.axis_index("fsdp")
    width = weights[0].shape[1]
    index = jnp.stack([jnp.asarray(me ^ j, jnp.int32) for j in partners])
    if earlier:
        index = after(index, *earlier)
    const = lambda shape: pl.BlockSpec(shape, lambda i, index: (0, 0))
    return pl.pallas_call(
        lambda *refs: blocks_kernel(*refs, count=len(weights), added=len(plus)),
        grid_spec=pltpu.PrefetchScalarGridSpec(
            num_scalar_prefetch=1,
            grid=(len(partners),),
            in_specs=[const(w.shape) for w in weights]
            + [pl.BlockSpec((g.shape[0], rows), lambda i, index: (0, index[i])) for g in grads]
            + [const(a.shape) for a in plus],
            out_specs=[const((rows, width))] * len(partners),
        ),
        out_shape=[jax.ShapeDtypeStruct((rows, width), dtype)] * len(partners),
        compiler_params=pltpu.CompilerParams(vmem_limit_bytes=60 * 2**20),
        cost_estimate=SMALL,
        name="token_chunks",
    )(index, *weights, *grads, *plus)


def body(
    tokens, cotangent, gain_attn, gain_ffn, w_query, w_key, w_value, w_out, w_gate, w_up, w_down
):
    rows, width = tokens.shape
    size = lax.axis_size("fsdp")
    reps = lax.axis_size("rep")
    span = rows * size
    me = lax.axis_index("fsdp")
    replica = lax.axis_index("rep")
    width_cols = width // size
    hidden_cols = w_gate.shape[1]
    heads = width_cols // HD

    half = HD // 2
    frequency = 10000.0 ** (-(jnp.arange(half, dtype=full) * 2.0 / HD))
    angles = frequency[:, None] * jnp.arange(span, dtype=jnp.int32).astype(full)[None, :]
    cosine, sine = jnp.cos(angles), jnp.sin(angles)

    def own_gain(gain):
        return lax.dynamic_slice_in_dim(gain, me * width_cols, width_cols, 0)[:, None]

    down_turned = w_down.T
    share = width_cols // reps

    def down_part(j):
        return lax.dynamic_slice(
            down_turned, (replica * share, (me ^ j) * hidden_cols), (share, hidden_cols)
        )

    parts = [down_part(2), down_part(3)]

    def project(normed):
        found = []
        for weight in (w_query, w_key, w_value):
            field = jnp.einsum("de,td->et", weight, normed, preferred_element_type=full)
            found.append(field.reshape(heads, HD, normed.shape[0]))
        return found

    tokens_chip = swap(tokens, 2)
    normed_here, tokens_part, normed_part = spread(
        [tokens, swap(tokens, 1)], (0, 1), gain_attn, True
    )
    here = project(normed_here)
    tokens_chip = after(tokens_chip, *here)
    parts = [swap(after(part, tokens_chip), 2) for part in parts]
    normed_there, tokens_own, normed_turned = spread(
        [tokens_chip, swap(tokens_chip, 1)],
        (2, 3),
        gain_attn,
        True,
        (tokens_part, normed_part),
    )
    there = project(normed_there)
    parts = [after(part, *there) for part in parts]
    cotangent_chip = swap(after(cotangent, *parts), 2)
    parts_all = lax.all_gather(
        jnp.stack([parts[0], swap(parts[1], 1)]), "rep", axis=1, tiled=True
    )
    attended, query_low, key_low, value_low, lse = attention_forward(here, there, cosine, sine)

    cotangent_blocks = [
        cotangent, swap(cotangent, 1), cotangent_chip, swap(after(cotangent_chip, attended), 1)
    ]
    d_ffn, cotangent_own = spread(cotangent_blocks, (0, 1, 2, 3), gain_attn, False)
    d_ffn_own = (branch_scale * cotangent_own).astype(low)
    me_later = after(me, d_ffn)

    def down_block(j):
        return lax.dynamic_slice_in_dim(
            down_turned, (me_later ^ j) * hidden_cols, hidden_cols, 1
        )

    down_near = [down_block(0), swap(down_block(1), 1)]
    gate_tall, up_tall = flip([w_gate.T, w_up.T], 6, [down_near[0]])
    (out_tall,) = flip([w_out.T], 6, [gate_tall])
    attended_blocks = gather(attended.reshape(width_cols, span), out_tall)

    gain_own = own_gain(gain_ffn)
    hidden, scaled_first, scaled_second, attended_all = hidden_state(
        attended_blocks, w_out.T, tokens_own, gain_own
    )
    scaled_chip = swap(scaled_first, 2)

    down_own = place(
        [after(down_near[0], hidden), down_near[1], parts_all[0], parts_all[1]], limit=16
    )
    d_inner = jnp.einsum("ef,te->ft", down_own, d_ffn, preferred_element_type=full).astype(low)
    scaled_chip = after(scaled_chip, d_inner)
    scaled_first = [scaled_first, swap(scaled_first, 1), scaled_chip, swap(scaled_chip, 1)]
    second_chip = swap(after(scaled_second, scaled_chip), 2)

    first = stage(lambda: inner_part(0, scaled_first, w_gate.T, w_up.T, d_inner), d_inner)
    second_chip = after(second_chip, first[2])
    scaled_second = [scaled_second, swap(scaled_second, 1), second_chip, swap(second_chip, 1)]
    inner, ffn_grads, mean, factor, scaled_all = inner_part(
        1, scaled_second, w_gate.T, w_up.T, d_inner, first
    )
    ffn_grads = ffn_grads.reshape(2 * hidden_cols, span)
    scaled_all = scaled_all.reshape(width, span)

    third = 2 * hidden_cols // 3
    sum_most = GradSum(scaled_all, [ffn_grads], columns=2 * third)
    sum_rest = GradSum(scaled_all, [ffn_grads], columns=third)
    token = sum_rest.line_first()
    token = sum_most.send([token])
    sum_most.transfer(token)
    inner_chip = swap(inner, 2)
    inner_core = swap(inner, 1)
    ffn_weights = (gate_tall, up_tall)

    def first_stage():
        far, near = feature_chunks(ffn_weights, ffn_grads, (3, 1), extra=mean)
        far, near = swap(far, 1), swap(near, 1)
        (chunk,) = feature_chunks(ffn_weights, ffn_grads, (2,), plus=[far], extra=mean)
        return chunk, near

    chunk, near = stage(first_stage, token)
    across = swap(chunk, 2)
    (own,) = feature_chunks(ffn_weights, ffn_grads, (0,), plus=[near], extra=mean, dtype=full)
    inner_late = after(inner_chip, own)
    inner_all = place([inner, inner_core, inner_late, swap(inner_late, 1)])
    sum_down = GradSum(inner_all, [d_ffn_own], turned=True)
    token = sum_down.send()
    sum_down.transfer(token)
    d_attn, d_hidden, gain_ffn_term = attn_grad(
        own, after(across, token), cotangent_own, hidden, gain_own, factor, width
    )

    far, near = feature_chunks([out_tall], d_attn, (3, 1))
    far, near = swap(far, 1), swap(near, 1)
    (chunk,) = feature_chunks([out_tall], d_attn, (2,), plus=[far])
    across = swap(chunk, 2)
    token = sum_most.keep([chunk], sum_rest)
    (own,) = feature_chunks([out_tall], d_attn, (0,), plus=[near], dtype=full, earlier=[token])
    sum_out = GradSum(attended_all, [d_attn])
    token = sum_out.send([own])
    sum_out.transfer(token)
    across = after(across, token)

    def second_stage():
        d_query, d_key, d_value = (
            field.reshape(width_cols, span)
            for field in attention_backward(
                query_low,
                key_low,
                value_low,
                own.reshape(heads, HD, span),
                across.reshape(heads, HD, span),
                lse,
                cosine,
                sine,
            )
        )
        sent = GradSum(normed_turned, [d_query, d_key, d_value]).send()
        return d_query, d_key, d_value, sent

    d_query, d_key, d_value, sent = second_stage()
    sum_attn = GradSum(normed_turned, [d_query, d_key, d_value])
    sum_attn.transfer(sent)
    token = sum_down.keep([sent], sum_most)

    def third_stage():
        attn_weights, attn_grads = (w_query.T, w_key.T, w_value.T), (d_query, d_key, d_value)
        far, near = token_chunks(attn_weights, attn_grads, (3, 1), rows)
        far, near = swap(far, 1), swap(near, 1)
        (chunk,) = token_chunks(attn_weights, attn_grads, (2,), rows, plus=[far])
        across = swap(chunk, 2)
        (own,) = token_chunks(
            attn_weights, attn_grads, (0,), rows, plus=[near], dtype=full, earlier=[chunk]
        )
        return own, across

    own, across = stage(third_stage, token)
    token = sum_out.keep([own], sum_down)
    ffn_result = jnp.einsum(
        "fe,ft->et", w_down, after(inner_all, token), preferred_element_type=full
    )
    output_turned = (hidden + branch_scale * ffn_result).astype(low)
    output = to_rows(output_turned, rows)
    hidden_rows = to_rows(after(d_hidden, output_turned), rows)
    d_normed = own + after(across, token).astype(full)
    x_own = tokens.astype(full)
    factor_own = lax.rsqrt(jnp.mean(x_own * x_own, axis=-1, keepdims=True) + epsilon)
    unit_own = x_own * factor_own
    part = d_normed * gain_attn
    gain_attn_term = jnp.sum(d_normed * unit_own, axis=0)
    gain_ffn_wide = lax.dynamic_update_slice_in_dim(
        jnp.zeros((width,), full), gain_ffn_term[:, 0], me * width_cols, 0
    )
    d_tokens = hidden_rows.astype(full) + factor_own * (
        part - unit_own * jnp.mean(part * unit_own, axis=-1, keepdims=True)
    )
    grad_rest = sum_rest.sides_last([token])
    token = sum_attn.keep([d_tokens, output], sum_out)
    grad_gain_attn, grad_gain_ffn = sum_everywhere(jnp.stack([gain_attn_term, gain_ffn_wide]))
    grad_rest = sum_rest.sides_last([token])
    grad_query, grad_key, grad_value = sum_attn.result()
    (grad_out,) = sum_out.result()
    (grad_most,) = sum_most.result()
    grad_gate = grad_most[:, :hidden_cols]
    grad_up = jnp.concatenate([grad_most[:, hidden_cols:], grad_rest], axis=1)
    (grad_down,) = sum_down.result()
    return (
        output,
        d_tokens,
        grad_gain_attn,
        grad_gain_ffn,
        grad_query,
        grad_key,
        grad_value,
        grad_out,
        grad_gate,
        grad_up,
        grad_down.T,
    )


def solution(mesh):
    rows = P(("rep", "fsdp"), None)
    columns = P(None, "fsdp")
    both = P("rep", "fsdp")
    return jax.shard_map(
        body,
        mesh=mesh,
        in_specs=(rows, rows, P(), P()) + (columns,) * 7,
        out_specs=(rows, rows, P(), P()) + (both,) * 7,
        check_vma=False,
    )
```

```python
import math

import jax
import jax.numpy as jnp
from jax import lax
from jax.experimental import pallas as pl
from jax.experimental.pallas import tpu as pltpu
from jax.sharding import PartitionSpec as P

HD = 64
BLK = 256
NT = (((1,), (1,)), ((), ()))

epsilon = 1e-05
branch_scale = 1.4 / math.sqrt(40.0)
low = jnp.bfloat16
full = jnp.float32

SMALL = pl.CostEstimate(flops=0, bytes_accessed=0, transcendentals=0)


def turn(field, cosine, sine):
    half = field.shape[0] // 2
    first, second = field[:half], field[half:]
    return jnp.concatenate(
        [first * cosine - second * sine, second * cosine + first * sine], axis=0
    )


def forward_kernel(
    q_here, k_here, v_here, q_there, k_there, v_there, cos_ref, sin_ref,
    out_ref, ql_ref, kl_ref, vl_ref, lse_ref,
):
    cosine, sine = cos_ref[...], sin_ref[...]
    span = cosine.shape[1]
    chip = lax.axis_index("fsdp") // 2

    def join(here, there):
        return jnp.concatenate(
            [jnp.where(chip == 0, here[0], there[0]), jnp.where(chip == 0, there[0], here[0])],
            axis=1,
        )

    q_low = turn(join(q_here, q_there), cosine, sine).astype(low)
    k_low = turn(join(k_here, k_there), cosine, sine).astype(low)
    v_low = join(v_here, v_there).astype(low)
    ql_ref[0] = q_low
    kl_ref[0] = k_low
    vl_ref[0] = v_low
    q_scaled = (q_low * (HD ** (-0.5))).astype(low)
    k_rows = k_low.T
    for j in range(span // BLK):
        kv = (j + 1) * BLK
        cols = slice(j * BLK, kv)
        scores = jnp.dot(k_rows[:kv], q_scaled[:, cols], preferred_element_type=full)
        top = jnp.max(scores, axis=0, keepdims=True)
        expo = jnp.exp(scores - top)
        total = jnp.sum(expo, axis=0, keepdims=True)
        mixed = jnp.dot(v_low[:, :kv], expo.astype(low), preferred_element_type=full)
        out_ref[0, :, cols] = (mixed * (1.0 / total)).astype(low)
        lse_ref[0, :, cols] = top + jnp.log(total)


def attention_forward(here, there, cosine, sine):
    heads, _, part = here[0].shape
    span = cosine.shape[1]
    half = pl.BlockSpec((1, HD, part), lambda h: (h, 0, 0))
    spec = pl.BlockSpec((1, HD, span), lambda h: (h, 0, 0))
    table = pl.BlockSpec((HD // 2, span), lambda h: (0, 0))
    field = jax.ShapeDtypeStruct((heads, HD, span), low)
    row = pl.BlockSpec((1, 1, span), lambda h: (h, 0, 0))
    return pl.pallas_call(
        forward_kernel,
        grid=(heads,),
        in_specs=[half] * 6 + [table, table],
        out_specs=[spec, spec, spec, spec, row],
        out_shape=[field, field, field, field, jax.ShapeDtypeStruct((heads, 1, span), full)],
        compiler_params=pltpu.CompilerParams(vmem_limit_bytes=60 * 2**20),
        cost_estimate=SMALL,
        name="attention_forward",
    )(*here, *there, cosine, sine)


def backward_kernel(
    q_ref, k_ref, v_ref, g_ref, h_ref, out_ref, lse_ref, cos_ref, sin_ref, dq_ref, dk_ref, dv_ref, dk_acc, dv_acc
):
    cosine, sine = cos_ref[...], sin_ref[...]
    span = q_ref.shape[2]
    q_scaled = (q_ref[0] * (HD ** (-0.5))).astype(low)
    k_low, v_low = k_ref[0], v_ref[0]
    grad = (g_ref[0] + h_ref[0].astype(full)).astype(low)
    k_rows, v_rows = k_low.T, v_low.T
    deltas = jnp.sum(grad.astype(full) * out_ref[0].astype(full), axis=0, keepdims=True)
    dk_acc[...] = jnp.zeros_like(dk_acc)
    dv_acc[...] = jnp.zeros_like(dv_acc)
    for j in range(span // BLK):
        kv = (j + 1) * BLK
        cols = slice(j * BLK, kv)
        q_j, g_j = q_scaled[:, cols], grad[:, cols]
        scores = jnp.dot(k_rows[:kv], q_j, preferred_element_type=full)
        probs = jnp.exp(scores - lse_ref[0, :, cols])
        probs_low = probs.astype(low)
        d_probs = jnp.dot(v_rows[:kv], g_j, preferred_element_type=full)
        d_scores = (probs * (d_probs - deltas[:, cols])).astype(low)
        dq = jnp.dot(k_low[:, :kv], d_scores, preferred_element_type=full) * (HD ** (-0.5))
        dq_ref[0, :, cols] = turn(dq, cosine[:, cols], -sine[:, cols]).astype(low)
        dk_acc[:, :kv] += lax.dot_general(q_j, d_scores, NT, preferred_element_type=full)
        dv_acc[:, :kv] += lax.dot_general(g_j, probs_low, NT, preferred_element_type=full)
    dk_ref[0] = turn(dk_acc[...], cosine, -sine).astype(low)
    dv_ref[0] = dv_acc[...].astype(low)


def attention_backward(query, key, value, grad, rest, attended, lse, cosine, sine):
    heads, _, span = query.shape
    spec = pl.BlockSpec((1, HD, span), lambda h: (h, 0, 0))
    table = pl.BlockSpec((HD // 2, span), lambda h: (0, 0))
    row = pl.BlockSpec((1, 1, span), lambda h: (h, 0, 0))
    field = jax.ShapeDtypeStruct((heads, HD, span), low)
    return pl.pallas_call(
        backward_kernel,
        grid=(heads,),
        in_specs=[spec] * 6 + [row, table, table],
        out_specs=[spec, spec, spec],
        out_shape=[field, field, field],
        scratch_shapes=[pltpu.VMEM((HD, span), full), pltpu.VMEM((HD, span), full)],
        compiler_params=pltpu.CompilerParams(vmem_limit_bytes=60 * 2**20),
        cost_estimate=SMALL,
        name="attention_backward",
    )(query, key, value, grad, rest, attended, lse, cosine, sine)


def swap(array, j):
    size = lax.axis_size("fsdp")
    return lax.ppermute(array, "fsdp", [(i, i ^ j) for i in range(size)])


def after(value, *earlier):
    return lax.optimization_barrier((value, *earlier))[0]


def stage(run, *earlier):
    blank = lambda: jax.tree.map(lambda a: jnp.zeros(a.shape, a.dtype), jax.eval_shape(run))
    return lax.cond(after(jnp.bool_(True), *earlier), run, blank)


def place_kernel(*refs, parts):
    *blocks, out, held, arrived, left = refs
    me = lax.axis_index("fsdp")
    into, back = [], []
    for j in range(held.shape[0]):
        at = 0
        for i in range(j * parts, (j + 1) * parts):
            rows = blocks[i].shape[0]
            into.append(
                pltpu.make_async_copy(blocks[i], held.at[j, pl.ds(at, rows)], arrived.at[i])
            )
            at += rows
        back.append(
            pltpu.make_async_copy(
                held.at[j], out.at[lax.bitwise_xor(me, jnp.int32(j))], left.at[j]
            )
        )
    for copy in into:
        copy.start()
    for j, copy in enumerate(back):
        for part in into[j * parts : (j + 1) * parts]:
            part.wait()
        copy.start()
    for copy in back:
        copy.wait()


def place(blocks, parts=1, limit=60):
    count = len(blocks)
    size = count // parts
    rows = sum(block.shape[0] for block in blocks[:parts])
    shape = (size, rows, blocks[0].shape[1])
    dtype = blocks[0].dtype
    whole = pl.pallas_call(
        lambda *refs: place_kernel(*refs, parts=parts),
        in_specs=[pl.BlockSpec(memory_space=pl.ANY)] * count,
        out_specs=pl.BlockSpec(memory_space=pl.ANY),
        out_shape=jax.ShapeDtypeStruct(shape, dtype),
        scratch_shapes=[
            pltpu.VMEM(shape, dtype),
            pltpu.SemaphoreType.DMA((count,)),
            pltpu.SemaphoreType.DMA((size,)),
        ],
        compiler_params=pltpu.CompilerParams(vmem_limit_bytes=limit * 2**20),
        cost_estimate=SMALL,
        name="place",
    )(*blocks)
    return whole.reshape(size * rows, shape[2])


def gather(array, *before_last):
    core = swap(array, 1)
    chip = swap(array, 2)
    return [array, core, chip, swap(after(chip, *before_last) if before_last else chip, 1)]


def bring(blocks, held, arrived, rest=None):
    me = lax.axis_index("fsdp")
    cols = held.shape[1]
    count = len(blocks)
    copies = []
    for j, block in enumerate(blocks):
        to = held.at[lax.bitwise_xor(me, jnp.int32(j))]
        if rest is None:
            copies.append(pltpu.make_async_copy(block, to, arrived.at[j]))
        else:
            copies.append(pltpu.make_async_copy(block.at[pl.ds(0, cols)], to, arrived.at[j]))
            copies.append(
                pltpu.make_async_copy(
                    block.at[pl.ds(cols, 16)], rest.at[j], arrived.at[count + j]
                )
            )
    for copy in copies:
        copy.start()
    for copy in copies:
        copy.wait()


def spread_kernel(index, *refs, count, kept, normalize):
    step = pl.program_id(0)
    blocks, gain = refs[:count], refs[count]
    outs = refs[count + 1 + kept :]
    me = index[count]
    for j, block in enumerate(blocks):

        @pl.when(step == j)
        def _():
            x = block[...].astype(full)
            cols = outs[1].shape[0]
            if normalize:
                factor = lax.rsqrt(jnp.mean(x * x, axis=-1, keepdims=True) + epsilon)
                wide = (x * factor * gain[...]).astype(low)
                outs[2][...] = wide.T
            else:
                wide = (branch_scale * x).astype(low)
            outs[0][...] = wide
            for g in range(x.shape[1] // cols):

                @pl.when(me == g)
                def _():
                    outs[1][...] = x[:, g * cols : (g + 1) * cols].T


def spread(blocks, partners, gain, normalize, earlier=None):
    rows, width = blocks[0].shape
    size = lax.axis_size("fsdp")
    count = len(blocks)
    me = lax.axis_index("fsdp")
    tokens = [me ^ j for j in partners]
    local = [block % count for block in tokens]
    index = jnp.stack([jnp.asarray(v, jnp.int32) for v in (*local, me, *tokens)])
    const = lambda shape: pl.BlockSpec(shape, lambda i, index: (0,) * len(shape))
    kept = len(earlier) if earlier else 0
    outs = [
        (
            pl.BlockSpec((rows, width), lambda i, index: (index[i], 0)),
            jax.ShapeDtypeStruct((count * rows, width), low),
        ),
        (
            pl.BlockSpec((width // size, rows), lambda i, index: (0, index[count + 1 + i])),
            jax.ShapeDtypeStruct((width // size, size * rows), full),
        ),
    ]
    if normalize:
        outs.append(
            (
                pl.BlockSpec((width, rows), lambda i, index: (0, index[count + 1 + i])),
                jax.ShapeDtypeStruct((width, size * rows), low),
            )
        )
    return pl.pallas_call(
        lambda *refs: spread_kernel(*refs, count=count, kept=kept, normalize=normalize),
        grid_spec=pltpu.PrefetchScalarGridSpec(
            num_scalar_prefetch=1,
            grid=(count,),
            in_specs=[const((rows, width))] * count
            + [const((1, width))]
            + [pl.BlockSpec(memory_space=pl.ANY)] * kept,
            out_specs=[spec for spec, _ in outs],
        ),
        out_shape=[shape for _, shape in outs],
        input_output_aliases={count + 2 + i: 1 + i for i in range(kept)},
        compiler_params=pltpu.CompilerParams(vmem_limit_bytes=32 * 2**20),
        cost_estimate=SMALL,
        name="spread",
    )(index, *blocks, gain[None, :], *(earlier or ()))


def hidden_kernel(
    own, core, chip, both, weight, tokens, gain, hidden_ref, first_ref, second_ref, all_ref,
    squares_ref, held, arrived, left,
):
    step = pl.program_id(0)
    out = pltpu.make_async_copy(held, all_ref, left.at[0])

    @pl.when(step == 0)
    def _():
        bring((own, core, chip, both), held, arrived)
        out.start()

    span = held.shape[2]
    result = jnp.dot(
        weight[...], held[...].reshape(-1, span), preferred_element_type=full
    )
    hidden = tokens[...] + branch_scale * result
    tile = hidden.shape[0]
    at = pl.multiple_of(step * tile, tile)
    hidden_ref[pl.ds(at, tile), :] = hidden
    part = span // 2
    halves = [(first_ref, slice(0, part)), (second_ref, slice(part, span))]
    for ref, cut in halves:
        ref[pl.ds(at, tile), :] = (hidden[:, cut] * gain[...]).astype(low)
    squares = jnp.sum(hidden * hidden, axis=0, keepdims=True)

    @pl.when(step == 0)
    def _():
        squares_ref[...] = squares

    @pl.when(step != 0)
    def _():
        squares_ref[...] += squares

    @pl.when(step == pl.num_programs(0) - 1)
    def _():
        total = squares_ref[...]
        high = total.astype(low)
        rest = (total - high.astype(full)).astype(low)
        cols = hidden_ref.shape[0]
        for ref, cut in halves:
            ref[cols : cols + 8] = jnp.broadcast_to(high[:, cut], (8, part))
            ref[cols + 8 :] = jnp.broadcast_to(rest[:, cut], (8, part))
        out.wait()


def hidden_state(blocks, weight, tokens, gain):
    cols, span = blocks[0].shape
    size = len(blocks)
    tiles = 2
    tile = cols // tiles
    hbm = pl.BlockSpec(memory_space=pl.ANY)
    rows = lambda wide: pl.BlockSpec((tile, wide), lambda i: (i, 0))
    const = lambda shape: pl.BlockSpec(shape, lambda i: (0, 0))
    half = const((cols + 16, span // 2))
    hidden, first, second, whole = pl.pallas_call(
        hidden_kernel,
        grid=(tiles,),
        in_specs=[hbm] * 4 + [rows(size * cols), rows(span), rows(1)],
        out_specs=[const((cols, span)), half, half, hbm],
        out_shape=[
            jax.ShapeDtypeStruct((cols, span), full),
            jax.ShapeDtypeStruct((cols + 16, span // 2), low),
            jax.ShapeDtypeStruct((cols + 16, span // 2), low),
            jax.ShapeDtypeStruct((size, cols, span), low),
        ],
        scratch_shapes=[
            pltpu.VMEM((1, span), full),
            pltpu.VMEM((size, cols, span), low),
            pltpu.SemaphoreType.DMA((size,)),
            pltpu.SemaphoreType.DMA((1,)),
        ],
        compiler_params=pltpu.CompilerParams(vmem_limit_bytes=60 * 2**20),
        cost_estimate=SMALL,
        name="hidden_state",
    )(*blocks, weight, tokens, gain)
    return hidden, first, second, whole.reshape(size * cols, span)


def inner_kernel(*refs, half):
    blocks, (w_gate, w_up, d_inner), refs = refs[:4], refs[4:7], refs[7:]
    inner_ref, grads_ref, mean_ref, factor_ref, all_ref, held, rest, arrived, left = refs[5 * half :]
    step = pl.program_id(0)
    span = held.shape[2]
    out = pltpu.make_async_copy(
        held, all_ref.at[:, :, pl.ds(half * span, span)], left.at[0]
    )

    @pl.when(step == 0)
    def _():
        bring(blocks, held, arrived, rest)
        out.start()
        squares = [
            rest[j, 0:1].astype(full) + rest[j, 8:9].astype(full) for j in range(held.shape[0])
        ]
        total = (squares[0] + squares[1]) + (squares[2] + squares[3])
        factor_ref[...] = lax.rsqrt(total / (held.shape[0] * held.shape[1]) + epsilon)

        mean_ref[...] = jnp.zeros_like(mean_ref)

    wide = BLK
    for part in range(span // wide):
        cut = slice(part * wide, (part + 1) * wide)
        scaled = held[:, :, cut].reshape(-1, wide)
        factor = factor_ref[:, cut]
        gate = factor * jnp.dot(w_gate[...], scaled, preferred_element_type=full)
        up = factor * jnp.dot(w_up[...], scaled, preferred_element_type=full)
        sigmoid = 0.5 * jnp.tanh(0.5 * gate) + 0.5
        activated = gate * sigmoid
        inner_ref[:, cut] = (activated * up).astype(low)
        grad = factor * d_inner[:, cut].astype(full)
        d_up = grad * activated
        d_gate = grad * up * (sigmoid + activated * (1.0 - sigmoid))
        grads_ref[0, :, cut] = d_gate.astype(low)
        grads_ref[1, :, cut] = d_up.astype(low)
        mean_ref[:, cut] += jnp.sum(d_gate * gate + d_up * up, axis=0, keepdims=True)

    @pl.when(step == pl.num_programs(0) - 1)
    def _():
        out.wait()


def inner_part(half, blocks, w_gate, w_up, d_inner, before=()):
    tall, span = blocks[0].shape
    cols = tall - 16
    size = len(blocks)
    units = w_gate.shape[0]
    tile = units // 3
    hbm = pl.BlockSpec(memory_space=pl.ANY)
    weight = pl.BlockSpec((tile, size * cols), lambda i: (i, 0))
    part = pl.BlockSpec((tile, span), lambda i: (i, half))
    row = pl.BlockSpec((1, span), lambda i: (0, half))
    return pl.pallas_call(
        lambda *refs: inner_kernel(*refs, half=half),
        grid=(units // tile,),
        in_specs=[hbm] * 4 + [weight, weight, part] + [hbm] * len(before),
        out_specs=[part, pl.BlockSpec((2, tile, span), lambda i: (0, i, half)), row, row, hbm],
        out_shape=[
            jax.ShapeDtypeStruct((units, 2 * span), low),
            jax.ShapeDtypeStruct((2, units, 2 * span), low),
            jax.ShapeDtypeStruct((1, 2 * span), full),
            jax.ShapeDtypeStruct((1, 2 * span), full),
            jax.ShapeDtypeStruct((size, cols, 2 * span), low),
        ],
        input_output_aliases={7 + i: i for i in range(len(before))},
        scratch_shapes=[
            pltpu.VMEM((size, cols, span), low),
            pltpu.VMEM((size, 16, span), low),
            pltpu.SemaphoreType.DMA((2 * size,)),
            pltpu.SemaphoreType.DMA((1,)),
        ],
        compiler_params=pltpu.CompilerParams(vmem_limit_bytes=60 * 2**20),
        cost_estimate=SMALL,
        name="inner_part",
    )(*blocks, w_gate, w_up, d_inner, *before)


def to_rows(field, rows):
    me = lax.axis_index("fsdp")
    size = lax.axis_size("fsdp")
    blocks = []
    for j in range(size):
        block = lax.dynamic_slice_in_dim(field, (me ^ j) * rows, rows, 1)
        blocks.append(block if j == 0 else swap(block, j))
    return place(blocks).T


def product_kernel(index, act, *refs, count, adds, turned):
    grads = refs[:count]
    added = refs[count] if adds else None
    out = refs[-1]
    rows = act[:, 0].reshape(-1, act.shape[-1])
    for k in range(count):
        pair = (grads[k][...], rows) if turned else (rows, grads[k][...])
        total = lax.dot_general(*pair, NT, preferred_element_type=full)
        if turned:
            if adds:
                total = total + added[0, k].astype(full)
            out[0, k] = total.astype(low)
            continue
        total = total.reshape((act.shape[0], act.shape[2]) + total.shape[1:])
        if adds:
            total = total + added[:, k].astype(full)
        out[:, k] = total.astype(low)


def half_product(act, grads, side, added=None, turned=False, columns=None, earlier=()):
    size = lax.axis_size("rep")
    count = len(grads)
    tokens = grads[0].shape[1]
    columns = columns or grads[0].shape[0]
    lines, rows = size // 2, act.shape[0] // size
    index = jnp.asarray(side, jnp.int32)[None]
    if earlier:
        index = after(index, *earlier)
    steps = lines
    some = lines // steps
    shape = (columns, rows) if turned else (rows, columns)
    piece = pl.BlockSpec((some, count) + shape, lambda i, index: (i, 0, 0, 0))
    return pl.pallas_call(
        lambda *refs: product_kernel(*refs, count=count, adds=added is not None, turned=turned),
        grid_spec=pltpu.PrefetchScalarGridSpec(
            num_scalar_prefetch=1,
            grid=(steps,),
            in_specs=[pl.BlockSpec((some, 1, rows, tokens), lambda i, index: (i, index[0], 0, 0))]
            + [pl.BlockSpec((columns, tokens), lambda i, index: (0, 0))] * count
            + ([] if added is None else [piece]),
            out_specs=piece,
        ),
        out_shape=jax.ShapeDtypeStruct((lines, count) + shape, low),
        compiler_params=pltpu.CompilerParams(vmem_limit_bytes=60 * 2**20),
        cost_estimate=SMALL,
        name="half_product",
    )(index, act.reshape(lines, 2, rows, tokens), *grads, *(() if added is None else (added,)))


def whole_kernel(act, grad, out):
    out[0] = lax.dot_general(act[0], grad[...], NT, preferred_element_type=full).astype(low)


def whole_product(act, grad, columns):
    lines = lax.axis_size("rep") // 2
    tokens = grad.shape[1]
    last = grad.shape[0] // columns - 1
    rows = act.shape[0] // lines
    return pl.pallas_call(
        whole_kernel,
        grid=(lines,),
        in_specs=[
            pl.BlockSpec((1, rows, tokens), lambda i: (i, 0, 0)),
            pl.BlockSpec((columns, tokens), lambda i: (last, 0)),
        ],
        out_specs=pl.BlockSpec((1, rows, columns), lambda i: (i, 0, 0)),
        out_shape=jax.ShapeDtypeStruct((lines, rows, columns), low),
        compiler_params=pltpu.CompilerParams(vmem_limit_bytes=60 * 2**20),
        cost_estimate=SMALL,
        name="whole_product",
    )(act.reshape(lines, rows, tokens), grad)


def neighbour(array):
    return lax.ppermute(array, "rep", [(i, i ^ 1) for i in range(lax.axis_size("rep"))])


def line_scatter(array):
    size = lax.axis_size("rep")
    groups = [list(range(side, size, 2)) for side in range(2)]
    return lax.psum_scatter(
        array, "rep", scatter_dimension=0, tiled=True, axis_index_groups=groups
    )


class GradSum:
    def __init__(self, act, grads, turned=False, columns=None):
        self.act, self.grads, self.turned, self.columns = act, grads, turned, columns
        self.side = lax.axis_index("rep") % 2

    def send(self, earlier=()):
        sent = half_product(
            self.act,
            self.grads,
            1 - self.side,
            turned=self.turned,
            columns=self.columns,
            earlier=earlier,
        )
        return sent

    def transfer(self, sent):
        self.arrived = neighbour(sent)

    def keep(self, earlier=(), last=None):
        kept = half_product(
            self.act,
            self.grads,
            self.side,
            self.arrived,
            turned=self.turned,
            columns=self.columns,
            earlier=earlier,
        )
        self.sums = line_scatter(kept if last is None else after(kept, last.sums))
        return kept

    def line_first(self, earlier=()):
        whole = whole_product(self.act, after(self.grads[0], *earlier), self.columns)
        self.sums = line_scatter(whole)
        return whole

    def sides_last(self, earlier=()):
        _, rows, columns = self.sums.shape
        parts = self.sums.reshape(2, rows // 2, columns)
        side = after(self.side, *earlier)
        sent = lax.dynamic_index_in_dim(parts, 1 - side, 0, False)
        kept = lax.dynamic_index_in_dim(parts, side, 0, False)
        return kept.astype(full) + neighbour(sent).astype(full)

    def result(self):
        return [self.sums[0, k].astype(full) for k in range(len(self.grads))]


def sum_everywhere(array):
    array = (array + swap(array, 1)) + (swap(array, 2) + swap(array, 3))
    size = lax.axis_size("rep")
    far = 1
    while far < size:
        array = array + lax.ppermute(array, "rep", [(i, i ^ far) for i in range(size)])
        far *= 2
    return array


def flip_kernel(*refs):
    count = len(refs) // 2
    for wide, tall in zip(refs[:count], refs[count:]):
        tall[...] = wide[...].T


def flip(arrays, tiles, earlier=()):
    width = arrays[0].shape[1]
    tile = width // tiles
    index = jnp.zeros((1,), jnp.int32)
    if earlier:
        index = after(index, *earlier)
    return pl.pallas_call(
        lambda index, *refs: flip_kernel(*refs),
        grid_spec=pltpu.PrefetchScalarGridSpec(
            num_scalar_prefetch=1,
            grid=(tiles,),
            in_specs=[pl.BlockSpec((a.shape[0], tile), lambda i, index: (0, i)) for a in arrays],
            out_specs=[pl.BlockSpec((tile, a.shape[0]), lambda i, index: (i, 0)) for a in arrays],
        ),
        out_shape=[jax.ShapeDtypeStruct((width, a.shape[0]), a.dtype) for a in arrays],
        compiler_params=pltpu.CompilerParams(vmem_limit_bytes=60 * 2**20),
        cost_estimate=SMALL,
        name="flip",
    )(index, *arrays)


def chunks_kernel(index, *refs, count, ways, added, extra):
    step = pl.program_id(1)
    weights, grads, refs = refs[:count], refs[count], refs[count + 1 :]
    plus, refs = refs[:added], refs[added:]
    row, outs = refs[:extra], refs[extra:]
    total, at = None, 0
    for weight in weights:
        units = weight.shape[1]
        term = jnp.dot(weight[...], grads[at : at + units], preferred_element_type=full)
        total = term if total is None else total + term
        at += units
    cols = total.shape[0]
    for way, out in enumerate(outs):

        @pl.when(step == way)
        def _():
            found = total + plus[way][:cols].astype(full) if plus else total
            out[:cols] = found.astype(out.dtype)
            if row:
                found = row[0][...]
                if plus:
                    found = found + plus[way][cols : cols + 1].astype(full)
                out[cols:] = jnp.broadcast_to(
                    found.astype(out.dtype), (out.shape[0] - cols, found.shape[1])
                )


def feature_chunks(weights, grads, partners, plus=(), extra=None, dtype=low, earlier=()):
    me = lax.axis_index("fsdp")
    span = grads.shape[1]
    cols = weights[0].shape[0] // lax.axis_size("fsdp")
    tall = cols + (0 if extra is None else 16)
    index = jnp.stack([jnp.asarray(me ^ j, jnp.int32) for j in partners])
    if earlier:
        index = after(index, *earlier)
    extra = () if extra is None else (extra,)
    tiles = 2
    tile = lambda rows: pl.BlockSpec((rows, span // tiles), lambda i, k, index: (0, i))
    return pl.pallas_call(
        lambda *refs: chunks_kernel(
            *refs, count=len(weights), ways=len(partners), added=len(plus), extra=len(extra)
        ),
        grid_spec=pltpu.PrefetchScalarGridSpec(
            num_scalar_prefetch=1,
            grid=(tiles, len(partners)),
            in_specs=[
                pl.BlockSpec((cols, w.shape[1]), lambda i, k, index: (index[k], 0))
                for w in weights
            ]
            + [tile(a.shape[0]) for a in (grads, *plus, *extra)],
            out_specs=[tile(tall)] * len(partners),
        ),
        out_shape=[jax.ShapeDtypeStruct((tall, span), dtype)] * len(partners),
        compiler_params=pltpu.CompilerParams(vmem_limit_bytes=60 * 2**20),
        cost_estimate=SMALL,
        name="feature_chunks",
    )(index, *weights, grads, *plus, *extra)


def attn_grad_kernel(
    own, across, cotangent, hidden, gain, factor, attn_ref, hidden_ref, term_ref, *, width
):
    cols = hidden.shape[0]
    mean = (own[cols : cols + 1] + across[cols : cols + 1].astype(full)) * (1.0 / width)
    scaled = own[:cols] + across[:cols].astype(full)
    state = hidden[...]
    term = jnp.sum(scaled * state, axis=1, keepdims=True)
    step = pl.program_id(0)

    @pl.when(step == 0)
    def _():
        term_ref[...] = term

    @pl.when(step != 0)
    def _():
        term_ref[...] += term

    grad = cotangent[...] + gain[...] * scaled - state * (factor[...] * mean)
    hidden_ref[...] = grad.astype(low)
    attn_ref[...] = (branch_scale * grad).astype(low)


def attn_grad(own, across, cotangent, hidden, gain, factor, width):
    cols, span = hidden.shape
    field = jax.ShapeDtypeStruct((cols, span), low)
    tiles = 4
    tile = lambda rows: pl.BlockSpec((rows, span // tiles), lambda i: (0, i))
    once = pl.BlockSpec((cols, 1), lambda i: (0, 0))
    return pl.pallas_call(
        lambda *refs: attn_grad_kernel(*refs, width=width),
        grid=(tiles,),
        in_specs=[tile(cols + 16), tile(cols + 16), tile(cols), tile(cols), once, tile(1)],
        out_specs=[tile(cols), tile(cols), once],
        out_shape=[field, field, jax.ShapeDtypeStruct((cols, 1), full)],
        compiler_params=pltpu.CompilerParams(vmem_limit_bytes=60 * 2**20),
        cost_estimate=SMALL,
        name="attn_grad",
    )(own, across, cotangent, hidden, gain, factor)


def blocks_kernel(index, *refs, count, added):
    step = pl.program_id(0)
    weights, refs = refs[:count], refs[count:]
    grads, refs = refs[:count], refs[count:]
    plus, outs = refs[:added], refs[added:]
    total = None
    for weight, grad in zip(weights, grads):
        term = jnp.dot(grad[...].T, weight[...], preferred_element_type=full)
        total = term if total is None else total + term
    for way, out in enumerate(outs):

        @pl.when(step == way)
        def _():
            found = total + plus[way][...].astype(full) if plus else total
            out[...] = found.astype(out.dtype)


def token_chunks(weights, grads, partners, rows, plus=(), dtype=low, earlier=()):
    me = lax.axis_index("fsdp")
    width = weights[0].shape[1]
    index = jnp.stack([jnp.asarray(me ^ j, jnp.int32) for j in partners])
    if earlier:
        index = after(index, *earlier)
    const = lambda shape: pl.BlockSpec(shape, lambda i, index: (0, 0))
    return pl.pallas_call(
        lambda *refs: blocks_kernel(*refs, count=len(weights), added=len(plus)),
        grid_spec=pltpu.PrefetchScalarGridSpec(
            num_scalar_prefetch=1,
            grid=(len(partners),),
            in_specs=[const(w.shape) for w in weights]
            + [pl.BlockSpec((g.shape[0], rows), lambda i, index: (0, index[i])) for g in grads]
            + [const(a.shape) for a in plus],
            out_specs=[const((rows, width))] * len(partners),
        ),
        out_shape=[jax.ShapeDtypeStruct((rows, width), dtype)] * len(partners),
        compiler_params=pltpu.CompilerParams(vmem_limit_bytes=60 * 2**20),
        cost_estimate=SMALL,
        name="token_chunks",
    )(index, *weights, *grads, *plus)


def body(
    tokens, cotangent, gain_attn, gain_ffn, w_query, w_key, w_value, w_out, w_gate, w_up, w_down
):
    rows, width = tokens.shape
    size = lax.axis_size("fsdp")
    reps = lax.axis_size("rep")
    span = rows * size
    me = lax.axis_index("fsdp")
    replica = lax.axis_index("rep")
    width_cols = width // size
    hidden_cols = w_gate.shape[1]
    heads = width_cols // HD

    half = HD // 2
    frequency = 10000.0 ** (-(jnp.arange(half, dtype=full) * 2.0 / HD))
    angles = frequency[:, None] * jnp.arange(span, dtype=jnp.int32).astype(full)[None, :]
    cosine, sine = jnp.cos(angles), jnp.sin(angles)

    def own_gain(gain):
        return lax.dynamic_slice_in_dim(gain, me * width_cols, width_cols, 0)[:, None]

    down_turned = w_down.T
    share = width_cols // reps

    def down_part(j):
        return lax.dynamic_slice(
            down_turned, (replica * share, (me ^ j) * hidden_cols), (share, hidden_cols)
        )

    parts = [down_part(2), down_part(3)]

    def project(normed):
        found = []
        for weight in (w_query, w_key, w_value):
            field = jnp.einsum("de,td->et", weight, normed, preferred_element_type=full)
            found.append(field.reshape(heads, HD, normed.shape[0]))
        return found

    tokens_chip = swap(tokens, 2)
    normed_here, tokens_part, normed_part = spread(
        [tokens, swap(tokens, 1)], (0, 1), gain_attn, True
    )
    here = project(normed_here)
    tokens_chip = after(tokens_chip, *here)
    parts = [swap(after(part, tokens_chip), 2) for part in parts]
    normed_there, tokens_own, normed_turned = spread(
        [tokens_chip, swap(tokens_chip, 1)],
        (2, 3),
        gain_attn,
        True,
        (tokens_part, normed_part),
    )
    there = project(normed_there)
    parts = [after(part, *there) for part in parts]
    cotangent_chip = swap(after(cotangent, *parts), 2)
    parts_all = lax.all_gather(
        jnp.stack([parts[0], swap(parts[1], 1)]), "rep", axis=1, tiled=True
    )
    attended, query_low, key_low, value_low, lse = attention_forward(here, there, cosine, sine)

    cotangent_blocks = [
        cotangent, swap(cotangent, 1), cotangent_chip, swap(after(cotangent_chip, attended), 1)
    ]
    d_ffn, cotangent_own = spread(cotangent_blocks, (0, 1, 2, 3), gain_attn, False)
    d_ffn_own = (branch_scale * cotangent_own).astype(low)
    me_later = after(me, d_ffn)

    def down_block(j):
        return lax.dynamic_slice_in_dim(
            down_turned, (me_later ^ j) * hidden_cols, hidden_cols, 1
        )

    down_near = [down_block(0), swap(down_block(1), 1)]
    gate_tall, up_tall = flip([w_gate.T, w_up.T], 6, [down_near[0]])
    (out_tall,) = flip([w_out.T], 6, [gate_tall])
    attended_blocks = gather(attended.reshape(width_cols, span), out_tall)

    gain_own = own_gain(gain_ffn)
    hidden, scaled_first, scaled_second, attended_all = hidden_state(
        attended_blocks, w_out.T, tokens_own, gain_own
    )
    scaled_chip = swap(scaled_first, 2)

    down_own = place(
        [after(down_near[0], hidden), down_near[1], parts_all[0], parts_all[1]], limit=16
    )
    d_inner = jnp.einsum("ef,te->ft", down_own, d_ffn, preferred_element_type=full).astype(low)
    scaled_chip = after(scaled_chip, d_inner)
    scaled_first = [scaled_first, swap(scaled_first, 1), scaled_chip, swap(scaled_chip, 1)]
    second_chip = swap(after(scaled_second, scaled_chip), 2)

    first = stage(lambda: inner_part(0, scaled_first, w_gate.T, w_up.T, d_inner), d_inner)
    second_chip = after(second_chip, first[2])
    scaled_second = [scaled_second, swap(scaled_second, 1), second_chip, swap(second_chip, 1)]
    inner, ffn_grads, mean, factor, scaled_all = inner_part(
        1, scaled_second, w_gate.T, w_up.T, d_inner, first
    )
    ffn_grads = ffn_grads.reshape(2 * hidden_cols, span)
    scaled_all = scaled_all.reshape(width, span)

    third = 2 * hidden_cols // 3
    sum_most = GradSum(scaled_all, [ffn_grads], columns=2 * third)
    sum_rest = GradSum(scaled_all, [ffn_grads], columns=third)
    token = sum_rest.line_first()
    token = sum_most.send([token])
    sum_most.transfer(token)
    inner_chip = swap(inner, 2)
    inner_core = swap(inner, 1)
    ffn_weights = (gate_tall, up_tall)

    def first_stage():
        far, near = feature_chunks(ffn_weights, ffn_grads, (3, 1), extra=mean)
        far, near = swap(far, 1), swap(near, 1)
        (chunk,) = feature_chunks(ffn_weights, ffn_grads, (2,), plus=[far], extra=mean)
        return chunk, near

    chunk, near = stage(first_stage, token)
    across = swap(chunk, 2)
    (own,) = feature_chunks(ffn_weights, ffn_grads, (0,), plus=[near], extra=mean, dtype=full)
    inner_late = after(inner_chip, own)
    inner_all = place([inner, inner_core, inner_late, swap(inner_late, 1)])
    sum_down = GradSum(inner_all, [d_ffn_own], turned=True)
    token = sum_down.send()
    sum_down.transfer(token)
    d_attn, d_hidden, gain_ffn_term = attn_grad(
        own, after(across, token), cotangent_own, hidden, gain_own, factor, width
    )

    far, near = feature_chunks([out_tall], d_attn, (3, 1))
    far, near = swap(far, 1), swap(near, 1)
    token = sum_most.keep([far], sum_rest)
    (chunk,) = feature_chunks([out_tall], d_attn, (2,), plus=[far], earlier=[token])
    across = swap(chunk, 2)
    (own,) = feature_chunks([out_tall], d_attn, (0,), plus=[near], dtype=full, earlier=[chunk])
    sum_out = GradSum(attended_all, [d_attn])
    token = sum_out.send([own])
    sum_out.transfer(token)
    across = after(across, token)

    def second_stage():
        d_query, d_key, d_value = (
            field.reshape(width_cols, span)
            for field in attention_backward(
                query_low,
                key_low,
                value_low,
                own.reshape(heads, HD, span),
                across.reshape(heads, HD, span),
                attended,
                lse,
                cosine,
                sine,
            )
        )
        sent = GradSum(normed_turned, [d_query, d_key, d_value]).send()
        return d_query, d_key, d_value, sent

    d_query, d_key, d_value, sent = second_stage()
    sum_attn = GradSum(normed_turned, [d_query, d_key, d_value])
    sum_attn.transfer(sent)
    token = sum_down.keep([sent], sum_most)

    def third_stage():
        attn_weights, attn_grads = (w_query.T, w_key.T, w_value.T), (d_query, d_key, d_value)
        far, near = token_chunks(attn_weights, attn_grads, (3, 1), rows)
        far, near = swap(far, 1), swap(near, 1)
        (chunk,) = token_chunks(attn_weights, attn_grads, (2,), rows, plus=[far])
        across = swap(chunk, 2)
        (own,) = token_chunks(
            attn_weights, attn_grads, (0,), rows, plus=[near], dtype=full, earlier=[chunk]
        )
        return own, across

    own, across = stage(third_stage, token)
    token = sum_out.keep([own], sum_down)
    ffn_result = jnp.einsum(
        "fe,ft->et", w_down, after(inner_all, token), preferred_element_type=full
    )
    output_turned = (hidden + branch_scale * ffn_result).astype(low)
    output = to_rows(output_turned, rows)
    hidden_rows = to_rows(after(d_hidden, output_turned), rows)
    d_normed = own + after(across, token).astype(full)
    x_own = tokens.astype(full)
    factor_own = lax.rsqrt(jnp.mean(x_own * x_own, axis=-1, keepdims=True) + epsilon)
    unit_own = x_own * factor_own
    part = d_normed * gain_attn
    gain_attn_term = jnp.sum(d_normed * unit_own, axis=0)
    gain_ffn_wide = lax.dynamic_update_slice_in_dim(
        jnp.zeros((width,), full), gain_ffn_term[:, 0], me * width_cols, 0
    )
    d_tokens = hidden_rows.astype(full) + factor_own * (
        part - unit_own * jnp.mean(part * unit_own, axis=-1, keepdims=True)
    )
    grad_rest = sum_rest.sides_last([token])
    token = sum_attn.keep([d_tokens, output], sum_out)
    grad_gain_attn, grad_gain_ffn = sum_everywhere(jnp.stack([gain_attn_term, gain_ffn_wide]))
    grad_rest = sum_rest.sides_last([token])
    grad_query, grad_key, grad_value = sum_attn.result()
    (grad_out,) = sum_out.result()
    (grad_most,) = sum_most.result()
    grad_gate = grad_most[:, :hidden_cols]
    grad_up = jnp.concatenate([grad_most[:, hidden_cols:], grad_rest], axis=1)
    (grad_down,) = sum_down.result()
    return (
        output,
        d_tokens,
        grad_gain_attn,
        grad_gain_ffn,
        grad_query,
        grad_key,
        grad_value,
        grad_out,
        grad_gate,
        grad_up,
        grad_down.T,
    )


def solution(mesh):
    rows = P(("rep", "fsdp"), None)
    columns = P(None, "fsdp")
    both = P("rep", "fsdp")
    return jax.shard_map(
        body,
        mesh=mesh,
        in_specs=(rows, rows, P(), P()) + (columns,) * 7,
        out_specs=(rows, rows, P(), P()) + (both,) * 7,
        check_vma=False,
    )
```

```python
import math

import jax
import jax.numpy as jnp
from jax import lax
from jax.experimental import pallas as pl
from jax.experimental.pallas import tpu as pltpu
from jax.sharding import PartitionSpec as P

HD = 64
BLK = 256
NT = (((1,), (1,)), ((), ()))

epsilon = 1e-05
branch_scale = 1.4 / math.sqrt(40.0)
low = jnp.bfloat16
full = jnp.float32

SMALL = pl.CostEstimate(flops=0, bytes_accessed=0, transcendentals=0)


def turn(field, cosine, sine):
    half = field.shape[0] // 2
    first, second = field[:half], field[half:]
    return jnp.concatenate(
        [first * cosine - second * sine, second * cosine + first * sine], axis=0
    )


def forward_kernel(
    q_here, k_here, v_here, q_there, k_there, v_there, cos_ref, sin_ref,
    out_ref, ql_ref, kl_ref, vl_ref, lse_ref,
):
    cosine, sine = cos_ref[...], sin_ref[...]
    span = cosine.shape[1]
    chip = lax.axis_index("fsdp") // 2

    def join(here, there):
        return jnp.concatenate(
            [jnp.where(chip == 0, here[0], there[0]), jnp.where(chip == 0, there[0], here[0])],
            axis=1,
        )

    q_low = turn(join(q_here, q_there), cosine, sine).astype(low)
    k_low = turn(join(k_here, k_there), cosine, sine).astype(low)
    v_low = join(v_here, v_there).astype(low)
    ql_ref[0] = q_low
    kl_ref[0] = k_low
    vl_ref[0] = v_low
    q_scaled = (q_low * (HD ** (-0.5))).astype(low)
    k_rows = k_low.T
    for j in range(span // BLK):
        kv = (j + 1) * BLK
        cols = slice(j * BLK, kv)
        scores = jnp.dot(k_rows[:kv], q_scaled[:, cols], preferred_element_type=full)
        top = jnp.max(scores, axis=0, keepdims=True)
        expo = jnp.exp(scores - top)
        total = jnp.sum(expo, axis=0, keepdims=True)
        mixed = jnp.dot(v_low[:, :kv], expo.astype(low), preferred_element_type=full)
        out_ref[0, :, cols] = (mixed * (1.0 / total)).astype(low)
        lse_ref[0, :, cols] = top + jnp.log(total)


def attention_forward(here, there, cosine, sine):
    heads, _, part = here[0].shape
    span = cosine.shape[1]
    half = pl.BlockSpec((1, HD, part), lambda h: (h, 0, 0))
    spec = pl.BlockSpec((1, HD, span), lambda h: (h, 0, 0))
    table = pl.BlockSpec((HD // 2, span), lambda h: (0, 0))
    field = jax.ShapeDtypeStruct((heads, HD, span), low)
    row = pl.BlockSpec((1, 1, span), lambda h: (h, 0, 0))
    return pl.pallas_call(
        forward_kernel,
        grid=(heads,),
        in_specs=[half] * 6 + [table, table],
        out_specs=[spec, spec, spec, spec, row],
        out_shape=[field, field, field, field, jax.ShapeDtypeStruct((heads, 1, span), full)],
        compiler_params=pltpu.CompilerParams(vmem_limit_bytes=60 * 2**20),
        cost_estimate=SMALL,
        name="attention_forward",
    )(*here, *there, cosine, sine)


def backward_kernel(
    q_ref, k_ref, v_ref, g_ref, h_ref, out_ref, lse_ref, cos_ref, sin_ref, dq_ref, dk_ref, dv_ref, dk_acc, dv_acc
):
    cosine, sine = cos_ref[...], sin_ref[...]
    span = q_ref.shape[2]
    q_scaled = (q_ref[0] * (HD ** (-0.5))).astype(low)
    k_low, v_low = k_ref[0], v_ref[0]
    grad = (g_ref[0] + h_ref[0].astype(full)).astype(low)
    k_rows, v_rows = k_low.T, v_low.T
    deltas = jnp.sum(grad.astype(full) * out_ref[0].astype(full), axis=0, keepdims=True)
    dk_acc[...] = jnp.zeros_like(dk_acc)
    dv_acc[...] = jnp.zeros_like(dv_acc)
    for j in range(span // BLK):
        kv = (j + 1) * BLK
        cols = slice(j * BLK, kv)
        q_j, g_j = q_scaled[:, cols], grad[:, cols]
        scores = jnp.dot(k_rows[:kv], q_j, preferred_element_type=full)
        probs = jnp.exp(scores - lse_ref[0, :, cols])
        probs_low = probs.astype(low)
        d_probs = jnp.dot(v_rows[:kv], g_j, preferred_element_type=full)
        d_scores = (probs * (d_probs - deltas[:, cols])).astype(low)
        dq = jnp.dot(k_low[:, :kv], d_scores, preferred_element_type=full) * (HD ** (-0.5))
        dq_ref[0, :, cols] = turn(dq, cosine[:, cols], -sine[:, cols]).astype(low)
        dk_acc[:, :kv] += lax.dot_general(q_j, d_scores, NT, preferred_element_type=full)
        dv_acc[:, :kv] += lax.dot_general(g_j, probs_low, NT, preferred_element_type=full)
    dk_ref[0] = turn(dk_acc[...], cosine, -sine).astype(low)
    dv_ref[0] = dv_acc[...].astype(low)


def attention_backward(query, key, value, grad, rest, attended, lse, cosine, sine):
    heads, _, span = query.shape
    spec = pl.BlockSpec((1, HD, span), lambda h: (h, 0, 0))
    table = pl.BlockSpec((HD // 2, span), lambda h: (0, 0))
    row = pl.BlockSpec((1, 1, span), lambda h: (h, 0, 0))
    field = jax.ShapeDtypeStruct((heads, HD, span), low)
    return pl.pallas_call(
        backward_kernel,
        grid=(heads,),
        in_specs=[spec] * 6 + [row, table, table],
        out_specs=[spec, spec, spec],
        out_shape=[field, field, field],
        scratch_shapes=[pltpu.VMEM((HD, span), full), pltpu.VMEM((HD, span), full)],
        compiler_params=pltpu.CompilerParams(vmem_limit_bytes=60 * 2**20),
        cost_estimate=SMALL,
        name="attention_backward",
    )(query, key, value, grad, rest, attended, lse, cosine, sine)


def swap(array, j):
    size = lax.axis_size("fsdp")
    return lax.ppermute(array, "fsdp", [(i, i ^ j) for i in range(size)])


def after(value, *earlier):
    return lax.optimization_barrier((value, *earlier))[0]


def stage(run, *earlier):
    blank = lambda: jax.tree.map(lambda a: jnp.zeros(a.shape, a.dtype), jax.eval_shape(run))
    return lax.cond(after(jnp.bool_(True), *earlier), run, blank)


def place_kernel(*refs, parts):
    *blocks, out, held, arrived, left = refs
    me = lax.axis_index("fsdp")
    into, back = [], []
    for j in range(held.shape[0]):
        at = 0
        for i in range(j * parts, (j + 1) * parts):
            rows = blocks[i].shape[0]
            into.append(
                pltpu.make_async_copy(blocks[i], held.at[j, pl.ds(at, rows)], arrived.at[i])
            )
            at += rows
        back.append(
            pltpu.make_async_copy(
                held.at[j], out.at[lax.bitwise_xor(me, jnp.int32(j))], left.at[j]
            )
        )
    for copy in into:
        copy.start()
    for j, copy in enumerate(back):
        for part in into[j * parts : (j + 1) * parts]:
            part.wait()
        copy.start()
    for copy in back:
        copy.wait()


def place(blocks, parts=1, limit=60):
    count = len(blocks)
    size = count // parts
    rows = sum(block.shape[0] for block in blocks[:parts])
    shape = (size, rows, blocks[0].shape[1])
    dtype = blocks[0].dtype
    whole = pl.pallas_call(
        lambda *refs: place_kernel(*refs, parts=parts),
        in_specs=[pl.BlockSpec(memory_space=pl.ANY)] * count,
        out_specs=pl.BlockSpec(memory_space=pl.ANY),
        out_shape=jax.ShapeDtypeStruct(shape, dtype),
        scratch_shapes=[
            pltpu.VMEM(shape, dtype),
            pltpu.SemaphoreType.DMA((count,)),
            pltpu.SemaphoreType.DMA((size,)),
        ],
        compiler_params=pltpu.CompilerParams(vmem_limit_bytes=limit * 2**20),
        cost_estimate=SMALL,
        name="place",
    )(*blocks)
    return whole.reshape(size * rows, shape[2])


def gather(array, *before_last):
    core = swap(array, 1)
    chip = swap(array, 2)
    return [array, core, chip, swap(after(chip, *before_last) if before_last else chip, 1)]


def bring(blocks, held, arrived, rest=None):
    me = lax.axis_index("fsdp")
    cols = held.shape[1]
    count = len(blocks)
    copies = []
    for j, block in enumerate(blocks):
        to = held.at[lax.bitwise_xor(me, jnp.int32(j))]
        if rest is None:
            copies.append(pltpu.make_async_copy(block, to, arrived.at[j]))
        else:
            copies.append(pltpu.make_async_copy(block.at[pl.ds(0, cols)], to, arrived.at[j]))
            copies.append(
                pltpu.make_async_copy(
                    block.at[pl.ds(cols, 16)], rest.at[j], arrived.at[count + j]
                )
            )
    for copy in copies:
        copy.start()
    for copy in copies:
        copy.wait()


def spread_kernel(index, *refs, count, kept, normalize):
    step = pl.program_id(0)
    blocks, gain = refs[:count], refs[count]
    outs = refs[count + 1 + kept :]
    me = index[count]
    for j, block in enumerate(blocks):

        @pl.when(step == j)
        def _():
            x = block[...].astype(full)
            cols = outs[1].shape[0]
            if normalize:
                factor = lax.rsqrt(jnp.mean(x * x, axis=-1, keepdims=True) + epsilon)
                wide = (x * factor * gain[...]).astype(low)
                outs[2][...] = wide.T
            else:
                wide = (branch_scale * x).astype(low)
            outs[0][...] = wide
            for g in range(x.shape[1] // cols):

                @pl.when(me == g)
                def _():
                    outs[1][...] = x[:, g * cols : (g + 1) * cols].T


def spread(blocks, partners, gain, normalize, earlier=None):
    rows, width = blocks[0].shape
    size = lax.axis_size("fsdp")
    count = len(blocks)
    me = lax.axis_index("fsdp")
    tokens = [me ^ j for j in partners]
    local = [block % count for block in tokens]
    index = jnp.stack([jnp.asarray(v, jnp.int32) for v in (*local, me, *tokens)])
    const = lambda shape: pl.BlockSpec(shape, lambda i, index: (0,) * len(shape))
    kept = len(earlier) if earlier else 0
    outs = [
        (
            pl.BlockSpec((rows, width), lambda i, index: (index[i], 0)),
            jax.ShapeDtypeStruct((count * rows, width), low),
        ),
        (
            pl.BlockSpec((width // size, rows), lambda i, index: (0, index[count + 1 + i])),
            jax.ShapeDtypeStruct((width // size, size * rows), full),
        ),
    ]
    if normalize:
        outs.append(
            (
                pl.BlockSpec((width, rows), lambda i, index: (0, index[count + 1 + i])),
                jax.ShapeDtypeStruct((width, size * rows), low),
            )
        )
    return pl.pallas_call(
        lambda *refs: spread_kernel(*refs, count=count, kept=kept, normalize=normalize),
        grid_spec=pltpu.PrefetchScalarGridSpec(
            num_scalar_prefetch=1,
            grid=(count,),
            in_specs=[const((rows, width))] * count
            + [const((1, width))]
            + [pl.BlockSpec(memory_space=pl.ANY)] * kept,
            out_specs=[spec for spec, _ in outs],
        ),
        out_shape=[shape for _, shape in outs],
        input_output_aliases={count + 2 + i: 1 + i for i in range(kept)},
        compiler_params=pltpu.CompilerParams(vmem_limit_bytes=32 * 2**20),
        cost_estimate=SMALL,
        name="spread",
    )(index, *blocks, gain[None, :], *(earlier or ()))


def hidden_kernel(
    own, core, chip, both, weight, tokens, gain, hidden_ref, first_ref, second_ref, all_ref,
    squares_ref, held, arrived, left,
):
    step = pl.program_id(0)
    out = pltpu.make_async_copy(held, all_ref, left.at[0])

    @pl.when(step == 0)
    def _():
        bring((own, core, chip, both), held, arrived)
        out.start()

    span = held.shape[2]
    result = jnp.dot(
        weight[...], held[...].reshape(-1, span), preferred_element_type=full
    )
    hidden = tokens[...] + branch_scale * result
    tile = hidden.shape[0]
    at = pl.multiple_of(step * tile, tile)
    hidden_ref[pl.ds(at, tile), :] = hidden
    part = span // 2
    halves = [(first_ref, slice(0, part)), (second_ref, slice(part, span))]
    for ref, cut in halves:
        ref[pl.ds(at, tile), :] = (hidden[:, cut] * gain[...]).astype(low)
    squares = jnp.sum(hidden * hidden, axis=0, keepdims=True)

    @pl.when(step == 0)
    def _():
        squares_ref[...] = squares

    @pl.when(step != 0)
    def _():
        squares_ref[...] += squares

    @pl.when(step == pl.num_programs(0) - 1)
    def _():
        total = squares_ref[...]
        high = total.astype(low)
        rest = (total - high.astype(full)).astype(low)
        cols = hidden_ref.shape[0]
        for ref, cut in halves:
            ref[cols : cols + 8] = jnp.broadcast_to(high[:, cut], (8, part))
            ref[cols + 8 :] = jnp.broadcast_to(rest[:, cut], (8, part))
        out.wait()


def hidden_state(blocks, weight, tokens, gain):
    cols, span = blocks[0].shape
    size = len(blocks)
    tiles = 2
    tile = cols // tiles
    hbm = pl.BlockSpec(memory_space=pl.ANY)
    rows = lambda wide: pl.BlockSpec((tile, wide), lambda i: (i, 0))
    const = lambda shape: pl.BlockSpec(shape, lambda i: (0, 0))
    half = const((cols + 16, span // 2))
    hidden, first, second, whole = pl.pallas_call(
        hidden_kernel,
        grid=(tiles,),
        in_specs=[hbm] * 4 + [rows(size * cols), rows(span), rows(1)],
        out_specs=[const((cols, span)), half, half, hbm],
        out_shape=[
            jax.ShapeDtypeStruct((cols, span), full),
            jax.ShapeDtypeStruct((cols + 16, span // 2), low),
            jax.ShapeDtypeStruct((cols + 16, span // 2), low),
            jax.ShapeDtypeStruct((size, cols, span), low),
        ],
        scratch_shapes=[
            pltpu.VMEM((1, span), full),
            pltpu.VMEM((size, cols, span), low),
            pltpu.SemaphoreType.DMA((size,)),
            pltpu.SemaphoreType.DMA((1,)),
        ],
        compiler_params=pltpu.CompilerParams(vmem_limit_bytes=60 * 2**20),
        cost_estimate=SMALL,
        name="hidden_state",
    )(*blocks, weight, tokens, gain)
    return hidden, first, second, whole.reshape(size * cols, span)


def inner_kernel(*refs, half):
    blocks, (w_gate, w_up, d_inner), refs = refs[:4], refs[4:7], refs[7:]
    inner_ref, grads_ref, mean_ref, factor_ref, all_ref, held, rest, arrived, left = refs[5 * half :]
    step = pl.program_id(0)
    span = held.shape[2]
    out = pltpu.make_async_copy(
        held, all_ref.at[:, :, pl.ds(half * span, span)], left.at[0]
    )

    @pl.when(step == 0)
    def _():
        bring(blocks, held, arrived, rest)
        out.start()
        squares = [
            rest[j, 0:1].astype(full) + rest[j, 8:9].astype(full) for j in range(held.shape[0])
        ]
        total = (squares[0] + squares[1]) + (squares[2] + squares[3])
        factor_ref[...] = lax.rsqrt(total / (held.shape[0] * held.shape[1]) + epsilon)

        mean_ref[...] = jnp.zeros_like(mean_ref)

    wide = BLK
    for part in range(span // wide):
        cut = slice(part * wide, (part + 1) * wide)
        scaled = held[:, :, cut].reshape(-1, wide)
        factor = factor_ref[:, cut]
        gate = factor * jnp.dot(w_gate[...], scaled, preferred_element_type=full)
        up = factor * jnp.dot(w_up[...], scaled, preferred_element_type=full)
        sigmoid = 0.5 * jnp.tanh(0.5 * gate) + 0.5
        activated = gate * sigmoid
        inner_ref[:, cut] = (activated * up).astype(low)
        grad = factor * d_inner[:, cut].astype(full)
        d_up = grad * activated
        d_gate = grad * up * (sigmoid + activated * (1.0 - sigmoid))
        grads_ref[0, :, cut] = d_gate.astype(low)
        grads_ref[1, :, cut] = d_up.astype(low)
        mean_ref[:, cut] += jnp.sum(d_gate * gate + d_up * up, axis=0, keepdims=True)

    @pl.when(step == pl.num_programs(0) - 1)
    def _():
        out.wait()


def inner_part(half, blocks, w_gate, w_up, d_inner, before=()):
    tall, span = blocks[0].shape
    cols = tall - 16
    size = len(blocks)
    units = w_gate.shape[0]
    tile = units // 3
    hbm = pl.BlockSpec(memory_space=pl.ANY)
    weight = pl.BlockSpec((tile, size * cols), lambda i: (i, 0))
    part = pl.BlockSpec((tile, span), lambda i: (i, half))
    row = pl.BlockSpec((1, span), lambda i: (0, half))
    return pl.pallas_call(
        lambda *refs: inner_kernel(*refs, half=half),
        grid=(units // tile,),
        in_specs=[hbm] * 4 + [weight, weight, part] + [hbm] * len(before),
        out_specs=[part, pl.BlockSpec((2, tile, span), lambda i: (0, i, half)), row, row, hbm],
        out_shape=[
            jax.ShapeDtypeStruct((units, 2 * span), low),
            jax.ShapeDtypeStruct((2, units, 2 * span), low),
            jax.ShapeDtypeStruct((1, 2 * span), full),
            jax.ShapeDtypeStruct((1, 2 * span), full),
            jax.ShapeDtypeStruct((size, cols, 2 * span), low),
        ],
        input_output_aliases={7 + i: i for i in range(len(before))},
        scratch_shapes=[
            pltpu.VMEM((size, cols, span), low),
            pltpu.VMEM((size, 16, span), low),
            pltpu.SemaphoreType.DMA((2 * size,)),
            pltpu.SemaphoreType.DMA((1,)),
        ],
        compiler_params=pltpu.CompilerParams(vmem_limit_bytes=60 * 2**20),
        cost_estimate=SMALL,
        name="inner_part",
    )(*blocks, w_gate, w_up, d_inner, *before)


def to_rows(field, rows):
    me = lax.axis_index("fsdp")
    size = lax.axis_size("fsdp")
    blocks = []
    for j in range(size):
        block = lax.dynamic_slice_in_dim(field, (me ^ j) * rows, rows, 1)
        blocks.append(block if j == 0 else swap(block, j))
    return place(blocks).T


def product_kernel(index, act, *refs, count, adds, turned):
    grads = refs[:count]
    added = refs[count] if adds else None
    out = refs[-1]
    rows = act[:, 0].reshape(-1, act.shape[-1])
    for k in range(count):
        pair = (grads[k][...], rows) if turned else (rows, grads[k][...])
        total = lax.dot_general(*pair, NT, preferred_element_type=full)
        if turned:
            if adds:
                total = total + added[0, k].astype(full)
            out[0, k] = total.astype(low)
            continue
        total = total.reshape((act.shape[0], act.shape[2]) + total.shape[1:])
        if adds:
            total = total + added[:, k].astype(full)
        out[:, k] = total.astype(low)


def half_product(act, grads, side, added=None, turned=False, columns=None, earlier=()):
    size = lax.axis_size("rep")
    count = len(grads)
    tokens = grads[0].shape[1]
    columns = columns or grads[0].shape[0]
    lines, rows = size // 2, act.shape[0] // size
    index = jnp.asarray(side, jnp.int32)[None]
    if earlier:
        index = after(index, *earlier)
    steps = lines
    some = lines // steps
    shape = (columns, rows) if turned else (rows, columns)
    piece = pl.BlockSpec((some, count) + shape, lambda i, index: (i, 0, 0, 0))
    return pl.pallas_call(
        lambda *refs: product_kernel(*refs, count=count, adds=added is not None, turned=turned),
        grid_spec=pltpu.PrefetchScalarGridSpec(
            num_scalar_prefetch=1,
            grid=(steps,),
            in_specs=[pl.BlockSpec((some, 1, rows, tokens), lambda i, index: (i, index[0], 0, 0))]
            + [pl.BlockSpec((columns, tokens), lambda i, index: (0, 0))] * count
            + ([] if added is None else [piece]),
            out_specs=piece,
        ),
        out_shape=jax.ShapeDtypeStruct((lines, count) + shape, low),
        compiler_params=pltpu.CompilerParams(vmem_limit_bytes=60 * 2**20),
        cost_estimate=SMALL,
        name="half_product",
    )(index, act.reshape(lines, 2, rows, tokens), *grads, *(() if added is None else (added,)))


def whole_kernel(act, grad, out):
    out[0] = lax.dot_general(act[0], grad[...], NT, preferred_element_type=full).astype(low)


def whole_product(act, grad, columns):
    lines = lax.axis_size("rep") // 2
    tokens = grad.shape[1]
    last = grad.shape[0] // columns - 1
    rows = act.shape[0] // lines
    return pl.pallas_call(
        whole_kernel,
        grid=(lines,),
        in_specs=[
            pl.BlockSpec((1, rows, tokens), lambda i: (i, 0, 0)),
            pl.BlockSpec((columns, tokens), lambda i: (last, 0)),
        ],
        out_specs=pl.BlockSpec((1, rows, columns), lambda i: (i, 0, 0)),
        out_shape=jax.ShapeDtypeStruct((lines, rows, columns), low),
        compiler_params=pltpu.CompilerParams(vmem_limit_bytes=60 * 2**20),
        cost_estimate=SMALL,
        name="whole_product",
    )(act.reshape(lines, rows, tokens), grad)


def neighbour(array):
    return lax.ppermute(array, "rep", [(i, i ^ 1) for i in range(lax.axis_size("rep"))])


def line_scatter(array):
    size = lax.axis_size("rep")
    groups = [list(range(side, size, 2)) for side in range(2)]
    return lax.psum_scatter(
        array, "rep", scatter_dimension=0, tiled=True, axis_index_groups=groups
    )


class GradSum:
    def __init__(self, act, grads, turned=False, columns=None):
        self.act, self.grads, self.turned, self.columns = act, grads, turned, columns
        self.side = lax.axis_index("rep") % 2

    def send(self, earlier=()):
        sent = half_product(
            self.act,
            self.grads,
            1 - self.side,
            turned=self.turned,
            columns=self.columns,
            earlier=earlier,
        )
        return sent

    def transfer(self, sent):
        self.arrived = neighbour(sent)

    def keep(self, earlier=(), last=None):
        kept = half_product(
            self.act,
            self.grads,
            self.side,
            self.arrived,
            turned=self.turned,
            columns=self.columns,
            earlier=earlier,
        )
        self.sums = line_scatter(kept if last is None else after(kept, last.sums))
        return kept

    def line_first(self, earlier=()):
        whole = whole_product(self.act, after(self.grads[0], *earlier), self.columns)
        self.sums = line_scatter(whole)
        return whole

    def sides_last(self, earlier=()):
        _, rows, columns = self.sums.shape
        parts = self.sums.reshape(2, rows // 2, columns)
        side = after(self.side, *earlier)
        sent = lax.dynamic_index_in_dim(parts, 1 - side, 0, False)
        kept = lax.dynamic_index_in_dim(parts, side, 0, False)
        return kept.astype(full) + neighbour(sent).astype(full)

    def result(self):
        return [self.sums[0, k].astype(full) for k in range(len(self.grads))]


def sum_everywhere(array):
    array = (array + swap(array, 1)) + (swap(array, 2) + swap(array, 3))
    size = lax.axis_size("rep")
    far = 1
    while far < size:
        array = array + lax.ppermute(array, "rep", [(i, i ^ far) for i in range(size)])
        far *= 2
    return array


def flip_kernel(*refs):
    count = len(refs) // 2
    for wide, tall in zip(refs[:count], refs[count:]):
        tall[...] = wide[...].T


def flip(arrays, tiles, earlier=()):
    width = arrays[0].shape[1]
    tile = width // tiles
    index = jnp.zeros((1,), jnp.int32)
    if earlier:
        index = after(index, *earlier)
    return pl.pallas_call(
        lambda index, *refs: flip_kernel(*refs),
        grid_spec=pltpu.PrefetchScalarGridSpec(
            num_scalar_prefetch=1,
            grid=(tiles,),
            in_specs=[pl.BlockSpec((a.shape[0], tile), lambda i, index: (0, i)) for a in arrays],
            out_specs=[pl.BlockSpec((tile, a.shape[0]), lambda i, index: (i, 0)) for a in arrays],
        ),
        out_shape=[jax.ShapeDtypeStruct((width, a.shape[0]), a.dtype) for a in arrays],
        compiler_params=pltpu.CompilerParams(vmem_limit_bytes=60 * 2**20),
        cost_estimate=SMALL,
        name="flip",
    )(index, *arrays)


def chunks_kernel(index, *refs, count, ways, added, extra):
    step = pl.program_id(1)
    weights, grads, refs = refs[:count], refs[count], refs[count + 1 :]
    plus, refs = refs[:added], refs[added:]
    row, outs = refs[:extra], refs[extra:]
    total, at = None, 0
    for weight in weights:
        units = weight.shape[1]
        term = jnp.dot(weight[...], grads[at : at + units], preferred_element_type=full)
        total = term if total is None else total + term
        at += units
    cols = total.shape[0]
    for way, out in enumerate(outs):

        @pl.when(step == way)
        def _():
            found = total + plus[way][:cols].astype(full) if plus else total
            out[:cols] = found.astype(out.dtype)
            if row:
                found = row[0][...]
                if plus:
                    found = found + plus[way][cols : cols + 1].astype(full)
                out[cols:] = jnp.broadcast_to(
                    found.astype(out.dtype), (out.shape[0] - cols, found.shape[1])
                )


def feature_chunks(weights, grads, partners, plus=(), extra=None, dtype=low, earlier=()):
    me = lax.axis_index("fsdp")
    span = grads.shape[1]
    cols = weights[0].shape[0] // lax.axis_size("fsdp")
    tall = cols + (0 if extra is None else 16)
    index = jnp.stack([jnp.asarray(me ^ j, jnp.int32) for j in partners])
    if earlier:
        index = after(index, *earlier)
    extra = () if extra is None else (extra,)
    tiles = 2
    tile = lambda rows: pl.BlockSpec((rows, span // tiles), lambda i, k, index: (0, i))
    return pl.pallas_call(
        lambda *refs: chunks_kernel(
            *refs, count=len(weights), ways=len(partners), added=len(plus), extra=len(extra)
        ),
        grid_spec=pltpu.PrefetchScalarGridSpec(
            num_scalar_prefetch=1,
            grid=(tiles, len(partners)),
            in_specs=[
                pl.BlockSpec((cols, w.shape[1]), lambda i, k, index: (index[k], 0))
                for w in weights
            ]
            + [tile(a.shape[0]) for a in (grads, *plus, *extra)],
            out_specs=[tile(tall)] * len(partners),
        ),
        out_shape=[jax.ShapeDtypeStruct((tall, span), dtype)] * len(partners),
        compiler_params=pltpu.CompilerParams(vmem_limit_bytes=60 * 2**20),
        cost_estimate=SMALL,
        name="feature_chunks",
    )(index, *weights, grads, *plus, *extra)


def attn_grad_kernel(
    own, across, cotangent, hidden, gain, factor, attn_ref, hidden_ref, term_ref, *, width
):
    cols = hidden.shape[0]
    mean = (own[cols : cols + 1] + across[cols : cols + 1].astype(full)) * (1.0 / width)
    scaled = own[:cols] + across[:cols].astype(full)
    state = hidden[...]
    term = jnp.sum(scaled * state, axis=1, keepdims=True)
    step = pl.program_id(0)

    @pl.when(step == 0)
    def _():
        term_ref[...] = term

    @pl.when(step != 0)
    def _():
        term_ref[...] += term

    grad = cotangent[...] + gain[...] * scaled - state * (factor[...] * mean)
    hidden_ref[...] = grad.astype(low)
    attn_ref[...] = (branch_scale * grad).astype(low)


def attn_grad(own, across, cotangent, hidden, gain, factor, width):
    cols, span = hidden.shape
    field = jax.ShapeDtypeStruct((cols, span), low)
    tiles = 4
    tile = lambda rows: pl.BlockSpec((rows, span // tiles), lambda i: (0, i))
    once = pl.BlockSpec((cols, 1), lambda i: (0, 0))
    return pl.pallas_call(
        lambda *refs: attn_grad_kernel(*refs, width=width),
        grid=(tiles,),
        in_specs=[tile(cols + 16), tile(cols + 16), tile(cols), tile(cols), once, tile(1)],
        out_specs=[tile(cols), tile(cols), once],
        out_shape=[field, field, jax.ShapeDtypeStruct((cols, 1), full)],
        compiler_params=pltpu.CompilerParams(vmem_limit_bytes=60 * 2**20),
        cost_estimate=SMALL,
        name="attn_grad",
    )(own, across, cotangent, hidden, gain, factor)


def blocks_kernel(index, *refs, count, added):
    step = pl.program_id(0)
    weights, refs = refs[:count], refs[count:]
    grads, refs = refs[:count], refs[count:]
    plus, outs = refs[:added], refs[added:]
    total = None
    for weight, grad in zip(weights, grads):
        term = jnp.dot(grad[...].T, weight[...], preferred_element_type=full)
        total = term if total is None else total + term
    for way, out in enumerate(outs):

        @pl.when(step == way)
        def _():
            found = total + plus[way][...].astype(full) if plus else total
            out[...] = found.astype(out.dtype)


def token_chunks(weights, grads, partners, rows, plus=(), dtype=low, earlier=()):
    me = lax.axis_index("fsdp")
    width = weights[0].shape[1]
    index = jnp.stack([jnp.asarray(me ^ j, jnp.int32) for j in partners])
    if earlier:
        index = after(index, *earlier)
    const = lambda shape: pl.BlockSpec(shape, lambda i, index: (0, 0))
    return pl.pallas_call(
        lambda *refs: blocks_kernel(*refs, count=len(weights), added=len(plus)),
        grid_spec=pltpu.PrefetchScalarGridSpec(
            num_scalar_prefetch=1,
            grid=(len(partners),),
            in_specs=[const(w.shape) for w in weights]
            + [pl.BlockSpec((g.shape[0], rows), lambda i, index: (0, index[i])) for g in grads]
            + [const(a.shape) for a in plus],
            out_specs=[const((rows, width))] * len(partners),
        ),
        out_shape=[jax.ShapeDtypeStruct((rows, width), dtype)] * len(partners),
        compiler_params=pltpu.CompilerParams(vmem_limit_bytes=60 * 2**20),
        cost_estimate=SMALL,
        name="token_chunks",
    )(index, *weights, *grads, *plus)


def body(
    tokens, cotangent, gain_attn, gain_ffn, w_query, w_key, w_value, w_out, w_gate, w_up, w_down
):
    rows, width = tokens.shape
    size = lax.axis_size("fsdp")
    reps = lax.axis_size("rep")
    span = rows * size
    me = lax.axis_index("fsdp")
    replica = lax.axis_index("rep")
    width_cols = width // size
    hidden_cols = w_gate.shape[1]
    heads = width_cols // HD

    half = HD // 2
    frequency = 10000.0 ** (-(jnp.arange(half, dtype=full) * 2.0 / HD))
    angles = frequency[:, None] * jnp.arange(span, dtype=jnp.int32).astype(full)[None, :]
    cosine, sine = jnp.cos(angles), jnp.sin(angles)

    def own_gain(gain):
        return lax.dynamic_slice_in_dim(gain, me * width_cols, width_cols, 0)[:, None]

    down_turned = w_down.T
    share = width_cols // reps

    def down_part(j):
        return lax.dynamic_slice(
            down_turned, (replica * share, (me ^ j) * hidden_cols), (share, hidden_cols)
        )

    parts = [down_part(2), down_part(3)]

    def project(normed):
        found = []
        for weight in (w_query, w_key, w_value):
            field = jnp.einsum("de,td->et", weight, normed, preferred_element_type=full)
            found.append(field.reshape(heads, HD, normed.shape[0]))
        return found

    tokens_chip = swap(tokens, 2)
    normed_here, tokens_part, normed_part = spread(
        [tokens, swap(tokens, 1)], (0, 1), gain_attn, True
    )
    here = project(normed_here)
    tokens_chip = after(tokens_chip, *here)
    parts = [swap(after(part, tokens_chip), 2) for part in parts]
    normed_there, tokens_own, normed_turned = spread(
        [tokens_chip, swap(tokens_chip, 1)],
        (2, 3),
        gain_attn,
        True,
        (tokens_part, normed_part),
    )
    there = project(normed_there)
    parts = [after(part, *there) for part in parts]
    cotangent_chip = swap(after(cotangent, *parts), 2)
    parts_all = lax.all_gather(
        jnp.stack([parts[0], swap(parts[1], 1)]), "rep", axis=1, tiled=True
    )
    attended, query_low, key_low, value_low, lse = attention_forward(here, there, cosine, sine)

    def spread_cotangent():
        blocks = [cotangent, swap(cotangent, 1), cotangent_chip, swap(cotangent_chip, 1)]
        return spread(blocks, (0, 1, 2, 3), gain_attn, False)

    d_ffn, cotangent_own = stage(spread_cotangent, attended)
    d_ffn_own = (branch_scale * cotangent_own).astype(low)
    me_later = after(me, d_ffn)

    def down_block(j):
        return lax.dynamic_slice_in_dim(
            down_turned, (me_later ^ j) * hidden_cols, hidden_cols, 1
        )

    down_near = [down_block(0), swap(down_block(1), 1)]
    gate_tall, up_tall = flip([w_gate.T, w_up.T], 6, [down_near[0]])
    (out_tall,) = flip([w_out.T], 6, [gate_tall])
    attended_blocks = gather(attended.reshape(width_cols, span), out_tall)

    gain_own = own_gain(gain_ffn)
    hidden, scaled_first, scaled_second, attended_all = hidden_state(
        attended_blocks, w_out.T, tokens_own, gain_own
    )
    scaled_chip = swap(scaled_first, 2)

    down_own = place(
        [after(down_near[0], hidden), down_near[1], parts_all[0], parts_all[1]], limit=16
    )
    d_inner = jnp.einsum("ef,te->ft", down_own, d_ffn, preferred_element_type=full).astype(low)
    scaled_chip = after(scaled_chip, d_inner)
    scaled_first = [scaled_first, swap(scaled_first, 1), scaled_chip, swap(scaled_chip, 1)]
    second_chip = swap(after(scaled_second, scaled_chip), 2)

    first = stage(lambda: inner_part(0, scaled_first, w_gate.T, w_up.T, d_inner), d_inner)
    second_chip = after(second_chip, first[2])
    scaled_second = [scaled_second, swap(scaled_second, 1), second_chip, swap(second_chip, 1)]
    inner, ffn_grads, mean, factor, scaled_all = inner_part(
        1, scaled_second, w_gate.T, w_up.T, d_inner, first
    )
    ffn_grads = ffn_grads.reshape(2 * hidden_cols, span)
    scaled_all = scaled_all.reshape(width, span)

    third = 2 * hidden_cols // 3
    sum_most = GradSum(scaled_all, [ffn_grads], columns=2 * third)
    sum_rest = GradSum(scaled_all, [ffn_grads], columns=third)
    token = sum_rest.line_first()
    token = sum_most.send([token])
    sum_most.transfer(token)
    inner_chip = swap(inner, 2)
    inner_core = swap(inner, 1)
    ffn_weights = (gate_tall, up_tall)

    def first_stage():
        far, near = feature_chunks(ffn_weights, ffn_grads, (3, 1), extra=mean)
        far, near = swap(far, 1), swap(near, 1)
        (chunk,) = feature_chunks(ffn_weights, ffn_grads, (2,), plus=[far], extra=mean)
        return chunk, near

    chunk, near = stage(first_stage, token)
    across = swap(chunk, 2)
    (own,) = feature_chunks(ffn_weights, ffn_grads, (0,), plus=[near], extra=mean, dtype=full)
    inner_late = after(inner_chip, own)
    inner_all = place([inner, inner_core, inner_late, swap(inner_late, 1)])
    sum_down = GradSum(inner_all, [d_ffn_own], turned=True)
    token = sum_down.send()
    sum_down.transfer(token)
    d_attn, d_hidden, gain_ffn_term = attn_grad(
        own, after(across, token), cotangent_own, hidden, gain_own, factor, width
    )

    far, near = feature_chunks([out_tall], d_attn, (3, 1))
    far, near = swap(far, 1), swap(near, 1)
    token = sum_most.keep([far], sum_rest)
    (chunk,) = feature_chunks([out_tall], d_attn, (2,), plus=[far], earlier=[token])
    across = swap(chunk, 2)
    (own,) = feature_chunks([out_tall], d_attn, (0,), plus=[near], dtype=full, earlier=[chunk])
    sum_out = GradSum(attended_all, [d_attn])
    token = sum_out.send([own])
    sum_out.transfer(token)
    across = after(across, token)

    def second_stage():
        d_query, d_key, d_value = (
            field.reshape(width_cols, span)
            for field in attention_backward(
                query_low,
                key_low,
                value_low,
                own.reshape(heads, HD, span),
                across.reshape(heads, HD, span),
                attended,
                lse,
                cosine,
                sine,
            )
        )
        sent = GradSum(normed_turned, [d_query, d_key, d_value]).send()
        return d_query, d_key, d_value, sent

    d_query, d_key, d_value, sent = second_stage()
    sum_attn = GradSum(normed_turned, [d_query, d_key, d_value])
    sum_attn.transfer(sent)
    token = sum_down.keep([sent], sum_most)

    def third_stage():
        attn_weights, attn_grads = (w_query.T, w_key.T, w_value.T), (d_query, d_key, d_value)
        far, near = token_chunks(attn_weights, attn_grads, (3, 1), rows)
        far, near = swap(far, 1), swap(near, 1)
        (chunk,) = token_chunks(attn_weights, attn_grads, (2,), rows, plus=[far])
        across = swap(chunk, 2)
        (own,) = token_chunks(
            attn_weights, attn_grads, (0,), rows, plus=[near], dtype=full, earlier=[chunk]
        )
        return own, across

    own, across = stage(third_stage, token)
    token = sum_out.keep([own], sum_down)
    ffn_result = jnp.einsum(
        "fe,ft->et", w_down, after(inner_all, token), preferred_element_type=full
    )
    output_turned = (hidden + branch_scale * ffn_result).astype(low)
    output = to_rows(output_turned, rows)
    hidden_rows = to_rows(after(d_hidden, output_turned), rows)
    d_normed = own + after(across, token).astype(full)
    x_own = tokens.astype(full)
    factor_own = lax.rsqrt(jnp.mean(x_own * x_own, axis=-1, keepdims=True) + epsilon)
    unit_own = x_own * factor_own
    part = d_normed * gain_attn
    gain_attn_term = jnp.sum(d_normed * unit_own, axis=0)
    gain_ffn_wide = lax.dynamic_update_slice_in_dim(
        jnp.zeros((width,), full), gain_ffn_term[:, 0], me * width_cols, 0
    )
    d_tokens = hidden_rows.astype(full) + factor_own * (
        part - unit_own * jnp.mean(part * unit_own, axis=-1, keepdims=True)
    )
    grad_rest = sum_rest.sides_last([token])
    token = sum_attn.keep([d_tokens, output], sum_out)
    grad_gain_attn, grad_gain_ffn = sum_everywhere(jnp.stack([gain_attn_term, gain_ffn_wide]))
    grad_rest = sum_rest.sides_last([token])
    grad_query, grad_key, grad_value = sum_attn.result()
    (grad_out,) = sum_out.result()
    (grad_most,) = sum_most.result()
    grad_gate = grad_most[:, :hidden_cols]
    grad_up = jnp.concatenate([grad_most[:, hidden_cols:], grad_rest], axis=1)
    (grad_down,) = sum_down.result()
    return (
        output,
        d_tokens,
        grad_gain_attn,
        grad_gain_ffn,
        grad_query,
        grad_key,
        grad_value,
        grad_out,
        grad_gate,
        grad_up,
        grad_down.T,
    )


def solution(mesh):
    rows = P(("rep", "fsdp"), None)
    columns = P(None, "fsdp")
    both = P("rep", "fsdp")
    return jax.shard_map(
        body,
        mesh=mesh,
        in_specs=(rows, rows, P(), P()) + (columns,) * 7,
        out_specs=(rows, rows, P(), P()) + (both,) * 7,
        check_vma=False,
    )
```
